32 devices in a mesh: section: 2 (over y), dp: 16 (over z, x, core).
Axes of the slice: x: 2, y: 2, z: 4, core: 2. Of those that a mesh axis runs over, the one named last changes fastest.
Arguments:
- block_input: bfloat16 [65536, 256], P('dp'), may hold values from -6 to 6
- embedding: bfloat16 [65536, 256], P('dp'), may hold values from -6 to 6
- out_grad: bfloat16 [65536, 256], P('dp'), may hold values from -6 to 6
- example_counts: int32 [512], P('dp'), may hold values from 10 to 50
- example_lengths: int32 [512, 50], P('dp'), may hold values from 1 to 2
- norm1_gain: bfloat16 [256], replicated, may hold values from 0.25 to 1.75
- norm1_bias: bfloat16 [256], replicated, may hold values from -1.5 to 1.5
- query_weight: bfloat16 [256, 256], replicated, may hold values from -0.375 to 0.375
- query_bias: bfloat16 [256], replicated, may hold values from -1.5 to 1.5
- key_weight: bfloat16 [256, 256], replicated, may hold values from -0.375 to 0.375
- value_weight: bfloat16 [256, 256], replicated, may hold values from -0.375 to 0.375
- value_bias: bfloat16 [256], replicated, may hold values from -1.5 to 1.5
- out_weight: bfloat16 [256, 256], replicated, may hold values from -1 to 1
- out_bias: bfloat16 [256], replicated, may hold values from -1.5 to 1.5
- norm2_gain: bfloat16 [256], replicated, may hold values from 0.25 to 1.75
- norm2_bias: bfloat16 [256], replicated, may hold values from -1.5 to 1.5
- up_weight: bfloat16 [256, 1024], replicated, may hold values from -0.375 to 0.375
- up_bias: bfloat16 [1024], replicated, may hold values from -1.5 to 1.5
- down_weight: bfloat16 [1024, 256], replicated, may hold values from -0.1875 to 0.1875
- down_bias: bfloat16 [256], replicated, may hold values from -1.5 to 1.5
Outputs:
- states: bfloat16 [2, 65536, 256], P('section', 'dp')
- state_grads: float32 [2, 65536, 256], P('section', 'dp')
- grad_norm1_gain: float32 [256], replicated
- grad_norm1_bias: float32 [256], replicated
- grad_query_weight: float32 [256, 256], replicated
- grad_query_bias: float32 [256], replicated
- grad_key_weight: float32 [256, 256], replicated
- grad_value_weight: float32 [256, 256], replicated
- grad_value_bias: float32 [256], replicated
- grad_out_weight: float32 [256, 256], replicated
- grad_out_bias: float32 [256], replicated
- grad_norm2_gain: float32 [256], replicated
- grad_norm2_bias: float32 [256], replicated
- grad_up_weight: float32 [256, 1024], replicated
- grad_up_bias: float32 [1024], replicated
- grad_down_weight: float32 [1024, 256], replicated
- grad_down_bias: float32 [256], replicated
The draws below stay inside these ranges and needn't reach their ends.
Inputs may be any that keep to these rules, and one draw needn't show every extreme that they name: Prompt p uses its first sum of example_lengths[p, j] over j < example_counts[p] slots, at most 100.
All inputs are finite; a program needn't handle non-finite values.
Results may differ from the reference program's by a relative error of at most 0.013.
Values may be sent and summed in bfloat16 or wider, within the bound.
A program may use at most 128 MiB of HBM per device.

```python
import jax
import jax.numpy as jnp
from jax import lax

D = 256
HEADS = 8
HEAD_DIM = 32
FF = 1024
SLOTS = 128
PER_ROW = 8
MINEX = 10
MAXEX = 50
TOKENS = 65536
PROMPTS = 512


def plant(values, stream_key, smallest, top_value):
    longest = values.shape.index(max(values.shape))
    spots = []
    for shift in (0, 1):
        where = [jax.random.randint(jax.random.fold_in(stream_key, axis), (), 0, length) for axis, length in enumerate(values.shape)]
        where[longest] = (where[longest] + shift) % values.shape[longest]
        spots.append(tuple(where))
    return values.at[spots[0]].set(smallest).at[spots[1]].set(top_value)


def steps_of(key, shape, cuts, smallest, largest):
    def one(position, blocks):
        steps = jax.random.uniform(jax.random.fold_in(jax.random.fold_in(key, 6), position), (blocks,), jnp.float32, smallest / len(cuts), largest / len(cuts))
        return jnp.repeat(jnp.exp(steps), shape[position] // blocks).reshape((-1,) + (1,) * (len(shape) - position - 1))

    factor_of = one(*cuts[0])
    for cut in cuts[1:]:
        factor_of = factor_of * one(*cut)
    return factor_of


def bell_draw(stream_key, shape, deviation, most, shards=(), kind=jnp.bfloat16):
    values = jax.random.normal(stream_key, shape, jnp.float32) * deviation
    if len(shards) > 0:
        values = steps_of(stream_key, shape, shards, -0.22, 0.18) * values
    return jnp.clip(values, min=-most, max=most).astype(kind)


def setup_inputs(seed: int = 0) -> dict:
    key_of = jax.random.split(jax.random.key(seed), 21)
    block_input = bell_draw(key_of[0], (TOKENS, D), 1.0, 6.0, ((0, 16),))
    embedding = bell_draw(key_of[1], (TOKENS, D), 1.0, 6.0, ((0, 16),))
    out_grad = bell_draw(key_of[2], (TOKENS, D), 1.0, 6.0, ((0, 16),))
    example_counts = plant(jax.random.randint(key_of[3], (PROMPTS,), MINEX, MAXEX + 1), jax.random.fold_in(key_of[3], 1), MINEX, MAXEX).astype(jnp.int32)
    example_lengths = plant(jax.random.randint(key_of[4], (PROMPTS, MAXEX), 1, 3), jax.random.fold_in(key_of[4], 1), 1, 2).astype(jnp.int32)
    norm1_gain = jnp.clip(1.0 + 0.15 * jax.random.normal(key_of[5], (D,), jnp.float32), 0.25, 1.75).astype(jnp.bfloat16)
    norm1_bias = bell_draw(key_of[6], (D,), 0.3, 1.5)
    query_weight = bell_draw(key_of[7], (D, D), D ** -0.5, 0.375)
    query_bias = bell_draw(key_of[8], (D,), 0.3, 1.5)
    key_weight = bell_draw(key_of[9], (D, D), D ** -0.5, 0.375)
    value_weight = bell_draw(key_of[10], (D, D), D ** -0.5, 0.375)
    value_bias = bell_draw(key_of[11], (D,), 0.3, 1.5)
    out_weight = bell_draw(key_of[12], (D, D), (D // 8) ** -0.5, 1.0)
    out_bias = bell_draw(key_of[13], (D,), 0.3, 1.5)
    norm2_gain = jnp.clip(1.0 + 0.15 * jax.random.normal(key_of[14], (D,), jnp.float32), 0.25, 1.75).astype(jnp.bfloat16)
    norm2_bias = bell_draw(key_of[15], (D,), 0.3, 1.5)
    up_weight = bell_draw(key_of[16], (D, FF), D ** -0.5, 0.375)
    up_bias = bell_draw(key_of[17], (FF,), 0.3, 1.5)
    down_weight = bell_draw(key_of[18], (FF, D), FF ** -0.5, 0.1875)
    down_bias = bell_draw(key_of[19], (D,), 0.3, 1.5)
    return {"block_input": block_input, "embedding": embedding, "out_grad": out_grad, "example_counts": example_counts, "example_lengths": example_lengths, "norm1_gain": norm1_gain, "norm1_bias": norm1_bias, "query_weight": query_weight, "query_bias": query_bias, "key_weight": key_weight, "value_weight": value_weight, "value_bias": value_bias, "out_weight": out_weight, "out_bias": out_bias, "norm2_gain": norm2_gain, "norm2_bias": norm2_bias, "up_weight": up_weight, "up_bias": up_bias, "down_weight": down_weight, "down_bias": down_bias}


@jax.custom_vjp
def low(v):
    return lax.optimization_barrier(v.astype(jnp.bfloat16)).astype(jnp.float32)

@jax.custom_vjp
def low_back(v):
    return v

def low_keep(v):
    return (low(v), None)

def low_pass(kept, grad):
    return (grad,)

def back_keep(v):
    return (v, None)

def back_low(kept, grad):
    return (low(grad),)
low.defvjp(low_keep, low_pass)
low_back.defvjp(back_keep, back_low)

def layer_norm(values_in, ln_gain, ln_shift):
    row_mean = lax.optimization_barrier(jnp.mean(values_in, axis=-1, keepdims=True))
    centred = values_in - row_mean
    spread = lax.optimization_barrier(jnp.mean(centred * centred, axis=-1, keepdims=True))
    return centred * lax.rsqrt(spread + 1e-05) * ln_gain + ln_shift

def project(left_op, right_op):
    return jnp.einsum('gsd,de->gse', left_op, right_op, precision=lax.Precision.HIGHEST)

def prompt_block(stream, used_slots, params):
    norm1_gain, norm1_bias, query_weight, query_bias, key_weight, value_weight, value_bias, out_weight, out_bias, norm2_gain, norm2_bias, up_weight, up_bias, down_weight, down_bias = params
    groups = stream.shape[0]
    slot_iota = jnp.arange(SLOTS)
    causal = slot_iota[None, :] <= slot_iota[:, None]
    allowed = causal[None] & (slot_iota[None, None, :] < used_slots[:, None, None])
    normed_one = low(layer_norm(stream, norm1_gain, norm1_bias))
    queries = low_back(low(project(normed_one, query_weight) + query_bias))
    key_rows = low_back(low(project(normed_one, key_weight)))
    value_rows = low_back(low(project(normed_one, value_weight) + value_bias))
    query_heads = queries.reshape(groups, SLOTS, HEADS, HEAD_DIM)
    key_heads = key_rows.reshape(groups, SLOTS, HEADS, HEAD_DIM)
    value_heads = value_rows.reshape(groups, SLOTS, HEADS, HEAD_DIM)
    scores = jnp.einsum('gqhd,gkhd->ghqk', query_heads, key_heads, precision=lax.Precision.HIGHEST)
    scores = scores * HEAD_DIM ** (-0.5)
    scores = low_back(jnp.where(allowed[:, None], scores, -1e+30))
    row_max = lax.optimization_barrier(jnp.max(scores, axis=-1, keepdims=True))
    shifted = jnp.exp(scores - row_max)
    probabilities = shifted / lax.optimization_barrier(jnp.sum(shifted, axis=-1, keepdims=True))
    weights_low = low(probabilities)
    mixed = jnp.einsum('ghqk,gkhd->gqhd', weights_low, value_heads, precision=lax.Precision.HIGHEST)
    mixed = low_back(low(mixed.reshape(groups, SLOTS, HEADS * HEAD_DIM)))
    branch_one = low_back(project(mixed, out_weight) + out_bias)
    middle = stream + branch_one
    normed_two = low(layer_norm(middle, norm2_gain, norm2_bias))
    pre_gelu = low_back(project(normed_two, up_weight) + up_bias)
    hidden = low(jax.nn.gelu(pre_gelu))
    branch_two = low_back(project(hidden, down_weight) + down_bias)
    return middle + branch_two

def run_block(stream, used_slots, params):
    shaped = stream.reshape(-1, 4 * PER_ROW, SLOTS, stream.shape[-1])
    counted = used_slots.reshape(-1, 4 * PER_ROW)
    block_step = jax.checkpoint(prompt_block)
    result = lax.map(lambda group_pair: block_step(group_pair[0], group_pair[1], params), (shaped, counted))
    return result.reshape(stream.shape)

def reference(block_input, embedding, out_grad, example_counts, example_lengths, norm1_gain, norm1_bias, query_weight, query_bias, key_weight, value_weight, value_bias, out_weight, out_bias, norm2_gain, norm2_bias, up_weight, up_bias, down_weight, down_bias):
    params = tuple((weight_arr.astype(jnp.float32) for weight_arr in (norm1_gain, norm1_bias, query_weight, query_bias, key_weight, value_weight, value_bias, out_weight, out_bias, norm2_gain, norm2_bias, up_weight, up_bias, down_weight, down_bias)))
    example_iota = jnp.arange(MAXEX).astype(jnp.int32)
    used_slots = lax.optimization_barrier(jnp.sum(jnp.where(example_iota[None, :] < example_counts[:, None], example_lengths, 0), axis=1)).astype(jnp.int32)
    embed_rows = embedding.astype(jnp.float32)
    first_in = block_input.astype(jnp.float32) + embed_rows
    first_out, first_pull = jax.vjp(lambda stream, weights: run_block(stream, used_slots, weights), first_in, params)
    sent = low(first_out)
    second_in = sent + embed_rows
    second_out, second_pull = jax.vjp(lambda stream, weights: run_block(stream, used_slots, weights), second_in, params)
    grad_second, params_second = second_pull(out_grad.astype(jnp.float32))
    grad_first, params_first = first_pull(low(grad_second))
    states = jnp.stack([first_out, second_out]).astype(jnp.bfloat16)
    state_grads = jnp.stack([grad_first, grad_second])
    summed = [own_part + other_part for own_part, other_part in zip(params_first, params_second)]
    return (states, state_grads, summed[0], summed[1], summed[2], summed[3], summed[4], summed[5], summed[6], summed[7], summed[8], summed[9], summed[10], summed[11], summed[12], summed[13], summed[14])
```

```python
import functools
import math

import jax
import jax.numpy as jnp
from jax import lax
from jax.experimental import pallas as pl
from jax.experimental.pallas import tpu as pltpu
from jax.sharding import PartitionSpec as P

BF = jnp.bfloat16
F32 = jnp.float32
SLOTS = 128
HEADS = 8
KEYS = 112
GROUP = 256
EPS = 1e-5


def nn(a, b):
    return lax.dot_general(a, b, (((1,), (0,)), ((), ())), preferred_element_type=F32)


def nt(a, b):
    return lax.dot_general(a, b, (((1,), (1,)), ((), ())), preferred_element_type=F32)


def ln_forward(u, gain, bias, unit_ref, inv_ref, n_ref):
    d = u.shape[0]
    mean = jnp.sum(u, axis=0, keepdims=True) * (1.0 / d)
    c = u - mean
    var = jnp.sum(c * c, axis=0, keepdims=True) * (1.0 / d)
    inv = lax.rsqrt(var + EPS)
    unit = c * inv
    unit_ref[...] = unit
    inv_ref[...] = inv
    n_ref[0:d, :] = (unit * gain + bias).astype(BF)


def lanes2(ref):
    v = ref[...]
    return jnp.concatenate([v, v], axis=1)


def fold(v):
    return v[:, :128] + v[:, 128:]


def ln_backward(gn, unit, inv, gain, gain_acc, bias_acc):
    d = gn.shape[0]
    t = gn * unit
    gain_acc[...] += fold(t)
    bias_acc[...] += fold(gn)
    s = gn * gain
    m1 = jnp.sum(s, axis=0, keepdims=True) * (1.0 / d)
    m2 = jnp.sum(t * gain, axis=0, keepdims=True) * (1.0 / d)
    return inv * (s - m1 - unit * m2)


C0 = math.sqrt(2.0 / math.pi)
C1 = C0 * 0.044715


def kernel(off_ref, x_ref, e_ref, g_ref, used_ref,
           n1g_ref, n1b_ref, wq_ref, qb_ref, wk_ref, wv_ref, vb_ref, wo_ref, ob_ref,
           n2g_ref, n2b_ref, wu_ref, ub_ref, wd_ref, db_ref,
           st_ref, gr_ref, awd_ref, awu_ref, awqkv_ref, awo_ref, aln_ref,
           wqkvT, woT, wuT, wdT, wqkv, vecs, ubv,
           n1T, qkvT, vN, p32, p16, mixT, unit1, inv1, unit2, inv2, n2T, gp, hT,
           bd, ds16, dqkvT, goT, aln):
    step = pl.program_id(0)
    steps = pl.num_programs(0)
    D = 256
    FF = 1024
    scale = 32 ** -0.5

    @pl.when(step == 0)
    def _():
        wqkvT[0:256, :] = wq_ref[...].T
        wqkvT[256:512, :] = wk_ref[...].T
        wqkvT[512:768, :] = wv_ref[...].T
        woT[...] = wo_ref[...].T
        wuT[...] = wu_ref[...].T
        wdT[...] = wd_ref[...].T
        wqkv[:, 0:256] = wq_ref[...]
        wqkv[:, 256:512] = wk_ref[...]
        wqkv[:, 512:768] = wv_ref[...]
        for i, r in enumerate((n1g_ref, n1b_ref, qb_ref, vb_ref, ob_ref, n2g_ref, n2b_ref, db_ref)):
            vecs[i] = jnp.broadcast_to(r[...].astype(F32), (128, D)).T
        ubv[...] = jnp.broadcast_to(ub_ref[...].astype(F32), (128, FF)).T
        awd_ref[...] = jnp.zeros_like(awd_ref)
        awu_ref[...] = jnp.zeros_like(awu_ref)
        awqkv_ref[...] = jnp.zeros_like(awqkv_ref)
        awo_ref[...] = jnp.zeros_like(awo_ref)
        aln[...] = jnp.zeros_like(aln)
        bd[...] = jnp.zeros_like(bd)
        ds16[...] = jnp.zeros_like(ds16)
        p16[...] = jnp.zeros_like(p16)
        for it in range(2):
            n1T[it, D:, :] = jnp.ones((16, GROUP), BF)
            mixT[it, D:, :] = jnp.ones((16, GROUP), BF)
            n2T[it, D:, :] = jnp.ones((16, GROUP), BF)
            hT[it, FF:, :] = jnp.ones((16, GROUP), BF)

    k_iota = lax.broadcasted_iota(jnp.int32, (KEYS, SLOTS), 0)
    q_iota = lax.broadcasted_iota(jnp.int32, (KEYS, SLOTS), 1)
    masks = []
    for p in range(2):
        used = used_ref[step * 2 + p]
        masks.append(jnp.where((k_iota <= q_iota) & (k_iota < used), 0.0, -1e30).astype(F32))

    def forward(u, it):
        ln_forward(u, lanes2(vecs.at[0]), lanes2(vecs.at[1]), unit1.at[it], inv1.at[it], n1T.at[it])
        n1 = n1T[it, 0:D, :]
        qkvT[it, 0:256, :] = (nn(wqkvT[0:256, :], n1) + lanes2(vecs.at[2])).astype(BF)
        qkvT[it, 256:512, :] = nn(wqkvT[256:512, :], n1).astype(BF)
        qkvT[it, 512:768, :] = (nn(wqkvT[512:768, :], n1) + lanes2(vecs.at[3])).astype(BF)
        for p in range(2):
            tok = slice(p * 128, p * 128 + 128)
            kN = qkvT[it, 256:512, tok].T
            vN[it, p] = qkvT[it, 512:768, tok].T
            for h in range(HEADS):
                bd[p, 32 * h:32 * h + 32, 128 * h:128 * h + 128] = qkvT[it, 32 * h:32 * h + 32, tok]
            for h2 in range(HEADS // 2):
                sT2 = nn(kN[:KEYS], bd[p, :, 256 * h2:256 * h2 + 256])
                for hh in range(2):
                    h = h2 * 2 + hh
                    ln = slice(128 * h, 128 * h + 128)
                    s = sT2[:, 128 * hh:128 * hh + 128] + masks[p]
                    m = jnp.max(s, axis=0, keepdims=True)
                    pe = jnp.exp2((s - m) * (scale * math.log2(math.e)))
                    l = jnp.sum(pe, axis=0, keepdims=True)
                    pT = pe * (1.0 / l)
                    p32[it, p, :, ln] = pT
                    p16[it, p, 0:KEYS, ln] = pT.astype(BF)
                    o = nn(qkvT[it, 512 + 32 * h:544 + 32 * h, tok], p16[it, p, :, ln])
                    mixT[it, 32 * h:32 * h + 32, tok] = o.astype(BF)
        middle = u + nn(woT[...], mixT[it, 0:D, :]) + lanes2(vecs.at[4])
        ln_forward(middle, lanes2(vecs.at[5]), lanes2(vecs.at[6]), unit2.at[it], inv2.at[it], n2T.at[it])
        n2 = n2T[it, 0:D, :]
        for c in range(FF // 128):
            rows = slice(c * 128, c * 128 + 128)
            v = nn(wuT[rows, :], n2) + lanes2(ubv.at[rows])
            v2 = v * v
            t = jnp.tanh(v * (C0 + C1 * v2))
            h1 = 0.5 + 0.5 * t
            hid = v * h1
            gp[it, rows, :] = h1 + (hid - hid * h1) * (2.0 * C0 + 6.0 * C1 * v2)
            hT[it, rows, :] = hid.astype(BF)
        return middle + nn(wdT[...], hT[it, 0:FF, :]) + lanes2(vecs.at[7])

    def backward(g, it):
        low = g.astype(BF)
        awd_ref[...] += nt(hT[it], low)
        for c in range(FF // 128):
            rows = slice(c * 128, c * 128 + 128)
            dh = nn(wd_ref[rows, :], low)
            goT[rows, :] = (dh * gp[it, rows, :]).astype(BF)
        dpre = goT[...]
        awu_ref[...] += nt(n2T[it], dpre)
        dn2 = nn(wu_ref[...], dpre)
        dmid = g + ln_backward(dn2, unit2[it], inv2[it], lanes2(vecs.at[5]), aln.at[2], aln.at[3])
        alow = dmid.astype(BF)
        awo_ref[...] += nt(mixT[it], alow)
        dmix = nn(wo_ref[...], alow).astype(BF)
        for p in range(2):
            tok = slice(p * 128, p * 128 + 128)
            for h in range(HEADS):
                bd[p, 32 * h:32 * h + 32, 128 * h:128 * h + 128] = dmix[32 * h:32 * h + 32, tok]
            for h2 in range(HEADS // 2):
                dp2 = nn(vN[it, p, 0:KEYS, :], bd[p, :, 256 * h2:256 * h2 + 256])
                for hh in range(2):
                    h = h2 * 2 + hh
                    ln = slice(128 * h, 128 * h + 128)
                    hr = slice(32 * h, 32 * h + 32)
                    pT = p32[it, p, :, ln]
                    t = pT * dp2[:, 128 * hh:128 * hh + 128]
                    dsum = jnp.sum(t, axis=0, keepdims=True)
                    ds16[p, 0:KEYS, ln] = (t - pT * dsum).astype(BF)
                    ds = ds16[p, :, ln]
                    dqkvT[32 * h:32 * h + 32, tok] = (nn(qkvT[it, 256 + 32 * h:288 + 32 * h, tok], ds) * scale).astype(BF)
                    dqkvT[256 + 32 * h:288 + 32 * h, tok] = (nt(qkvT[it, hr, tok], ds) * scale).astype(BF)
                    dqkvT[512 + 32 * h:544 + 32 * h, tok] = nt(dmix[hr, tok], p16[it, p, :, ln]).astype(BF)
        dqkv = dqkvT[...]
        awqkv_ref[...] += nt(n1T[it], dqkv)
        dn1 = nn(wqkv[...], dqkv)
        return dmid + ln_backward(dn1, unit1[it], inv1[it], lanes2(vecs.at[0]), aln.at[0], aln.at[1])

    eT = e_ref[...].T.astype(F32)
    u1 = x_ref[...].T.astype(F32) + eT
    s1 = forward(u1, 0).astype(BF)
    st_ref[0] = s1.T
    u2 = s1.astype(F32) + eT
    s2 = forward(u2, 1).astype(BF)
    st_ref[1] = s2.T
    g2 = backward(g_ref[...].T.astype(F32), 1)
    g2l = g2.astype(BF)
    gr_ref[1] = g2l.T
    g1 = backward(g2l.astype(F32), 0)
    gr_ref[0] = g1.astype(BF).T

    @pl.when(step == steps - 1)
    def _():
        for i in range(4):
            aln_ref[i:i + 1, :] = jnp.sum(aln[i].T, axis=0, keepdims=True)


def compute(offset, x, e, g, used, params, rows):
    (n1g, n1b, wq, qb, wk, wv, vb, wo, ob, n2g, n2b, wu, ub, wd, db) = params
    row = lambda v: v.reshape(1, -1)
    steps = rows // GROUP
    blk = pl.BlockSpec((GROUP, 256), lambda i, off: (off[0] + i, 0))
    full = lambda a: pl.BlockSpec(a.shape, lambda i, off: (0,) * a.ndim)
    ws = [row(n1g), row(n1b), wq, row(qb), wk, wv, row(vb), wo, row(ob), row(n2g), row(n2b), wu, row(ub), wd, row(db)]
    outs = [
        jax.ShapeDtypeStruct((2, rows, 256), BF),
        jax.ShapeDtypeStruct((2, rows, 256), BF),
        jax.ShapeDtypeStruct((1040, 256), F32),
        jax.ShapeDtypeStruct((272, 1024), F32),
        jax.ShapeDtypeStruct((272, 768), F32),
        jax.ShapeDtypeStruct((272, 256), F32),
        jax.ShapeDtypeStruct((8, 256), F32),
    ]
    oblk = pl.BlockSpec((2, GROUP, 256), lambda i, off: (0, i, 0))
    return pl.pallas_call(
        kernel,
        out_shape=outs,
        grid_spec=pltpu.PrefetchScalarGridSpec(
            num_scalar_prefetch=1,
            grid=(steps,),
            in_specs=[blk, blk, blk, pl.BlockSpec(memory_space=pltpu.SMEM)] + [full(w) for w in ws],
            out_specs=[oblk, oblk] + [full(o) for o in outs[2:]],
            scratch_shapes=[
                pltpu.VMEM((768, 256), BF), pltpu.VMEM((256, 256), BF), pltpu.VMEM((1024, 256), BF),
                pltpu.VMEM((256, 1024), BF), pltpu.VMEM((256, 768), BF),
                pltpu.VMEM((8, 256, 128), F32), pltpu.VMEM((1024, 128), F32),
                pltpu.VMEM((2, 272, GROUP), BF),
                pltpu.VMEM((2, 768, GROUP), BF),
                pltpu.VMEM((2, 2, 128, 256), BF),
                pltpu.VMEM((2, 2, KEYS, 1024), F32),
                pltpu.VMEM((2, 2, 128, 1024), BF),
                pltpu.VMEM((2, 272, GROUP), BF),
                pltpu.VMEM((2, 256, GROUP), F32), pltpu.VMEM((2, 1, GROUP), F32),
                pltpu.VMEM((2, 256, GROUP), F32), pltpu.VMEM((2, 1, GROUP), F32),
                pltpu.VMEM((2, 272, GROUP), BF),
                pltpu.VMEM((2, 1024, GROUP), F32),
                pltpu.VMEM((2, 1040, GROUP), BF),
                pltpu.VMEM((2, 256, 1024), BF),
                pltpu.VMEM((2, 128, 1024), BF),
                pltpu.VMEM((768, GROUP), BF),
                pltpu.VMEM((1024, GROUP), BF),
                pltpu.VMEM((4, 256, 128), F32),
            ],
        ),
        compiler_params=pltpu.CompilerParams(vmem_limit_bytes=56 * 1024 * 1024),
    )(offset, x, e, g, used, *ws)


def body(block_input, embedding, out_grad, example_counts, example_lengths, *params):
    section = lax.axis_index("section")
    local = block_input.shape[0]
    rows = local // 2
    prompts = rows // SLOTS
    counts = lax.dynamic_slice_in_dim(example_counts, section * prompts, prompts, 0)
    lengths = lax.dynamic_slice_in_dim(example_lengths, section * prompts, prompts, 0)
    slots = jnp.arange(lengths.shape[1])
    used = jnp.sum(jnp.where(slots[None, :] < counts[:, None], lengths, 0), axis=1)
    offset = (section * (rows // GROUP)).astype(jnp.int32).reshape(1)
    st, gr, awd, awu, awqkv, awo, aln = compute(offset, block_input, embedding, out_grad, used, params, rows)

    def exchange(pair):
        mine = lax.dynamic_index_in_dim(pair, section, 0, keepdims=False)
        other = lax.dynamic_index_in_dim(pair, 1 - section, 0, keepdims=False)
        got = lax.ppermute(other, "section", [(0, 1), (1, 0)])
        first = jnp.where(section == 0, mine, got)
        second = jnp.where(section == 0, got, mine)
        return jnp.concatenate([first, second], axis=0)[None]

    awd, awu, awqkv, awo, aln = lax.psum((awd, awu, awqkv, awo, aln), ("section", "dp"))
    return (
        exchange(st),
        exchange(gr).astype(F32),
        aln[0],
        aln[1],
        awqkv[:256, :256],
        awqkv[256, :256],
        awqkv[:256, 256:512],
        awqkv[:256, 512:],
        awqkv[256, 512:],
        awo[:256],
        awo[256],
        aln[2],
        aln[3],
        awu[:256],
        awu[256],
        awd[:1024],
        awd[1024],
    )


def solution(mesh):
    placed = (P("dp", None),) * 3 + (P("dp"), P("dp", None)) + (P(),) * 15
    return jax.shard_map(
        body,
        mesh=mesh,
        in_specs=placed,
        out_specs=(P("section", "dp", None),) * 2 + (P(),) * 15,
        check_vma=False,
    )
```

```python
import functools
import math

import jax
import jax.numpy as jnp
from jax import lax
from jax.experimental import pallas as pl
from jax.experimental.pallas import tpu as pltpu
from jax.sharding import PartitionSpec as P

BF = jnp.bfloat16
F32 = jnp.float32
SLOTS = 128
HEADS = 8
KEYS = 112
GROUP = 256
EPS = 1e-5


def nn(a, b):
    return lax.dot_general(a, b, (((1,), (0,)), ((), ())), preferred_element_type=F32)


def nt(a, b):
    return lax.dot_general(a, b, (((1,), (1,)), ((), ())), preferred_element_type=F32)


def ln_forward(u, gain, bias, unit_ref, inv_ref, n_ref):
    d = u.shape[0]
    mean = jnp.sum(u, axis=0, keepdims=True) * (1.0 / d)
    c = u - mean
    var = jnp.sum(c * c, axis=0, keepdims=True) * (1.0 / d)
    inv = lax.rsqrt(var + EPS)
    unit = c * inv
    unit_ref[...] = unit
    inv_ref[...] = inv
    n_ref[0:d, :] = (unit * gain + bias).astype(BF)


def lanes2(ref):
    v = ref[...]
    return jnp.concatenate([v, v], axis=1)


def fold(v):
    return v[:, :128] + v[:, 128:]


def ln_backward(gn, unit, inv, gain, gain_acc, bias_acc):
    d = gn.shape[0]
    t = gn * unit
    gain_acc[...] += fold(t)
    bias_acc[...] += fold(gn)
    s = gn * gain
    m1 = jnp.sum(s, axis=0, keepdims=True) * (1.0 / d)
    m2 = jnp.sum(t * gain, axis=0, keepdims=True) * (1.0 / d)
    return inv * (s - m1 - unit * m2)


C0 = math.sqrt(2.0 / math.pi)
C1 = C0 * 0.044715


MESH = pl.DeviceIdType.MESH
PARTS = 3


def plan(dp_bits):
    first = [("dp", 1)]
    turned = [("dp", 2), ("section", 1), ("dp", 4)]
    last = [("dp", 1 << b) for b in range(3, dp_bits)]
    return [first + turned[p:] + turned[:p] + last for p in range(PARTS)]


def kernel(dp_bits, x_hbm, e_hbm, g_hbm, counts_ref, lengths_ref,
           n1g_ref, n1b_ref, wq_ref, qb_ref, wk_ref, wv_ref, vb_ref, wo_ref, ob_ref,
           n2g_ref, n2b_ref, wu_ref, ub_ref, wd_ref, db_ref,
           st_hbm, gr_hbm, sums_ref, vec_ref,
           xv, ev, gv, stS, grS, used_v,
           wqkvT, woT, wuT, wdT, wqkv, vecs, ubv,
           n1T, qkvT, vN, p32, p16, mixT, unit1, inv1, unit2, inv2, n2T, gp, hT,
           bd, ds16, dqkvT, goT, aln, acc, ones_acc, send_buf, recv_buf, vec_send, vec_recv,
           in_sem, local_sem, ex_send, ex_recv, rs_send, rs_recv, ag_send, ag_recv, vs_send, vs_recv):
    D = 256
    FF = 1024
    scale = 32 ** -0.5
    rows = xv.shape[0]
    groups = rows // GROUP
    section = lax.axis_index("section")
    dp = lax.axis_index("dp")
    orders = plan(dp_bits)

    def bit_of(axis, weight):
        return section if axis == "section" else lax.rem(lax.div(dp, weight), 2)

    def across(axis, weight):
        v = bit_of(axis, weight)
        if axis == "section":
            return (1 - section, dp)
        return (section, dp + (1 - 2 * v) * weight)

    barrier = pltpu.get_barrier_semaphore()
    for axis, weight in orders[0]:
        pl.semaphore_signal(barrier, inc=1, device_id=across(axis, weight), device_id_type=MESH)

    def load(g, k):
        src = (x_hbm, e_hbm, g_hbm)[k]
        dst = (xv, ev, gv)[k]
        start = pl.multiple_of(g * GROUP, GROUP)
        return pltpu.make_async_copy(
            src.at[pl.ds(pl.multiple_of(section * rows, GROUP) + start, GROUP), :],
            dst.at[pl.ds(start, GROUP), :], in_sem.at[g, k])

    def start_loads(g, c):
        for k in range(3):
            load(g, k).start()
        return c
    lax.fori_loop(0, groups, start_loads, 0)

    wqkvT[0:256, :] = wq_ref[...].T
    wqkvT[256:512, :] = wk_ref[...].T
    wqkvT[512:768, :] = wv_ref[...].T
    woT[...] = wo_ref[...].T
    wuT[...] = wu_ref[...].T
    wdT[...] = wd_ref[...].T
    wqkv[:, 0:256] = wq_ref[...]
    wqkv[:, 256:512] = wk_ref[...]
    wqkv[:, 512:768] = wv_ref[...]
    for i, r in enumerate((n1g_ref, n1b_ref, qb_ref, vb_ref, ob_ref, n2g_ref, n2b_ref, db_ref)):
        vecs[i] = jnp.broadcast_to(r[...].astype(F32)[None, :], (128, D)).T
    ubv[...] = jnp.broadcast_to(ub_ref[...].astype(F32)[None, :], (128, FF)).T
    acc[...] = jnp.zeros_like(acc)
    ones_acc[...] = jnp.zeros_like(ones_acc)
    aln[...] = jnp.zeros_like(aln)
    bd[...] = jnp.zeros_like(bd)
    ds16[...] = jnp.zeros_like(ds16)
    p16[...] = jnp.zeros_like(p16)
    for it in range(2):
        n1T[it, D:, :] = jnp.ones((16, GROUP), BF)
        mixT[it, D:, :] = jnp.ones((16, GROUP), BF)
        n2T[it, D:, :] = jnp.ones((16, GROUP), BF)
        hT[it, FF:, :] = jnp.ones((16, GROUP), BF)
    prompts = rows // SLOTS
    at_most = lengths_ref.shape[1]
    j_iota = lax.broadcasted_iota(jnp.int32, (1, at_most), 1)
    for p in range(prompts):
        count = counts_ref[section * prompts + p]
        kept = jnp.where(j_iota < count, lengths_ref[pl.ds(section * prompts + p, 1), :], 0)
        total = jnp.sum(kept.astype(F32), axis=1, keepdims=True).astype(jnp.int32)
        used_v[p:p + 1, :] = jnp.broadcast_to(total, (1, 128))

    k_iota = lax.broadcasted_iota(jnp.int32, (KEYS, SLOTS), 0)
    q_iota = lax.broadcasted_iota(jnp.int32, (KEYS, SLOTS), 1)

    def out_copies(g, k):
        stage, out = ((stS, st_hbm), (grS, gr_hbm))[k]
        here = pl.ds(pl.multiple_of(g * GROUP, GROUP), GROUP)
        there = pl.ds(pl.multiple_of(section * rows, GROUP) + pl.multiple_of(g * GROUP, GROUP), GROUP)
        own = pltpu.make_async_copy(stage.at[section, here, :], out.at[there, :], local_sem.at[g, k])
        sent = pltpu.make_async_remote_copy(
            src_ref=stage.at[1 - section, here, :], dst_ref=out.at[there, :],
            send_sem=ex_send.at[g, k], recv_sem=ex_recv.at[g, k],
            device_id=(1 - section, dp), device_id_type=MESH)
        return own, sent

    pl.semaphore_wait(barrier, len(orders[0]))

    def group(g, carry):
        here = pl.ds(pl.multiple_of(g * GROUP, GROUP), GROUP)
        masks = []
        for p in range(2):
            used = used_v[pl.ds(g * 2 + p, 1), :]
            masks.append(jnp.where((k_iota <= q_iota) & (k_iota < used), 0.0, -1e30).astype(F32))

        def forward(u, it):
            ln_forward(u, lanes2(vecs.at[0]), lanes2(vecs.at[1]), unit1.at[it], inv1.at[it], n1T.at[it])
            n1 = n1T[it, 0:D, :]
            qkvT[it, 0:256, :] = (nn(wqkvT[0:256, :], n1) + lanes2(vecs.at[2])).astype(BF)
            qkvT[it, 256:512, :] = nn(wqkvT[256:512, :], n1).astype(BF)
            qkvT[it, 512:768, :] = (nn(wqkvT[512:768, :], n1) + lanes2(vecs.at[3])).astype(BF)
            for p in range(2):
                tok = slice(p * 128, p * 128 + 128)
                kN = qkvT[it, 256:512, tok].T
                vN[it, p] = qkvT[it, 512:768, tok].T
                for h in range(HEADS):
                    bd[p, 32 * h:32 * h + 32, 128 * h:128 * h + 128] = qkvT[it, 32 * h:32 * h + 32, tok]
                for h2 in range(HEADS // 2):
                    sT2 = nn(kN[:KEYS], bd[p, :, 256 * h2:256 * h2 + 256])
                    for hh in range(2):
                        h = h2 * 2 + hh
                        ln = slice(128 * h, 128 * h + 128)
                        s = sT2[:, 128 * hh:128 * hh + 128] + masks[p]
                        m = jnp.max(s, axis=0, keepdims=True)
                        pe = jnp.exp2((s - m) * (scale * math.log2(math.e)))
                        l = jnp.sum(pe, axis=0, keepdims=True)
                        pT = pe * (1.0 / l)
                        p32[it, p, :, ln] = pT
                        p16[it, p, 0:KEYS, ln] = pT.astype(BF)
                        o = nn(qkvT[it, 512 + 32 * h:544 + 32 * h, tok], p16[it, p, :, ln])
                        mixT[it, 32 * h:32 * h + 32, tok] = o.astype(BF)
            middle = u + nn(woT[...], mixT[it, 0:D, :]) + lanes2(vecs.at[4])
            ln_forward(middle, lanes2(vecs.at[5]), lanes2(vecs.at[6]), unit2.at[it], inv2.at[it], n2T.at[it])
            n2 = n2T[it, 0:D, :]
            for c in range(FF // 128):
                rows = slice(c * 128, c * 128 + 128)
                v = nn(wuT[rows, :], n2) + lanes2(ubv.at[rows])
                v2 = v * v
                t = jnp.tanh(v * (C0 + C1 * v2))
                h1 = 0.5 + 0.5 * t
                hid = v * h1
                gp[it, rows, :] = h1 + (hid - hid * h1) * (2.0 * C0 + 6.0 * C1 * v2)
                hT[it, rows, :] = hid.astype(BF)
            return middle + nn(wdT[...], hT[it, 0:FF, :]) + lanes2(vecs.at[7])

        def backward(g, it):
            low = g.astype(BF)
            t = nt(hT[it], low)
            acc[0:FF, :] += t[0:FF]
            ones_acc[0] += t[FF:]
            for c in range(FF // 128):
                rows = slice(c * 128, c * 128 + 128)
                dh = nn(wd_ref[rows, :], low)
                goT[rows, :] = (dh * gp[it, rows, :]).astype(BF)
            dpre = goT[...]
            for j in range(FF // D):
                t = nt(n2T[it], goT[j * D:j * D + D, :])
                acc[FF + j * D:FF + j * D + D, :] += t[0:D]
                ones_acc[1 + j] += t[D:]
            dn2 = nn(wu_ref[...], dpre)
            dmid = g + ln_backward(dn2, unit2[it], inv2[it], lanes2(vecs.at[5]), aln.at[2], aln.at[3])
            alow = dmid.astype(BF)
            t = nt(mixT[it], alow)
            acc[2 * FF + 3 * D:2 * FF + 4 * D, :] += t[0:D]
            ones_acc[8] += t[D:]
            dmix = nn(wo_ref[...], alow).astype(BF)
            for p in range(2):
                tok = slice(p * 128, p * 128 + 128)
                for h in range(HEADS):
                    bd[p, 32 * h:32 * h + 32, 128 * h:128 * h + 128] = dmix[32 * h:32 * h + 32, tok]
                for h2 in range(HEADS // 2):
                    dp2 = nn(vN[it, p, 0:KEYS, :], bd[p, :, 256 * h2:256 * h2 + 256])
                    for hh in range(2):
                        h = h2 * 2 + hh
                        ln = slice(128 * h, 128 * h + 128)
                        hr = slice(32 * h, 32 * h + 32)
                        pT = p32[it, p, :, ln]
                        t = pT * dp2[:, 128 * hh:128 * hh + 128]
                        dsum = jnp.sum(t, axis=0, keepdims=True)
                        ds16[p, 0:KEYS, ln] = (t - pT * dsum).astype(BF)
                        ds = ds16[p, :, ln]
                        dqkvT[32 * h:32 * h + 32, tok] = (nn(qkvT[it, 256 + 32 * h:288 + 32 * h, tok], ds) * scale).astype(BF)
                        dqkvT[256 + 32 * h:288 + 32 * h, tok] = (nt(qkvT[it, hr, tok], ds) * scale).astype(BF)
                        dqkvT[512 + 32 * h:544 + 32 * h, tok] = nt(dmix[hr, tok], p16[it, p, :, ln]).astype(BF)
            dqkv = dqkvT[...]
            for j in range(3):
                t = nt(n1T[it], dqkvT[j * D:j * D + D, :])
                acc[2 * FF + j * D:2 * FF + j * D + D, :] += t[0:D]
                ones_acc[5 + j] += t[D:]
            dn1 = nn(wqkv[...], dqkv)
            return dmid + ln_backward(dn1, unit1[it], inv1[it], lanes2(vecs.at[0]), aln.at[0], aln.at[1])


        for k in range(3):
            load(g, k).wait()
        eT = ev[here, :].T.astype(F32)
        u1 = xv[here, :].T.astype(F32) + eT
        s1 = forward(u1, 0).astype(BF)
        stS[0, here, :] = s1.T
        u2 = s1.astype(F32) + eT
        s2 = forward(u2, 1).astype(BF)
        stS[1, here, :] = s2.T
        for c in out_copies(g, 0):
            c.start()
        g2 = backward(gv[here, :].T.astype(F32), 1)
        g2l = g2.astype(BF)
        grS[1, here, :] = g2l.T
        g1 = backward(g2l.astype(F32), 0)
        grS[0, here, :] = g1.astype(BF).T
        for c in out_copies(g, 1):
            c.start()
        return carry

    lax.fori_loop(0, groups, group, 0)

    for i, j in enumerate((0, 1, 5, 6)):
        vec_ref[j:j + 1, :] = jnp.sum(aln[i].T, axis=0, keepdims=True)
    for i, j in ((0, 7), (1, 8), (2, 9), (3, 10), (4, 11), (5, 2), (7, 3), (8, 4)):
        vec_ref[j:j + 1, :] = ones_acc[i, 0:1, :]
    vec_ref[12:16, :] = jnp.zeros((4, D), F32)

    total_rows = acc.shape[0]
    part_rows = total_rows // PARTS
    offs = [p * part_rows for p in range(PARTS)]
    sizes = [part_rows] * PARTS
    pending = [None] * PARTS
    history = [[] for _ in range(PARTS)]
    used_rows = 0
    vec_pending = None

    def finish_vec():
        nonlocal vec_pending
        if vec_pending is not None:
            copy, s = vec_pending
            copy.wait()
            vec_ref[...] = vec_ref[...] + vec_recv[s]
            vec_pending = None

    for s in range(len(orders[0])):
        for p in range(PARTS):
            if pending[p] is not None:
                pending[p]()
            axis, weight = orders[p][s]
            v = bit_of(axis, weight)
            off, size = offs[p], sizes[p]
            halve = size >= 32
            n = size // 2 if halve else size
            src_off = pl.multiple_of(off + (1 - v) * n, 16) if halve else off
            keep = pl.multiple_of(off + v * n, 16) if halve else off
            region = pl.ds(used_rows, n)
            used_rows += n
            send_buf[region, :] = acc[pl.ds(src_off, n), :].astype(BF)
            copy = pltpu.make_async_remote_copy(
                src_ref=send_buf.at[region, :], dst_ref=recv_buf.at[region, :],
                send_sem=rs_send.at[s, p], recv_sem=rs_recv.at[s, p],
                device_id=across(axis, weight), device_id_type=MESH)
            copy.start()

            def finish(copy=copy, keep=keep, n=n, region=region, halve=halve):
                copy.wait()
                own = acc[pl.ds(keep, n), :]
                if not halve:
                    own = own.astype(BF).astype(F32)
                acc[pl.ds(keep, n), :] = own + recv_buf[region, :].astype(F32)
            pending[p] = finish
            if halve:
                history[p].append((axis, weight, off, n, keep))
                offs[p], sizes[p] = keep, n
        finish_vec()
        axis, weight = orders[0][s]
        vec_send[s] = vec_ref[...]
        copy = pltpu.make_async_remote_copy(
            src_ref=vec_send.at[s], dst_ref=vec_recv.at[s],
            send_sem=vs_send.at[s], recv_sem=vs_recv.at[s],
            device_id=across(axis, weight), device_id_type=MESH)
        copy.start()
        vec_pending = (copy, s)
    finish_vec()
    for p in range(PARTS):
        pending[p]()
        sums_ref[pl.ds(offs[p], sizes[p]), :] = acc[pl.ds(offs[p], sizes[p]), :].astype(BF)
    last = [None] * PARTS
    for s in range(max(len(h) for h in history)):
        for p in range(PARTS):
            if last[p] is not None:
                last[p].wait()
            axis, weight, off, n, keep = history[p][-1 - s]
            copy = pltpu.make_async_remote_copy(
                src_ref=sums_ref.at[pl.ds(keep, n), :], dst_ref=sums_ref.at[pl.ds(keep, n), :],
                send_sem=ag_send.at[s, p], recv_sem=ag_recv.at[s, p],
                device_id=across(axis, weight), device_id_type=MESH)
            copy.start()
            last[p] = copy
    for p in range(PARTS):
        last[p].wait()

    def finish_out(g, c):
        for k in range(2):
            own, sent = out_copies(g, k)
            own.wait()
            sent.wait()
        return c
    lax.fori_loop(0, groups, finish_out, 0)


def compute(x, e, g, counts, lengths, params, dp_size):
    local = x.shape[0]
    rows = local // 2
    groups = rows // GROUP
    dp_bits = dp_size.bit_length() - 1
    stages = dp_bits + 1
    hbm = pl.BlockSpec(memory_space=pl.ANY)
    smem = pl.BlockSpec(memory_space=pltpu.SMEM)
    vmem = pl.BlockSpec(memory_space=pltpu.VMEM)
    outs = [
        jax.ShapeDtypeStruct((local, 256), BF),
        jax.ShapeDtypeStruct((local, 256), BF),
        jax.ShapeDtypeStruct((3072, 256), BF),
        jax.ShapeDtypeStruct((16, 256), F32),
    ]
    buf_rows = 0
    size = 3072 // PARTS
    for _ in range(stages):
        n = size // 2 if size >= 32 else size
        buf_rows += n * PARTS
        size = n
    return pl.pallas_call(
        functools.partial(kernel, dp_bits),
        out_shape=outs,
        in_specs=[hbm, hbm, hbm, smem, vmem] + [vmem] * 15,
        out_specs=[hbm, hbm, vmem, vmem],
        scratch_shapes=[
            pltpu.VMEM((rows, 256), BF), pltpu.VMEM((rows, 256), BF), pltpu.VMEM((rows, 256), BF),
            pltpu.VMEM((2, rows, 256), BF), pltpu.VMEM((2, rows, 256), BF),
            pltpu.VMEM((rows // SLOTS, 128), jnp.int32),
            pltpu.VMEM((768, 256), BF), pltpu.VMEM((256, 256), BF), pltpu.VMEM((1024, 256), BF),
            pltpu.VMEM((256, 1024), BF), pltpu.VMEM((256, 768), BF),
            pltpu.VMEM((8, 256, 128), F32), pltpu.VMEM((1024, 128), F32),
            pltpu.VMEM((2, 272, GROUP), BF),
            pltpu.VMEM((2, 768, GROUP), BF),
            pltpu.VMEM((2, 2, 128, 256), BF),
            pltpu.VMEM((2, 2, KEYS, 1024), F32),
            pltpu.VMEM((2, 2, 128, 1024), BF),
            pltpu.VMEM((2, 272, GROUP), BF),
            pltpu.VMEM((2, 256, GROUP), F32), pltpu.VMEM((2, 1, GROUP), F32),
            pltpu.VMEM((2, 256, GROUP), F32), pltpu.VMEM((2, 1, GROUP), F32),
            pltpu.VMEM((2, 272, GROUP), BF),
            pltpu.VMEM((2, 1024, GROUP), F32),
            pltpu.VMEM((2, 1040, GROUP), BF),
            pltpu.VMEM((2, 256, 1024), BF),
            pltpu.VMEM((2, 128, 1024), BF),
            pltpu.VMEM((768, GROUP), BF),
            pltpu.VMEM((1024, GROUP), BF),
            pltpu.VMEM((4, 256, 128), F32),
            pltpu.VMEM((3072, 256), F32),
            pltpu.VMEM((9, 16, 256), F32),
            pltpu.VMEM((buf_rows, 256), BF), pltpu.VMEM((buf_rows, 256), BF),
            pltpu.VMEM((stages, 16, 256), F32), pltpu.VMEM((stages, 16, 256), F32),
            pltpu.SemaphoreType.DMA((groups, 3)),
            pltpu.SemaphoreType.DMA((groups, 2)),
            pltpu.SemaphoreType.DMA((groups, 2)),
            pltpu.SemaphoreType.DMA((groups, 2)),
            pltpu.SemaphoreType.DMA((stages, PARTS)),
            pltpu.SemaphoreType.DMA((stages, PARTS)),
            pltpu.SemaphoreType.DMA((stages, PARTS)),
            pltpu.SemaphoreType.DMA((stages, PARTS)),
            pltpu.SemaphoreType.DMA((stages,)),
            pltpu.SemaphoreType.DMA((stages,)),
        ],
        compiler_params=pltpu.CompilerParams(
            vmem_limit_bytes=56 * 1024 * 1024, collective_id=0, has_side_effects=True),
    )(x, e, g, counts, lengths, *params)


def widen_kernel(st_ref, gr_ref, sums_ref, vec_ref, st_out, gr_out, n1g, n1b, wq, qb, wk, wv, vb, wo, ob, n2g, n2b, wu, ub, wd, db):
    st_out[0] = st_ref[...]
    gr_out[0] = gr_ref[...].astype(F32)

    @pl.when(pl.program_id(0) == 0)
    def _():
        wd[...] = sums_ref[0:1024, :].astype(F32)
        for j in range(4):
            wu[:, 256 * j:256 * j + 256] = sums_ref[1024 + 256 * j:1280 + 256 * j, :].astype(F32)
            ub[256 * j:256 * j + 256] = vec_ref[8 + j]
        for j, r in enumerate((wq, wk, wv, wo)):
            r[...] = sums_ref[2048 + 256 * j:2304 + 256 * j, :].astype(F32)
        for j, r in enumerate((n1g, n1b, qb, vb, ob, n2g, n2b, db)):
            r[...] = vec_ref[j]


def widen(st, gr, sums, vec, params):
    local = st.shape[0]
    block = min(512, local)
    full = lambda a: pl.BlockSpec(a.shape, lambda i: (0,) * a.ndim)
    outs = [jax.ShapeDtypeStruct((1, local, 256), BF), jax.ShapeDtypeStruct((1, local, 256), F32)]
    outs += [jax.ShapeDtypeStruct(p.shape, F32) for p in params]
    blk = pl.BlockSpec((block, 256), lambda i: (i, 0))
    oblk = pl.BlockSpec((1, block, 256), lambda i: (0, i, 0))
    return pl.pallas_call(
        widen_kernel,
        grid=(local // block,),
        out_shape=outs,
        in_specs=[blk, blk, full(sums), full(vec)],
        out_specs=[oblk, oblk] + [full(o) for o in outs[2:]],
        compiler_params=pltpu.CompilerParams(vmem_limit_bytes=40 * 1024 * 1024),
    )(st, gr, sums, vec)


def solution(mesh):
    dp_size = mesh.shape["dp"]

    def body(x, e, g, counts, lengths, *params):
        st, gr, sums, vec = compute(x, e, g, counts, lengths, params, dp_size)
        return tuple(widen(st, gr, sums, vec, params))

    placed = (P("dp", None),) * 3 + (P("dp"), P("dp", None)) + (P(),) * 15
    return jax.shard_map(
        body,
        mesh=mesh,
        in_specs=placed,
        out_specs=(P("section", "dp", None),) * 2 + (P(),) * 15,
        check_vma=False,
    )
```

```python
import functools
import math

import jax
import jax.numpy as jnp
from jax import lax
from jax.experimental import pallas as pl
from jax.experimental.pallas import tpu as pltpu
from jax.sharding import PartitionSpec as P

BF = jnp.bfloat16
F32 = jnp.float32
SLOTS = 128
HEADS = 8
KEYS = 112
GROUP = 512
CH = 256
PG = GROUP // SLOTS
EPS = 1e-5


def nn(a, b):
    return lax.dot_general(a, b, (((1,), (0,)), ((), ())), preferred_element_type=F32)


def nt(a, b):
    return lax.dot_general(a, b, (((1,), (1,)), ((), ())), preferred_element_type=F32)


C0 = math.sqrt(2.0 / math.pi)
C1 = C0 * 0.044715
SCALE = 32 ** -0.5
D = 256
FF = 1024


def ln_forward(u_ref, gain, bias, unit_ref, inv_ref, n_ref, lanes):
    for b in range(lanes.start, lanes.stop, 128):
        ln = slice(b, b + 128)
        u = u_ref[:, ln]
        mean = jnp.sum(u, axis=0, keepdims=True) * (1.0 / D)
        c = u - mean
        var = jnp.sum(c * c, axis=0, keepdims=True) * (1.0 / D)
        inv = lax.rsqrt(var + EPS)
        unit = c * inv
        unit_ref[:, ln] = unit
        inv_ref[:, ln] = inv
        n_ref[0:D, ln] = (unit * gain[...] + bias[...]).astype(BF)


def ln_backward(gn_ref, res_ref, unit_ref, inv_ref, gain, gain_acc, bias_acc, out_ref, low_ref, lanes):
    for b in range(lanes.start, lanes.stop, 128):
        ln = slice(b, b + 128)
        gn = gn_ref[:, ln]
        unit = unit_ref[:, ln]
        t = gn * unit
        gain_acc[...] += t
        bias_acc[...] += gn
        s = gn * gain[...]
        m1 = jnp.sum(s, axis=0, keepdims=True) * (1.0 / D)
        m2 = jnp.sum(t * gain[...], axis=0, keepdims=True) * (1.0 / D)
        out = res_ref[:, ln] + inv_ref[:, ln] * (s - m1 - unit * m2)
        out_ref[:, ln] = out
        low_ref[:, ln] = out.astype(BF)


class Refs:
    pass


def chain(R, c, masks):
    L = slice(c * CH, c * CH + CH)
    prompts = range(c * CH // SLOTS, (c + 1) * CH // SLOTS)
    R.load(c)
    yield
    for it in range(2):
        ln_forward(R.uT, R.vecs.at[0], R.vecs.at[1], R.unit1.at[it], R.inv1.at[it], R.n1T.at[it], L)
        yield
        n1 = R.n1T[it, 0:D, L]
        for j, vec in ((0, 2), (1, None), (2, 3)):
            rows = slice(256 * j, 256 * j + 256)
            y = nn(R.wqkvT[rows, :], n1)
            if vec is not None:
                v = R.vecs[vec]
                y = y + jnp.concatenate([v] * (CH // 128), axis=1)
            R.qkvT[it, rows, L] = y.astype(BF)
        yield
        for p in prompts:
            tok = slice(p * 128, p * 128 + 128)
            for h in range(HEADS):
                R.bdq[p, h // 2, 32 * (h % 4):32 * (h % 4) + 32, 128 * (h % 2):128 * (h % 2) + 128] = R.qkvT[it, 32 * h:32 * h + 32, tok]
            R.kN[p] = R.qkvT[it, 256:512, tok].T
            for h2 in range(HEADS // 2):
                R.sc[p, :, 256 * h2:256 * h2 + 256] = nn(R.kN[p, 0:KEYS, 128 * (h2 // 2):128 * (h2 // 2) + 128], R.bdq[p, h2])
            R.vN[it, p] = R.qkvT[it, 512:768, tok].T
            yield
        for p in prompts:
            tok = slice(p * 128, p * 128 + 128)
            for h in range(HEADS):
                ln = slice(128 * h, 128 * h + 128)
                s = R.sc[p, :, ln] + masks[p]
                m = jnp.max(s, axis=0, keepdims=True)
                pe = jnp.exp2((s - m) * (SCALE * math.log2(math.e)))
                l = jnp.sum(pe, axis=0, keepdims=True)
                pT = pe * (1.0 / l)
                R.p32[it, p, :, ln] = pT
                R.p16[it, p, 0:KEYS, ln] = pT.astype(BF)
            yield
            for h2 in range(HEADS // 2):
                ln = slice(256 * h2, 256 * h2 + 256)
                o = nn(R.qkvT[it, 512 + 64 * h2:576 + 64 * h2, tok], R.p16[it, p, :, ln])
                R.mixT[it, 64 * h2:64 * h2 + 32, tok] = o[0:32, 0:128].astype(BF)
                R.mixT[it, 64 * h2 + 32:64 * h2 + 64, tok] = o[32:64, 128:256].astype(BF)
            yield
        y = nn(R.woT[...], R.mixT[it, 0:D, L])
        for b in range(L.start, L.stop, 128):
            R.mid[:, b:b + 128] = R.uT[:, b:b + 128] + R.vecs[4] + y[:, b - L.start:b - L.start + 128]
        yield
        for p in prompts:
            for h in range(HEADS):
                ln = slice(128 * h, 128 * h + 128)
                R.pN[it, p, :, ln] = R.p16[it, p, :, ln].T
        ln_forward(R.mid, R.vecs.at[5], R.vecs.at[6], R.unit2.at[it], R.inv2.at[it], R.n2T.at[it], L)
        yield
        n2 = R.n2T[it, 0:D, L]
        for half in range(2):
            rows = slice(512 * half, 512 * half + 512)
            R.pre[rows, L] = nn(R.wuT[rows, :], n2)
            yield
            for r in range(rows.start, rows.stop, 32):
                for b in range(L.start, L.stop, 128):
                    at = (slice(r, r + 32), slice(b, b + 128))
                    v = R.pre[at] + R.ubv[r:r + 32, :]
                    v2 = v * v
                    t = jnp.tanh(v * (C0 + C1 * v2))
                    h1 = 0.5 + 0.5 * t
                    hid = v * h1
                    R.gp[it, r:r + 32, b:b + 128] = h1 + (hid - hid * h1) * (2.0 * C0 + 6.0 * C1 * v2)
                    R.hT[it, r:r + 32, b:b + 128] = hid.astype(BF)
            yield
        y = nn(R.wdT[...], R.hT[it, 0:FF, L])
        for b in range(L.start, L.stop, 128):
            out = R.mid[:, b:b + 128] + R.vecs[7] + y[:, b - L.start:b - L.start + 128]
            R.finish_forward(it, b, out.astype(BF))
        if it == 1:
            R.send(c, 0)
        yield
    for it in (1, 0):
        for half in range(2):
            rows = slice(512 * half, 512 * half + 512)
            R.pre[rows, L] = nn(R.wd_ref[rows, :], R.lowT[it, :, L])
            yield
            for r in range(rows.start, rows.stop, 32):
                for b in range(L.start, L.stop, 128):
                    at = (slice(r, r + 32), slice(b, b + 128))
                    R.dpre[it, r:r + 32, b:b + 128] = (R.pre[at] * R.gp[it, r:r + 32, b:b + 128]).astype(BF)
            yield
        R.dn[:, L] = nn(R.wu_ref[...], R.dpre[it, :, L])
        yield
        ln_backward(R.dn, R.gT, R.unit2.at[it], R.inv2.at[it], R.vecs.at[5], R.aln.at[2], R.aln.at[3], R.gT, R.alow.at[it], L)
        yield
        R.dmixT[:, L] = nn(R.wo_ref[...], R.alow[it, :, L]).astype(BF)
        yield
        for p in prompts:
            tok = slice(p * 128, p * 128 + 128)
            for h in range(HEADS):
                R.bdo[p, h // 2, 32 * (h % 4):32 * (h % 4) + 32, 128 * (h % 2):128 * (h % 2) + 128] = R.dmixT[32 * h:32 * h + 32, tok]
            for h2 in range(HEADS // 2):
                R.sc[p, :, 256 * h2:256 * h2 + 256] = nn(R.vN[it, p, 0:KEYS, 128 * (h2 // 2):128 * (h2 // 2) + 128], R.bdo[p, h2])
            yield
        for p in prompts:
            tok = slice(p * 128, p * 128 + 128)
            for h in range(HEADS):
                ln = slice(128 * h, 128 * h + 128)
                pT = R.p32[it, p, :, ln]
                t = pT * R.sc[p, :, ln]
                dsum = jnp.sum(t, axis=0, keepdims=True)
                R.ds16[p, 0:KEYS, ln] = (t - pT * dsum).astype(BF)
                R.dsN[p, :, ln] = R.ds16[p, :, ln].T
            yield
            for h2 in range(HEADS // 2):
                r = 64 * h2
                ln = slice(256 * h2, 256 * h2 + 256)
                for base, left, right, scaled in (
                    (512, R.dmixT[r:r + 64, tok], R.pN[it, p, :, ln], None),
                    (0, R.qkvT[it, 256 + r:320 + r, tok], R.ds16[p, :, ln], SCALE),
                    (256, R.qkvT[it, r:r + 64, tok], R.dsN[p, :, ln], SCALE)):
                    d = nn(left, right)
                    top, low = d[0:32, 0:128], d[32:64, 128:256]
                    if scaled is not None:
                        top, low = top * scaled, low * scaled
                    R.dqkvT[it, base + r:base + r + 32, tok] = top.astype(BF)
                    R.dqkvT[it, base + r + 32:base + r + 64, tok] = low.astype(BF)
            yield
        R.dn[:, L] = nn(R.wqkv[...], R.dqkvT[it, :, L])
        yield
        ln_backward(R.dn, R.gT, R.unit1.at[it], R.inv1.at[it], R.vecs.at[0], R.aln.at[0], R.aln.at[1], R.gT, R.gl16, L)
        for b in range(L.start, L.stop, 128):
            R.finish_backward(it, b, R.gl16[:, b:b + 128])
        if it == 0:
            R.send(c, 1)
        yield


def weight_terms(R, it):
    for i in range(0, FF, 256):
        stop = i + 256 if i + 256 < FF else FF + 16
        R.add_wd(i, nt(R.hT[it, i:stop, :], R.lowT[it]))
        yield
    for j in range(FF // D):
        R.add_wu(j, nt(R.n2T[it], R.dpre[it, j * D:j * D + D, :]))
        yield
    R.add_wo(nt(R.mixT[it], R.alow[it]))
    yield
    for j in range(3):
        R.add_wqkv(j, nt(R.n1T[it], R.dqkvT[it, j * D:j * D + D, :]))
        yield


def run_group(R, masks, lag):
    chains = [chain(R, c, masks) for c in range(GROUP // CH)]
    counts = [0] * len(chains)
    done = [False] * len(chains)
    terms = []
    started = set()
    while not all(done) or terms:
        for i, ch in enumerate(chains):
            if done[i] or (i > 0 and counts[i] + lag > counts[i - 1] and not done[i - 1]):
                continue
            try:
                next(ch)
                counts[i] += 1
            except StopIteration:
                done[i] = True
        if min(counts) >= R.bwd1_done and 1 not in started:
            started.add(1)
            terms.append(weight_terms(R, 1))
        if all(done) and 0 not in started:
            started.add(0)
            terms.append(weight_terms(R, 0))
        for t in list(terms):
            try:
                next(t)
            except StopIteration:
                terms.remove(t)


SCRATCH = dict(
    wqkvT=((768, 256), BF), woT=((256, 256), BF), wuT=((1024, 256), BF), wdT=((256, 1024), BF), wqkv=((256, 768), BF),
    vecs=((8, 256, 128), F32), ubv=((1024, 128), F32),
    n1T=((2, 272, GROUP), BF), qkvT=((2, 768, GROUP), BF), kN=((PG, 128, 256), BF), vN=((2, PG, 128, 256), BF),
    bdq=((PG, 4, 128, 256), BF), bdo=((PG, 4, 128, 256), BF),
    sc=((PG, KEYS, 1024), F32), p32=((2, PG, KEYS, 1024), F32), p16=((2, PG, 128, 1024), BF), pN=((2, PG, 128, 1024), BF),
    ds16=((PG, 128, 1024), BF), dsN=((PG, 128, 1024), BF),
    mixT=((2, 272, GROUP), BF), uT=((256, GROUP), F32), eT=((256, GROUP), BF), mid=((256, GROUP), F32), gT=((256, GROUP), F32), dn=((256, GROUP), F32),
    gl16=((256, GROUP), BF),
    unit1=((2, 256, GROUP), F32), inv1=((2, 1, GROUP), F32), unit2=((2, 256, GROUP), F32), inv2=((2, 1, GROUP), F32),
    n2T=((2, 272, GROUP), BF), pre=((1024, GROUP), F32), gp=((2, 1024, GROUP), F32), hT=((2, 1040, GROUP), BF),
    lowT=((2, 256, GROUP), BF), dpre=((2, 1024, GROUP), BF), alow=((2, 256, GROUP), BF), dmixT=((256, GROUP), BF),
    dqkvT=((2, 768, GROUP), BF), aln=((4, 256, 128), F32))


def prologue(R, n1g, n1b, wq, qb, wk, wv, vb, wo, ob, n2g, n2b, wu, ub, wd, db):
    R.wqkvT[0:256, :] = wq[...].T
    R.wqkvT[256:512, :] = wk[...].T
    R.wqkvT[512:768, :] = wv[...].T
    R.woT[...] = wo[...].T
    R.wuT[...] = wu[...].T
    R.wdT[...] = wd[...].T
    R.wqkv[:, 0:256] = wq[...]
    R.wqkv[:, 256:512] = wk[...]
    R.wqkv[:, 512:768] = wv[...]
    for i, r in enumerate((n1g, n1b, qb, vb, ob, n2g, n2b, db)):
        R.vecs[i] = jnp.broadcast_to(r[...].astype(F32).reshape(1, D), (128, D)).T
    R.ubv[...] = jnp.broadcast_to(ub[...].astype(F32).reshape(1, FF), (128, FF)).T
    for r in (R.aln, R.bdq, R.bdo, R.ds16, R.p16):
        r[...] = jnp.zeros_like(r)
    for it in range(2):
        for r in (R.n1T, R.mixT, R.n2T):
            r[it, D:, :] = jnp.ones((16, GROUP), BF)
        R.hT[it, FF:, :] = jnp.ones((16, GROUP), BF)


LAG = 3
MESH = pl.DeviceIdType.MESH
PARTS = 3


def plan(dp_bits):
    first = [("dp", 1)]
    turned = [("dp", 2), ("section", 1), ("dp", 4)]
    last = [("dp", 1 << b) for b in range(3, dp_bits)]
    return [first + turned[p:] + turned[:p] + last for p in range(PARTS)]


def comm_scratch(rows, buf_rows, stages):
    blocks = rows // CH
    dma = pltpu.SemaphoreType.DMA
    return dict(
        xv=pltpu.VMEM((rows, 256), BF), ev=pltpu.VMEM((rows, 256), BF), gv=pltpu.VMEM((rows, 256), BF),
        stS=pltpu.VMEM((2, rows, 256), BF), grS=pltpu.VMEM((2, rows, 256), BF),
        used_v=pltpu.VMEM((rows // SLOTS, 128), jnp.int32),
        acc=pltpu.VMEM((3072, 256), F32), ones_acc=pltpu.VMEM((9, 16, 256), F32),
        send_buf=pltpu.VMEM((buf_rows, 256), BF), recv_buf=pltpu.VMEM((buf_rows, 256), BF),
        vec_send=pltpu.VMEM((stages, 16, 256), F32), vec_recv=pltpu.VMEM((stages, 16, 256), F32),
        in_sem=dma((blocks, 3)), local_sem=dma((blocks, 2)), ex_send=dma((blocks, 2)), ex_recv=dma((blocks, 2)),
        rs_send=dma((stages, PARTS)), rs_recv=dma((stages, PARTS)), ag_send=dma((stages, PARTS)), ag_recv=dma((stages, PARTS)),
        vs_send=dma((stages,)), vs_recv=dma((stages,)))


def kernel(dp_bits, x_hbm, e_hbm, g_hbm, counts_ref, lengths_ref, *refs):
    ws = refs[:15]
    st_hbm, gr_hbm, sums_ref, vec_ref = refs[15:19]
    R = Refs()
    for name, r in zip(list(SCRATCH) + list(comm_scratch(CH, 16, 1)), refs[19:]):
        setattr(R, name, r)
    R.wo_ref, R.wu_ref, R.wd_ref = ws[7], ws[11], ws[13]
    R.bwd1_done = 44
    aln, acc, ones_acc, send_buf, recv_buf, vec_send, vec_recv = R.aln, R.acc, R.ones_acc, R.send_buf, R.recv_buf, R.vec_send, R.vec_recv
    rs_send, rs_recv, ag_send, ag_recv, vs_send, vs_recv = R.rs_send, R.rs_recv, R.ag_send, R.ag_recv, R.vs_send, R.vs_recv
    rows = R.xv.shape[0]
    blocks = rows // CH
    section = lax.axis_index("section")
    dp = lax.axis_index("dp")
    orders = plan(dp_bits)

    def bit_of(axis, weight):
        return section if axis == "section" else lax.rem(lax.div(dp, weight), 2)

    def across(axis, weight):
        v = bit_of(axis, weight)
        if axis == "section":
            return (1 - section, dp)
        return (section, dp + (1 - 2 * v) * weight)

    barrier = pltpu.get_barrier_semaphore()
    for axis, weight in orders[0]:
        pl.semaphore_signal(barrier, inc=1, device_id=across(axis, weight), device_id_type=MESH)

    def fetch(b, k):
        src = (x_hbm, e_hbm, g_hbm)[k]
        dst = (R.xv, R.ev, R.gv)[k]
        start = pl.multiple_of(b * CH, CH)
        return pltpu.make_async_copy(
            src.at[pl.ds(pl.multiple_of(section * rows, CH) + start, CH), :],
            dst.at[pl.ds(start, CH), :], R.in_sem.at[b, k])

    def start_fetches(b, c):
        for k in range(3):
            fetch(b, k).start()
        return c
    lax.fori_loop(0, blocks, start_fetches, 0)

    prologue(R, *ws)
    acc[...] = jnp.zeros_like(acc)
    ones_acc[...] = jnp.zeros_like(ones_acc)
    prompts = rows // SLOTS
    at_most = lengths_ref.shape[1]
    j_iota = lax.broadcasted_iota(jnp.int32, (1, at_most), 1)
    for p in range(prompts):
        count = counts_ref[section * prompts + p]
        kept = jnp.where(j_iota < count, lengths_ref[pl.ds(section * prompts + p, 1), :], 0)
        total = jnp.sum(kept.astype(F32), axis=1, keepdims=True).astype(jnp.int32)
        R.used_v[p:p + 1, :] = jnp.broadcast_to(total, (1, 128))

    k_iota = lax.broadcasted_iota(jnp.int32, (KEYS, SLOTS), 0)
    q_iota = lax.broadcasted_iota(jnp.int32, (KEYS, SLOTS), 1)

    def out_copies(b, k):
        stage, out = ((R.stS, st_hbm), (R.grS, gr_hbm))[k]
        here = pl.ds(pl.multiple_of(b * CH, CH), CH)
        there = pl.ds(pl.multiple_of(section * rows, CH) + pl.multiple_of(b * CH, CH), CH)
        own = pltpu.make_async_copy(stage.at[section, here, :], out.at[there, :], R.local_sem.at[b, k])
        sent = pltpu.make_async_remote_copy(
            src_ref=stage.at[1 - section, here, :], dst_ref=out.at[there, :],
            send_sem=R.ex_send.at[b, k], recv_sem=R.ex_recv.at[b, k],
            device_id=(1 - section, dp), device_id_type=MESH)
        return own, sent

    def add_wd(i, t):
        n = min(256, FF - i)
        acc[i:i + n, :] += t[0:n]
        if t.shape[0] > n:
            ones_acc[0] += t[n:]

    def add_wu(j, t):
        acc[FF + j * D:FF + j * D + D, :] += t[0:D]
        ones_acc[1 + j] += t[D:]

    def add_wqkv(j, t):
        acc[2 * FF + j * D:2 * FF + j * D + D, :] += t[0:D]
        ones_acc[5 + j] += t[D:]

    def add_wo(t):
        acc[2 * FF + 3 * D:2 * FF + 4 * D, :] += t[0:D]
        ones_acc[8] += t[D:]
    R.add_wd, R.add_wu, R.add_wqkv, R.add_wo = add_wd, add_wu, add_wqkv, add_wo

    pl.semaphore_wait(barrier, len(orders[0]))

    def group(g, carry):
        def at(b):
            return pl.ds(pl.multiple_of(g * GROUP + b, 128), 128)

        def load(c):
            b = g * (GROUP // CH) + c
            for k in range(3):
                fetch(b, k).wait()
            tok = slice(c * CH, c * CH + CH)
            src = pl.ds(pl.multiple_of(b * CH, CH), CH)
            e = R.ev[src, :].T
            R.eT[:, tok] = e
            R.uT[:, tok] = R.xv[src, :].T.astype(F32) + e.astype(F32)
            grad = R.gv[src, :].T
            R.gT[:, tok] = grad.astype(F32)
            R.lowT[1, :, tok] = grad
        R.load = load

        def finish_forward(it, b, out):
            R.stS[it, at(b), :] = out.T
            if it == 0:
                R.uT[:, b:b + 128] = out.astype(F32) + R.eT[:, b:b + 128].astype(F32)
        R.finish_forward = finish_forward

        def finish_backward(it, b, low):
            R.grS[it, at(b), :] = low.T
            if it == 1:
                R.gT[:, b:b + 128] = low.astype(F32)
                R.lowT[0, :, b:b + 128] = low
        R.finish_backward = finish_backward

        def send(c, k):
            for copy in out_copies(g * (GROUP // CH) + c, k):
                copy.start()
        R.send = send

        masks = []
        for p in range(PG):
            used = R.used_v[pl.ds(g * PG + p, 1), :]
            masks.append(jnp.where((k_iota <= q_iota) & (k_iota < used), 0.0, -1e30).astype(F32))
        run_group(R, masks, LAG)
        return carry

    lax.fori_loop(0, rows // GROUP, group, 0)

    for i, j in enumerate((0, 1, 5, 6)):
        vec_ref[j:j + 1, :] = jnp.sum(aln[i].T, axis=0, keepdims=True)
    for i, j in ((0, 7), (1, 8), (2, 9), (3, 10), (4, 11), (5, 2), (7, 3), (8, 4)):
        vec_ref[j:j + 1, :] = ones_acc[i, 0:1, :]
    vec_ref[12:16, :] = jnp.zeros((4, D), F32)

    total_rows = acc.shape[0]
    part_rows = total_rows // PARTS
    offs = [p * part_rows for p in range(PARTS)]
    sizes = [part_rows] * PARTS
    pending = [None] * PARTS
    history = [[] for _ in range(PARTS)]
    used_rows = 0
    vec_pending = None

    def finish_vec():
        nonlocal vec_pending
        if vec_pending is not None:
            copy, s = vec_pending
            copy.wait()
            vec_ref[...] = vec_ref[...] + vec_recv[s]
            vec_pending = None

    for s in range(len(orders[0])):
        for p in range(PARTS):
            if pending[p] is not None:
                pending[p]()
            axis, weight = orders[p][s]
            v = bit_of(axis, weight)
            off, size = offs[p], sizes[p]
            halve = size >= 32
            n = size // 2 if halve else size
            src_off = pl.multiple_of(off + (1 - v) * n, 16) if halve else off
            keep = pl.multiple_of(off + v * n, 16) if halve else off
            region = pl.ds(used_rows, n)
            used_rows += n
            send_buf[region, :] = acc[pl.ds(src_off, n), :].astype(BF)
            copy = pltpu.make_async_remote_copy(
                src_ref=send_buf.at[region, :], dst_ref=recv_buf.at[region, :],
                send_sem=rs_send.at[s, p], recv_sem=rs_recv.at[s, p],
                device_id=across(axis, weight), device_id_type=MESH)
            copy.start()

            def finish(copy=copy, keep=keep, n=n, region=region, halve=halve):
                copy.wait()
                own = acc[pl.ds(keep, n), :]
                if not halve:
                    own = own.astype(BF).astype(F32)
                acc[pl.ds(keep, n), :] = own + recv_buf[region, :].astype(F32)
            pending[p] = finish
            if halve:
                history[p].append((axis, weight, off, n, keep))
                offs[p], sizes[p] = keep, n
        finish_vec()
        axis, weight = orders[0][s]
        vec_send[s] = vec_ref[...]
        copy = pltpu.make_async_remote_copy(
            src_ref=vec_send.at[s], dst_ref=vec_recv.at[s],
            send_sem=vs_send.at[s], recv_sem=vs_recv.at[s],
            device_id=across(axis, weight), device_id_type=MESH)
        copy.start()
        vec_pending = (copy, s)
    finish_vec()
    for p in range(PARTS):
        pending[p]()
        sums_ref[pl.ds(offs[p], sizes[p]), :] = acc[pl.ds(offs[p], sizes[p]), :].astype(BF)
    last = [None] * PARTS
    for s in range(max(len(h) for h in history)):
        for p in range(PARTS):
            if last[p] is not None:
                last[p].wait()
            axis, weight, off, n, keep = history[p][-1 - s]
            copy = pltpu.make_async_remote_copy(
                src_ref=sums_ref.at[pl.ds(keep, n), :], dst_ref=sums_ref.at[pl.ds(keep, n), :],
                send_sem=ag_send.at[s, p], recv_sem=ag_recv.at[s, p],
                device_id=across(axis, weight), device_id_type=MESH)
            copy.start()
            last[p] = copy
    for p in range(PARTS):
        last[p].wait()

    def finish_out(b, c):
        for k in range(2):
            own, sent = out_copies(b, k)
            own.wait()
            sent.wait()
        return c
    lax.fori_loop(0, blocks, finish_out, 0)


def compute(x, e, g, counts, lengths, params, dp_size):
    local = x.shape[0]
    rows = local // 2
    dp_bits = dp_size.bit_length() - 1
    stages = dp_bits + 1
    hbm = pl.BlockSpec(memory_space=pl.ANY)
    smem = pl.BlockSpec(memory_space=pltpu.SMEM)
    vmem = pl.BlockSpec(memory_space=pltpu.VMEM)
    outs = [
        jax.ShapeDtypeStruct((local, 256), BF),
        jax.ShapeDtypeStruct((local, 256), BF),
        jax.ShapeDtypeStruct((3072, 256), BF),
        jax.ShapeDtypeStruct((16, 256), F32),
    ]
    buf_rows = 0
    size = 3072 // PARTS
    for _ in range(stages):
        n = size // 2 if size >= 32 else size
        buf_rows += n * PARTS
        size = n
    return pl.pallas_call(
        functools.partial(kernel, dp_bits),
        out_shape=outs,
        in_specs=[hbm, hbm, hbm, smem, vmem] + [vmem] * 15,
        out_specs=[hbm, hbm, vmem, vmem],
        scratch_shapes=[pltpu.VMEM(s, t) for s, t in SCRATCH.values()] + list(comm_scratch(rows, buf_rows, stages).values()),
        compiler_params=pltpu.CompilerParams(
            vmem_limit_bytes=62 * 1024 * 1024, collective_id=0, has_side_effects=True),
    )(x, e, g, counts, lengths, *params)


def widen_kernel(st_ref, gr_ref, sums_ref, vec_ref, st_out, gr_out, n1g, n1b, wq, qb, wk, wv, vb, wo, ob, n2g, n2b, wu, ub, wd, db):
    st_out[0] = st_ref[...]
    gr_out[0] = gr_ref[...].astype(F32)

    @pl.when(pl.program_id(0) == 0)
    def _():
        wd[...] = sums_ref[0:1024, :].astype(F32)
        for j in range(4):
            wu[:, 256 * j:256 * j + 256] = sums_ref[1024 + 256 * j:1280 + 256 * j, :].astype(F32)
            ub[256 * j:256 * j + 256] = vec_ref[8 + j]
        for j, r in enumerate((wq, wk, wv, wo)):
            r[...] = sums_ref[2048 + 256 * j:2304 + 256 * j, :].astype(F32)
        for j, r in enumerate((n1g, n1b, qb, vb, ob, n2g, n2b, db)):
            r[...] = vec_ref[j]


def widen(st, gr, sums, vec, params):
    local = st.shape[0]
    block = min(512, local)
    full = lambda a: pl.BlockSpec(a.shape, lambda i: (0,) * a.ndim)
    outs = [jax.ShapeDtypeStruct((1, local, 256), BF), jax.ShapeDtypeStruct((1, local, 256), F32)]
    outs += [jax.ShapeDtypeStruct(p.shape, F32) for p in params]
    blk = pl.BlockSpec((block, 256), lambda i: (i, 0))
    oblk = pl.BlockSpec((1, block, 256), lambda i: (0, i, 0))
    return pl.pallas_call(
        widen_kernel,
        grid=(local // block,),
        out_shape=outs,
        in_specs=[blk, blk, full(sums), full(vec)],
        out_specs=[oblk, oblk] + [full(o) for o in outs[2:]],
        compiler_params=pltpu.CompilerParams(vmem_limit_bytes=60 * 1024 * 1024),
    )(st, gr, sums, vec)


def solution(mesh):
    dp_size = mesh.shape["dp"]

    def body(x, e, g, counts, lengths, *params):
        st, gr, sums, vec = compute(x, e, g, counts, lengths, params, dp_size)
        return tuple(widen(st, gr, sums, vec, params))

    placed = (P("dp", None),) * 3 + (P("dp"), P("dp", None)) + (P(),) * 15
    return jax.shard_map(
        body,
        mesh=mesh,
        in_specs=placed,
        out_specs=(P("section", "dp", None),) * 2 + (P(),) * 15,
        check_vma=False,
    )
```

```python
import functools
import math

import jax
import jax.numpy as jnp
from jax import lax
from jax.experimental import pallas as pl
from jax.experimental.pallas import tpu as pltpu
from jax.sharding import PartitionSpec as P

BF = jnp.bfloat16
F32 = jnp.float32
SLOTS = 128
HEADS = 8
KEYS = 112
GROUP = 512
CH = 256
PG = GROUP // SLOTS
EPS = 1e-5


def nn(a, b):
    return lax.dot_general(a, b, (((1,), (0,)), ((), ())), preferred_element_type=F32)


def nt(a, b):
    return lax.dot_general(a, b, (((1,), (1,)), ((), ())), preferred_element_type=F32)


C0 = math.sqrt(2.0 / math.pi)
C1 = C0 * 0.044715
SCALE = 32 ** -0.5
D = 256
FF = 1024


def ln_forward(u_ref, gain, bias, unit_ref, inv_ref, n_ref, lanes):
    for b in range(lanes.start, lanes.stop, 128):
        ln = slice(b, b + 128)
        u = u_ref[:, ln]
        mean = jnp.sum(u, axis=0, keepdims=True) * (1.0 / D)
        c = u - mean
        var = jnp.sum(c * c, axis=0, keepdims=True) * (1.0 / D)
        inv = lax.rsqrt(var + EPS)
        unit = c * inv
        unit_ref[:, ln] = unit
        inv_ref[:, ln] = inv
        n_ref[0:D, ln] = (unit * gain[...] + bias[...]).astype(BF)


def ln_backward(gn_ref, res_ref, unit_ref, inv_ref, gain, gain_acc, bias_acc, out_ref, low_ref, lanes):
    for b in range(lanes.start, lanes.stop, 128):
        ln = slice(b, b + 128)
        gn = gn_ref[:, ln]
        unit = unit_ref[:, ln]
        t = gn * unit
        gain_acc[...] += t
        bias_acc[...] += gn
        s = gn * gain[...]
        m1 = jnp.sum(s, axis=0, keepdims=True) * (1.0 / D)
        m2 = jnp.sum(t * gain[...], axis=0, keepdims=True) * (1.0 / D)
        out = res_ref[:, ln] + inv_ref[:, ln] * (s - m1 - unit * m2)
        out_ref[:, ln] = out
        low_ref[:, ln] = out.astype(BF)


class Refs:
    pass


def chain(R, c, masks):
    L = slice(c * CH, c * CH + CH)
    prompts = range(c * CH // SLOTS, (c + 1) * CH // SLOTS)
    R.load(c)
    yield
    for it in range(2):
        ln_forward(R.uT, R.vecs.at[0], R.vecs.at[1], R.unit1.at[it], R.inv1.at[it], R.n1T.at[it], L)
        yield
        n1 = R.n1T[it, 0:D, L]
        for j, vec in ((0, 2), (1, None), (2, 3)):
            rows = slice(256 * j, 256 * j + 256)
            y = nn(R.wqkvT[rows, :], n1)
            if vec is not None:
                v = R.vecs[vec]
                y = y + jnp.concatenate([v] * (CH // 128), axis=1)
            R.qkvT[it, rows, L] = y.astype(BF)
        yield
        for p in prompts:
            tok = slice(p * 128, p * 128 + 128)
            for h in range(HEADS):
                R.bdq[p, h // 2, 32 * (h % 4):32 * (h % 4) + 32, 128 * (h % 2):128 * (h % 2) + 128] = R.qkvT[it, 32 * h:32 * h + 32, tok]
            R.kN[p] = R.qkvT[it, 256:512, tok].T
            for h2 in range(HEADS // 2):
                R.sc[p, :, 256 * h2:256 * h2 + 256] = nn(R.kN[p, 0:KEYS, 128 * (h2 // 2):128 * (h2 // 2) + 128], R.bdq[p, h2])
            R.vN[it, p] = R.qkvT[it, 512:768, tok].T
            yield
        for p in prompts:
            tok = slice(p * 128, p * 128 + 128)
            for h in range(HEADS):
                ln = slice(128 * h, 128 * h + 128)
                s = R.sc[p, :, ln] + masks[p]
                m = jnp.max(s, axis=0, keepdims=True)
                pe = jnp.exp2((s - m) * (SCALE * math.log2(math.e)))
                l = jnp.sum(pe, axis=0, keepdims=True)
                pT = pe * (1.0 / l)
                R.p32[it, p, :, ln] = pT
                R.p16[it, p, 0:KEYS, ln] = pT.astype(BF)
            yield
            for h2 in range(HEADS // 2):
                ln = slice(256 * h2, 256 * h2 + 256)
                o = nn(R.qkvT[it, 512 + 64 * h2:576 + 64 * h2, tok], R.p16[it, p, :, ln])
                R.mixT[it, 64 * h2:64 * h2 + 32, tok] = o[0:32, 0:128].astype(BF)
                R.mixT[it, 64 * h2 + 32:64 * h2 + 64, tok] = o[32:64, 128:256].astype(BF)
            yield
        y = nn(R.woT[...], R.mixT[it, 0:D, L])
        for b in range(L.start, L.stop, 128):
            R.mid[:, b:b + 128] = R.uT[:, b:b + 128] + R.vecs[4] + y[:, b - L.start:b - L.start + 128]
        yield
        for p in prompts:
            for h in range(HEADS):
                ln = slice(128 * h, 128 * h + 128)
                R.pN[it, p, :, ln] = R.p16[it, p, :, ln].T
        ln_forward(R.mid, R.vecs.at[5], R.vecs.at[6], R.unit2.at[it], R.inv2.at[it], R.n2T.at[it], L)
        yield
        n2 = R.n2T[it, 0:D, L]
        for half in range(2):
            rows = slice(512 * half, 512 * half + 512)
            R.pre[rows, L] = nn(R.wuT[rows, :], n2)
            yield
            for r in range(rows.start, rows.stop, 32):
                for b in range(L.start, L.stop, 128):
                    at = (slice(r, r + 32), slice(b, b + 128))
                    v = R.pre[at] + R.ubv[r:r + 32, :]
                    v2 = v * v
                    t = jnp.tanh(v * (C0 + C1 * v2))
                    h1 = 0.5 + 0.5 * t
                    hid = v * h1
                    R.gp[it, r:r + 32, b:b + 128] = h1 + (hid - hid * h1) * (2.0 * C0 + 6.0 * C1 * v2)
                    R.hT[it, r:r + 32, b:b + 128] = hid.astype(BF)
            yield
        y = nn(R.wdT[...], R.hT[it, 0:FF, L])
        for b in range(L.start, L.stop, 128):
            out = R.mid[:, b:b + 128] + R.vecs[7] + y[:, b - L.start:b - L.start + 128]
            R.finish_forward(it, b, out.astype(BF))
        if it == 1:
            R.send(c, 0)
        yield
    for it in (1, 0):
        for half in range(2):
            rows = slice(512 * half, 512 * half + 512)
            R.pre[rows, L] = nn(R.wd_ref[rows, :], R.lowT[it, :, L])
            yield
            for r in range(rows.start, rows.stop, 32):
                for b in range(L.start, L.stop, 128):
                    at = (slice(r, r + 32), slice(b, b + 128))
                    R.dpre[it, r:r + 32, b:b + 128] = (R.pre[at] * R.gp[it, r:r + 32, b:b + 128]).astype(BF)
            yield
        R.dn[:, L] = nn(R.wu_ref[...], R.dpre[it, :, L])
        yield
        ln_backward(R.dn, R.gT, R.unit2.at[it], R.inv2.at[it], R.vecs.at[5], R.aln.at[2], R.aln.at[3], R.gT, R.alow.at[it], L)
        yield
        R.dmixT[:, L] = nn(R.wo_ref[...], R.alow[it, :, L]).astype(BF)
        yield
        for p in prompts:
            tok = slice(p * 128, p * 128 + 128)
            for h in range(HEADS):
                R.bdo[p, h // 2, 32 * (h % 4):32 * (h % 4) + 32, 128 * (h % 2):128 * (h % 2) + 128] = R.dmixT[32 * h:32 * h + 32, tok]
            for h2 in range(HEADS // 2):
                R.sc[p, :, 256 * h2:256 * h2 + 256] = nn(R.vN[it, p, 0:KEYS, 128 * (h2 // 2):128 * (h2 // 2) + 128], R.bdo[p, h2])
            yield
        for p in prompts:
            tok = slice(p * 128, p * 128 + 128)
            for h in range(HEADS):
                ln = slice(128 * h, 128 * h + 128)
                pT = R.p32[it, p, :, ln]
                t = pT * R.sc[p, :, ln]
                dsum = jnp.sum(t, axis=0, keepdims=True)
                R.ds16[p, 0:KEYS, ln] = (t - pT * dsum).astype(BF)
                R.dsN[p, :, ln] = R.ds16[p, :, ln].T
            yield
            for h2 in range(HEADS // 2):
                r = 64 * h2
                ln = slice(256 * h2, 256 * h2 + 256)
                for base, left, right, scaled in (
                    (512, R.dmixT[r:r + 64, tok], R.pN[it, p, :, ln], None),
                    (0, R.qkvT[it, 256 + r:320 + r, tok], R.ds16[p, :, ln], SCALE),
                    (256, R.qkvT[it, r:r + 64, tok], R.dsN[p, :, ln], SCALE)):
                    d = nn(left, right)
                    top, low = d[0:32, 0:128], d[32:64, 128:256]
                    if scaled is not None:
                        top, low = top * scaled, low * scaled
                    R.dqkvT[it, base + r:base + r + 32, tok] = top.astype(BF)
                    R.dqkvT[it, base + r + 32:base + r + 64, tok] = low.astype(BF)
            yield
        R.dn[:, L] = nn(R.wqkv[...], R.dqkvT[it, :, L])
        yield
        ln_backward(R.dn, R.gT, R.unit1.at[it], R.inv1.at[it], R.vecs.at[0], R.aln.at[0], R.aln.at[1], R.gT, R.gl16, L)
        for b in range(L.start, L.stop, 128):
            R.finish_backward(it, b, R.gl16[:, b:b + 128])
        if it == 0:
            R.send(c, 1)
        yield


def weight_terms(R, it):
    for i in range(0, FF, 256):
        stop = i + 256 if i + 256 < FF else FF + 16
        R.add_wd(i, nt(R.hT[it, i:stop, :], R.lowT[it]))
        yield
    for j in range(FF // D):
        R.add_wu(j, nt(R.n2T[it], R.dpre[it, j * D:j * D + D, :]))
        yield
    R.add_wo(nt(R.mixT[it], R.alow[it]))
    yield
    for j in range(3):
        R.add_wqkv(j, nt(R.n1T[it], R.dqkvT[it, j * D:j * D + D, :]))
        yield


def run_group(R, masks, lag):
    chains = [chain(R, c, masks) for c in range(GROUP // CH)]
    counts = [0] * len(chains)
    done = [False] * len(chains)
    terms = []
    started = set()
    while not all(done) or terms:
        for i, ch in enumerate(chains):
            if done[i] or (i > 0 and counts[i] + lag > counts[i - 1] and not done[i - 1]):
                continue
            try:
                next(ch)
                counts[i] += 1
            except StopIteration:
                done[i] = True
        if min(counts) >= R.bwd1_done and 1 not in started:
            started.add(1)
            terms.append(weight_terms(R, 1))
        if all(done) and 0 not in started:
            started.add(0)
            terms.append(weight_terms(R, 0))
        for t in list(terms):
            try:
                next(t)
            except StopIteration:
                terms.remove(t)


SCRATCH = dict(
    wqkvT=((768, 256), BF), woT=((256, 256), BF), wuT=((1024, 256), BF), wdT=((256, 1024), BF), wqkv=((256, 768), BF),
    vecs=((8, 256, 128), F32), ubv=((1024, 128), F32),
    n1T=((2, 272, GROUP), BF), qkvT=((2, 768, GROUP), BF), kN=((PG, 128, 256), BF), vN=((2, PG, 128, 256), BF),
    bdq=((PG, 4, 128, 256), BF), bdo=((PG, 4, 128, 256), BF),
    sc=((PG, KEYS, 1024), F32), p32=((2, PG, KEYS, 1024), F32), p16=((2, PG, 128, 1024), BF), pN=((2, PG, 128, 1024), BF),
    ds16=((PG, 128, 1024), BF), dsN=((PG, 128, 1024), BF),
    mixT=((2, 272, GROUP), BF), uT=((256, GROUP), F32), eT=((256, GROUP), BF), mid=((256, GROUP), F32), gT=((256, GROUP), F32), dn=((256, GROUP), F32),
    gl16=((256, GROUP), BF),
    unit1=((2, 256, GROUP), F32), inv1=((2, 1, GROUP), F32), unit2=((2, 256, GROUP), F32), inv2=((2, 1, GROUP), F32),
    n2T=((2, 272, GROUP), BF), pre=((1024, GROUP), F32), gp=((2, 1024, GROUP), F32), hT=((2, 1040, GROUP), BF),
    lowT=((2, 256, GROUP), BF), dpre=((2, 1024, GROUP), BF), alow=((2, 256, GROUP), BF), dmixT=((256, GROUP), BF),
    dqkvT=((2, 768, GROUP), BF), aln=((4, 256, 128), F32))


def prologue(R, n1g, n1b, wq, qb, wk, wv, vb, wo, ob, n2g, n2b, wu, ub, wd, db):
    R.wqkvT[0:256, :] = wq[...].T
    R.wqkvT[256:512, :] = wk[...].T
    R.wqkvT[512:768, :] = wv[...].T
    R.woT[...] = wo[...].T
    R.wuT[...] = wu[...].T
    R.wdT[...] = wd[...].T
    R.wqkv[:, 0:256] = wq[...]
    R.wqkv[:, 256:512] = wk[...]
    R.wqkv[:, 512:768] = wv[...]
    for i, r in enumerate((n1g, n1b, qb, vb, ob, n2g, n2b, db)):
        R.vecs[i] = jnp.broadcast_to(r[...].astype(F32).reshape(1, D), (128, D)).T
    R.ubv[...] = jnp.broadcast_to(ub[...].astype(F32).reshape(1, FF), (128, FF)).T
    for r in (R.aln, R.bdq, R.bdo, R.ds16, R.p16):
        r[...] = jnp.zeros_like(r)
    for it in range(2):
        for r in (R.n1T, R.mixT, R.n2T):
            r[it, D:, :] = jnp.ones((16, GROUP), BF)
        R.hT[it, FF:, :] = jnp.ones((16, GROUP), BF)


LAG = 3
MESH = pl.DeviceIdType.MESH
CUBE = (("dp", 2), ("section", 1), ("dp", 4))
PEERS = 7


class Place:
    def __init__(self, dp_bits):
        self.section = lax.axis_index("section")
        self.dp = lax.axis_index("dp")
        self.core = lax.rem(self.dp, 2)
        self.rest = [1 << b for b in range(3, dp_bits)]
        self.bits = [self.bit(axis, weight) for axis, weight in CUBE]
        self.cube = self.bits[0] + 2 * self.bits[1] + 4 * self.bits[2]

    def bit(self, axis, weight):
        return self.section if axis == "section" else lax.rem(lax.div(self.dp, weight), 2)

    def across(self, axis, weight):
        if axis == "section":
            return (1 - self.section, self.dp)
        return (self.section, self.dp + (1 - 2 * self.bit(axis, weight)) * weight)

    def peer(self, mask):
        section, dp, number = self.section, self.dp, 0
        for i, (axis, weight) in enumerate(CUBE):
            v = self.bits[i]
            if mask >> i & 1:
                if axis == "section":
                    section = 1 - section
                else:
                    dp = dp + (1 - 2 * v) * weight
                v = 1 - v
            number = number + v * (1 << i)
        return (section, dp), number

    def everyone(self):
        found = [self.across("dp", 1)] + [self.peer(m)[0] for m in range(1, PEERS + 1)]
        return found + [self.across("dp", w) for w in self.rest]


class Sums:
    def __init__(self, R, place, e, base, rows):
        self.R, self.place, self.e, self.base = R, place, e, base
        self.half, self.n = rows // 2, rows // 16
        self.sent = []
        self.buf = base // 2
        self.cbuf = base // 16
        self.keep = pl.multiple_of(base + place.core * self.half, 16)
        self.own = pl.multiple_of(self.keep + place.cube * self.n, 16)

    def copy(self, src, dst, slot, device):
        R = self.R
        c = pltpu.make_async_remote_copy(src_ref=src, dst_ref=dst, send_sem=R.sum_send.at[self.e, slot],
                                         recv_sem=R.sum_recv.at[self.e, slot], device_id=device, device_id_type=MESH)
        c.start()
        self.sent.append(c)
        return c

    def steps(self):
        R, place, half, n = self.R, self.place, self.half, self.n
        region = pl.ds(self.buf, half)
        away = pl.multiple_of(self.base + (1 - place.core) * half, 16)
        R.core_send[region, :] = R.acc[pl.ds(away, half), :].astype(BF)
        c = self.copy(R.core_send.at[region, :], R.core_recv.at[region, :], 0, place.across("dp", 1))
        yield
        c.wait_recv()
        small = pl.ds(self.cbuf, n)
        waits = []
        for m in range(1, PEERS + 1):
            device, number = place.peer(m)
            at = pl.multiple_of(number * n, 16)
            R.cube_send[m - 1, small, :] = (R.acc[pl.ds(pl.multiple_of(self.keep + at, 16), n), :]
                                            + R.core_recv[pl.ds(pl.multiple_of(self.buf + at, 16), n), :].astype(F32)).astype(BF)
            waits.append(self.copy(R.cube_send.at[m - 1, small, :], R.cube_recv.at[m - 1, small, :], m, device))
        total = R.acc[pl.ds(self.own, n), :] + R.core_recv[pl.ds(pl.multiple_of(self.buf + place.cube * n, 16), n), :].astype(F32)
        R.acc[pl.ds(self.own, n), :] = total
        yield
        for c in waits:
            c.wait_recv()
        total = R.acc[pl.ds(self.own, n), :]
        for m in range(PEERS):
            total = total + R.cube_recv[m, small, :].astype(F32)
        for i, weight in enumerate(place.rest):
            R.rest_send[i, small, :] = total.astype(BF)
            c = self.copy(R.rest_send.at[i, small, :], R.rest_recv.at[i, small, :], 2 * PEERS + 2 + i, place.across("dp", weight))
            yield
            c.wait_recv()
            total = R.rest_send[i, small, :].astype(F32) + R.rest_recv[i, small, :].astype(F32)
        own = pl.ds(self.own, n)
        R.sums[own, :] = total.astype(BF)
        waits = []
        for m in range(1, PEERS + 1):
            waits.append(self.copy(R.sums.at[own, :], R.sums.at[own, :], PEERS + m, place.peer(m)[0]))
        yield
        for c in waits:
            c.wait_recv()
        keep = pl.ds(self.keep, half)
        c = self.copy(R.sums.at[keep, :], R.sums.at[keep, :], 2 * PEERS + 1, place.across("dp", 1))
        yield
        c.wait_recv()

    def finish(self):
        for c in self.sent:
            c.wait_send()


class VectorSums(Sums):
    def __init__(self, R, place, e):
        self.R, self.place, self.e = R, place, e
        self.sent = []

    def steps(self):
        R, place = self.R, self.place
        R.vec_send[0] = R.vec[...]
        c = self.copy(R.vec_send.at[0], R.vec_recv.at[0], 0, place.across("dp", 1))
        yield
        c.wait_recv()
        R.vec_cube[place.cube] = R.vec_send[0] + R.vec_recv[0]
        waits = []
        for m in range(1, PEERS + 1):
            waits.append(self.copy(R.vec_cube.at[place.cube], R.vec_cube.at[place.cube], m, place.peer(m)[0]))
        yield
        for c in waits:
            c.wait_recv()
        total = R.vec_cube[0]
        for i in range(1, PEERS + 1):
            total = total + R.vec_cube[i]
        for i, weight in enumerate(place.rest):
            R.vec_send[1 + i] = total
            c = self.copy(R.vec_send.at[1 + i], R.vec_recv.at[1 + i], 2 * PEERS + 2 + i, place.across("dp", weight))
            yield
            c.wait_recv()
            total = R.vec_send[1 + i] + R.vec_recv[1 + i]
        R.vec[...] = total


FF_ROWS = 2 * FF + D
QKV_ROWS = 3 * D


def comm_scratch(rows, rest):
    blocks = rows // CH
    dma = pltpu.SemaphoreType.DMA
    total = FF_ROWS + QKV_ROWS
    slots = 2 * PEERS + 2 + rest
    return dict(
        xv=pltpu.VMEM((rows, 256), BF), ev=pltpu.VMEM((rows, 256), BF), gv=pltpu.VMEM((rows, 256), BF),
        stS=pltpu.VMEM((2, rows, 256), BF), grS=pltpu.VMEM((2, rows, 256), BF),
        used_v=pltpu.VMEM((rows // SLOTS, 128), jnp.int32),
        acc=pltpu.VMEM((total, 256), F32), ones_acc=pltpu.VMEM((9, 16, 256), F32),
        core_send=pltpu.VMEM((total // 2, 256), BF), core_recv=pltpu.VMEM((total // 2, 256), BF),
        cube_send=pltpu.VMEM((PEERS, total // 16, 256), BF), cube_recv=pltpu.VMEM((PEERS, total // 16, 256), BF),
        rest_send=pltpu.VMEM((rest, total // 16, 256), BF), rest_recv=pltpu.VMEM((rest, total // 16, 256), BF),
        vec_send=pltpu.VMEM((1 + rest, 16, 256), F32), vec_recv=pltpu.VMEM((1 + rest, 16, 256), F32),
        vec_cube=pltpu.VMEM((PEERS + 1, 16, 256), F32),
        in_sem=dma((blocks, 3)), local_sem=dma((blocks, 2)), ex_send=dma((blocks, 2)), ex_recv=dma((blocks, 2)),
        sum_send=dma((3, slots)), sum_recv=dma((3, slots)))


def kernel(dp_bits, x_hbm, e_hbm, g_hbm, counts_ref, lengths_ref, *refs):
    ws = refs[:15]
    st_hbm, gr_hbm, sums_ref, vec_ref = refs[15:19]
    R = Refs()
    for name, r in zip(list(SCRATCH) + list(comm_scratch(CH, 1)), refs[19:]):
        setattr(R, name, r)
    R.wo_ref, R.wu_ref, R.wd_ref = ws[7], ws[11], ws[13]
    R.sums, R.vec = sums_ref, vec_ref
    R.bwd1_done = 44
    aln, acc, ones_acc = R.aln, R.acc, R.ones_acc
    rows = R.xv.shape[0]
    blocks = rows // CH
    place = Place(dp_bits)
    section, dp = place.section, place.dp

    barrier = pltpu.get_barrier_semaphore()
    everyone = place.everyone()
    for device in everyone:
        pl.semaphore_signal(barrier, inc=1, device_id=device, device_id_type=MESH)

    def fetch(b, k):
        src = (x_hbm, e_hbm, g_hbm)[k]
        dst = (R.xv, R.ev, R.gv)[k]
        start = pl.multiple_of(b * CH, CH)
        return pltpu.make_async_copy(
            src.at[pl.ds(pl.multiple_of(section * rows, CH) + start, CH), :],
            dst.at[pl.ds(start, CH), :], R.in_sem.at[b, k])

    def start_fetches(b, c):
        for k in range(3):
            fetch(b, k).start()
        return c
    lax.fori_loop(0, blocks, start_fetches, 0)

    prologue(R, *ws)
    acc[...] = jnp.zeros_like(acc)
    ones_acc[...] = jnp.zeros_like(ones_acc)
    prompts = rows // SLOTS
    at_most = lengths_ref.shape[1]
    j_iota = lax.broadcasted_iota(jnp.int32, (1, at_most), 1)
    for p in range(prompts):
        count = counts_ref[section * prompts + p]
        kept = jnp.where(j_iota < count, lengths_ref[pl.ds(section * prompts + p, 1), :], 0)
        total = jnp.sum(kept.astype(F32), axis=1, keepdims=True).astype(jnp.int32)
        R.used_v[p:p + 1, :] = jnp.broadcast_to(total, (1, 128))

    k_iota = lax.broadcasted_iota(jnp.int32, (KEYS, SLOTS), 0)
    q_iota = lax.broadcasted_iota(jnp.int32, (KEYS, SLOTS), 1)

    def out_copies(b, k):
        stage, out = ((R.stS, st_hbm), (R.grS, gr_hbm))[k]
        here = pl.ds(pl.multiple_of(b * CH, CH), CH)
        there = pl.ds(pl.multiple_of(section * rows, CH) + pl.multiple_of(b * CH, CH), CH)
        own = pltpu.make_async_copy(stage.at[section, here, :], out.at[there, :], R.local_sem.at[b, k])
        sent = pltpu.make_async_remote_copy(
            src_ref=stage.at[1 - section, here, :], dst_ref=out.at[there, :],
            send_sem=R.ex_send.at[b, k], recv_sem=R.ex_recv.at[b, k],
            device_id=(1 - section, dp), device_id_type=MESH)
        return own, sent

    def add_wd(i, t):
        n = min(256, FF - i)
        acc[i:i + n, :] += t[0:n]
        if t.shape[0] > n:
            ones_acc[0] += t[n:]

    def add_wu(j, t):
        acc[FF + j * D:FF + j * D + D, :] += t[0:D]
        ones_acc[1 + j] += t[D:]

    def add_wqkv(j, t):
        acc[FF_ROWS + j * D:FF_ROWS + j * D + D, :] += t[0:D]
        ones_acc[5 + j] += t[D:]

    def add_wo(t):
        acc[2 * FF:2 * FF + D, :] += t[0:D]
        ones_acc[8] += t[D:]
    R.add_wd, R.add_wu, R.add_wqkv, R.add_wo = add_wd, add_wu, add_wqkv, add_wo

    pl.semaphore_wait(barrier, len(everyone))

    def group(g, carry):
        def at(b):
            return pl.ds(pl.multiple_of(g * GROUP + b, 128), 128)

        def load(c):
            b = g * (GROUP // CH) + c
            for k in range(3):
                fetch(b, k).wait()
            tok = slice(c * CH, c * CH + CH)
            src = pl.ds(pl.multiple_of(b * CH, CH), CH)
            e = R.ev[src, :].T
            R.eT[:, tok] = e
            R.uT[:, tok] = R.xv[src, :].T.astype(F32) + e.astype(F32)
            grad = R.gv[src, :].T
            R.gT[:, tok] = grad.astype(F32)
            R.lowT[1, :, tok] = grad
        R.load = load

        def finish_forward(it, b, out):
            R.stS[it, at(b), :] = out.T
            if it == 0:
                R.uT[:, b:b + 128] = out.astype(F32) + R.eT[:, b:b + 128].astype(F32)
        R.finish_forward = finish_forward

        def finish_backward(it, b, low):
            R.grS[it, at(b), :] = low.T
            if it == 1:
                R.gT[:, b:b + 128] = low.astype(F32)
                R.lowT[0, :, b:b + 128] = low
        R.finish_backward = finish_backward

        def send(c, k):
            for copy in out_copies(g * (GROUP // CH) + c, k):
                copy.start()
        R.send = send

        masks = []
        for p in range(PG):
            used = R.used_v[pl.ds(g * PG + p, 1), :]
            masks.append(jnp.where((k_iota <= q_iota) & (k_iota < used), 0.0, -1e30).astype(F32))
        run_group(R, masks, LAG)
        return carry

    lax.fori_loop(0, rows // GROUP, group, 0)

    for i, j in enumerate((0, 1, 5, 6)):
        vec_ref[j:j + 1, :] = jnp.sum(aln[i].T, axis=0, keepdims=True)
    for i, j in ((0, 7), (1, 8), (2, 9), (3, 10), (4, 11), (5, 2), (7, 3), (8, 4)):
        vec_ref[j:j + 1, :] = ones_acc[i, 0:1, :]
    vec_ref[12:16, :] = jnp.zeros((4, D), F32)

    sums = [Sums(R, place, 0, 0, FF_ROWS), Sums(R, place, 1, FF_ROWS, QKV_ROWS), VectorSums(R, place, 2)]
    running = [x.steps() for x in sums]
    while running:
        for x in list(running):
            try:
                next(x)
            except StopIteration:
                running.remove(x)
    for x in sums:
        x.finish()

    def finish_out(b, c):
        for k in range(2):
            own, sent = out_copies(b, k)
            own.wait()
            sent.wait()
        return c
    lax.fori_loop(0, blocks, finish_out, 0)


def compute(x, e, g, counts, lengths, params, dp_size):
    local = x.shape[0]
    rows = local // 2
    dp_bits = dp_size.bit_length() - 1
    rest = dp_bits - 3
    hbm = pl.BlockSpec(memory_space=pl.ANY)
    smem = pl.BlockSpec(memory_space=pltpu.SMEM)
    vmem = pl.BlockSpec(memory_space=pltpu.VMEM)
    outs = [
        jax.ShapeDtypeStruct((local, 256), BF),
        jax.ShapeDtypeStruct((local, 256), BF),
        jax.ShapeDtypeStruct((3072, 256), BF),
        jax.ShapeDtypeStruct((16, 256), F32),
    ]
    return pl.pallas_call(
        functools.partial(kernel, dp_bits),
        out_shape=outs,
        in_specs=[hbm, hbm, hbm, smem, vmem] + [vmem] * 15,
        out_specs=[hbm, hbm, vmem, vmem],
        scratch_shapes=[pltpu.VMEM(s, t) for s, t in SCRATCH.values()] + list(comm_scratch(rows, rest).values()),
        compiler_params=pltpu.CompilerParams(
            vmem_limit_bytes=62 * 1024 * 1024, collective_id=0, has_side_effects=True),
    )(x, e, g, counts, lengths, *params)


CHUNKS = 8


def widen_kernel(st_ref, gr_ref, sums_ref, vec_ref, st_out, gr_out, n1g, n1b, wq, qb, wk, wv, vb, wo, ob, n2g, n2b, wu, ub, wd, db,
                 st_v, gr_v, gr_w, sums_v, wd_v, wu_v, wa_v, st_in, gr_in, sum_in, st_sem, gr_sem, w_sem):
    block = st_v.shape[0] // CHUNKS
    sums_in = [pltpu.make_async_copy(sums_ref.at[rows, :], sums_v.at[rows, :], sum_in.at[i])
               for i, rows in enumerate((pl.ds(0, FF), pl.ds(FF, FF + D + QKV_ROWS)))]
    parts = [pl.ds(i * block, block) for i in range(CHUNKS)]
    gr_ins = [pltpu.make_async_copy(gr_ref.at[r, :], gr_v.at[r, :], gr_in.at[i]) for i, r in enumerate(parts)]
    st_ins = [pltpu.make_async_copy(st_ref.at[r, :], st_v.at[r, :], st_in.at[i]) for i, r in enumerate(parts)]
    outs = []

    def out(src, dst, sem):
        c = pltpu.make_async_copy(src, dst, sem)
        c.start()
        outs.append(c)

    for c in gr_ins[:2] + sums_in + gr_ins[2:] + st_ins:
        c.start()

    def gradients(i):
        gr_ins[i].wait()
        gr_w[parts[i], :] = gr_v[parts[i], :].astype(F32)
        out(gr_w.at[parts[i], :], gr_out.at[0, parts[i], :], gr_sem.at[i])

    gradients(0)
    gradients(1)
    sums_in[0].wait()
    wd_v[...] = sums_v[0:FF, :].astype(F32)
    out(wd_v, wd, w_sem.at[0])
    sums_in[1].wait()
    for j in range(FF // D):
        wu_v[:, D * j:D * j + D] = sums_v[FF + D * j:FF + D * j + D, :].astype(F32)
    out(wu_v, wu, w_sem.at[1])
    wa_v[...] = sums_v[2 * FF:2 * FF + 4 * D, :].astype(F32)
    for j, r in enumerate((wo, wq, wk, wv)):
        out(wa_v.at[D * j:D * j + D, :], r, w_sem.at[2 + j])
    for i in range(2, CHUNKS):
        gradients(i)
    for j in range(FF // D):
        ub[D * j:D * j + D] = vec_ref[8 + j]
    for j, r in enumerate((n1g, n1b, qb, vb, ob, n2g, n2b, db)):
        r[...] = vec_ref[j]
    for i in range(CHUNKS):
        st_ins[i].wait()
        out(st_v.at[parts[i], :], st_out.at[0, parts[i], :], st_sem.at[i])
    for c in outs:
        c.wait()


def widen(st, gr, sums, vec, params):
    local = st.shape[0]
    outs = [jax.ShapeDtypeStruct((1, local, 256), BF), jax.ShapeDtypeStruct((1, local, 256), F32)]
    outs += [jax.ShapeDtypeStruct(p.shape, F32) for p in params]
    hbm = pl.BlockSpec(memory_space=pl.ANY)
    vmem = pl.BlockSpec(memory_space=pltpu.VMEM)
    dma = pltpu.SemaphoreType.DMA
    return pl.pallas_call(
        widen_kernel,
        out_shape=outs,
        in_specs=[hbm, hbm, hbm, vmem],
        out_specs=[hbm, hbm] + [hbm if len(p.shape) == 2 else vmem for p in params],
        scratch_shapes=[
            pltpu.VMEM((local, 256), BF), pltpu.VMEM((local, 256), BF), pltpu.VMEM((local, 256), F32),
            pltpu.VMEM(sums.shape, BF), pltpu.VMEM((FF, D), F32), pltpu.VMEM((D, FF), F32), pltpu.VMEM((4 * D, D), F32),
            dma((CHUNKS,)), dma((CHUNKS,)), dma((2,)), dma((CHUNKS,)), dma((CHUNKS,)), dma((6,))],
        compiler_params=pltpu.CompilerParams(vmem_limit_bytes=60 * 1024 * 1024),
    )(st, gr, sums, vec)


def solution(mesh):
    dp_size = mesh.shape["dp"]

    def body(x, e, g, counts, lengths, *params):
        st, gr, sums, vec = compute(x, e, g, counts, lengths, params, dp_size)
        return tuple(widen(st, gr, sums, vec, params))

    placed = (P("dp", None),) * 3 + (P("dp"), P("dp", None)) + (P(),) * 15
    return jax.shard_map(
        body,
        mesh=mesh,
        in_specs=placed,
        out_specs=(P("section", "dp", None),) * 2 + (P(),) * 15,
        check_vma=False,
    )
```

```python
import functools
import math

import jax
import jax.numpy as jnp
from jax import lax
from jax.experimental import pallas as pl
from jax.experimental.pallas import tpu as pltpu
from jax.sharding import PartitionSpec as P

BF = jnp.bfloat16
F32 = jnp.float32
SLOTS = 128
HEADS = 8
KEYS = 112
GROUP = 512
CH = 256
PG = GROUP // SLOTS
EPS = 1e-5


def nn(a, b):
    return lax.dot_general(a, b, (((1,), (0,)), ((), ())), preferred_element_type=F32)


def nt(a, b):
    return lax.dot_general(a, b, (((1,), (1,)), ((), ())), preferred_element_type=F32)


C0 = math.sqrt(2.0 / math.pi)
C1 = C0 * 0.044715
SCALE = 32 ** -0.5
D = 256
FF = 1024


def ln_forward(u_ref, gain, bias, unit_ref, inv_ref, n_ref, lanes):
    for b in range(lanes.start, lanes.stop, 128):
        ln = slice(b, b + 128)
        u = u_ref[:, ln]
        mean = jnp.sum(u, axis=0, keepdims=True) * (1.0 / D)
        c = u - mean
        var = jnp.sum(c * c, axis=0, keepdims=True) * (1.0 / D)
        inv = lax.rsqrt(var + EPS)
        unit = c * inv
        unit_ref[:, ln] = unit
        inv_ref[:, ln] = inv
        n_ref[0:D, ln] = (unit * gain[...] + bias[...]).astype(BF)


def ln_backward(gn_ref, res_ref, unit_ref, inv_ref, gain, gain_acc, bias_acc, out_ref, low_ref, lanes):
    for b in range(lanes.start, lanes.stop, 128):
        ln = slice(b, b + 128)
        gn = gn_ref[:, ln]
        unit = unit_ref[:, ln]
        t = gn * unit
        gain_acc[...] += t
        bias_acc[...] += gn
        s = gn * gain[...]
        m1 = jnp.sum(s, axis=0, keepdims=True) * (1.0 / D)
        m2 = jnp.sum(t * gain[...], axis=0, keepdims=True) * (1.0 / D)
        out = res_ref[:, ln] + inv_ref[:, ln] * (s - m1 - unit * m2)
        out_ref[:, ln] = out
        low_ref[:, ln] = out.astype(BF)


class Refs:
    pass


def chain(R, c, masks):
    L = slice(c * CH, c * CH + CH)
    prompts = range(c * CH // SLOTS, (c + 1) * CH // SLOTS)
    R.load(c)
    yield
    for it in range(2):
        ln_forward(R.uT, R.vecs.at[0], R.vecs.at[1], R.unit1.at[it], R.inv1.at[it], R.n1T.at[it], L)
        yield
        n1 = R.n1T[it, 0:D, L]
        for j, vec in ((0, 2), (1, None), (2, 3)):
            rows = slice(256 * j, 256 * j + 256)
            y = nn(R.wqkvT[rows, :], n1)
            if vec is not None:
                v = R.vecs[vec]
                y = y + jnp.concatenate([v] * (CH // 128), axis=1)
            R.qkvT[it, rows, L] = y.astype(BF)
        yield
        for p in prompts:
            tok = slice(p * 128, p * 128 + 128)
            for h in range(HEADS):
                R.bdq[p, h // 2, 32 * (h % 4):32 * (h % 4) + 32, 128 * (h % 2):128 * (h % 2) + 128] = R.qkvT[it, 32 * h:32 * h + 32, tok]
            R.kN[p] = R.qkvT[it, 256:512, tok].T
            for h2 in range(HEADS // 2):
                R.sc[p, :, 256 * h2:256 * h2 + 256] = nn(R.kN[p, 0:KEYS, 128 * (h2 // 2):128 * (h2 // 2) + 128], R.bdq[p, h2])
            R.vN[it, p] = R.qkvT[it, 512:768, tok].T
            yield
        for p in prompts:
            tok = slice(p * 128, p * 128 + 128)
            for h in range(HEADS):
                ln = slice(128 * h, 128 * h + 128)
                s = R.sc[p, :, ln] + masks[p]
                m = jnp.max(s, axis=0, keepdims=True)
                pe = jnp.exp2((s - m) * (SCALE * math.log2(math.e)))
                l = jnp.sum(pe, axis=0, keepdims=True)
                pT = pe * (1.0 / l)
                R.p32[it, p, :, ln] = pT
                R.p16[it, p, 0:KEYS, ln] = pT.astype(BF)
            yield
            for h2 in range(HEADS // 2):
                ln = slice(256 * h2, 256 * h2 + 256)
                o = nn(R.qkvT[it, 512 + 64 * h2:576 + 64 * h2, tok], R.p16[it, p, :, ln])
                R.mixT[it, 64 * h2:64 * h2 + 32, tok] = o[0:32, 0:128].astype(BF)
                R.mixT[it, 64 * h2 + 32:64 * h2 + 64, tok] = o[32:64, 128:256].astype(BF)
            yield
        y = nn(R.woT[...], R.mixT[it, 0:D, L])
        for b in range(L.start, L.stop, 128):
            R.mid[:, b:b + 128] = R.uT[:, b:b + 128] + R.vecs[4] + y[:, b - L.start:b - L.start + 128]
        yield
        for p in prompts:
            for h in range(HEADS):
                ln = slice(128 * h, 128 * h + 128)
                R.pN[it, p, :, ln] = R.p16[it, p, :, ln].T
        ln_forward(R.mid, R.vecs.at[5], R.vecs.at[6], R.unit2.at[it], R.inv2.at[it], R.n2T.at[it], L)
        yield
        n2 = R.n2T[it, 0:D, L]
        for half in range(2):
            rows = slice(512 * half, 512 * half + 512)
            R.pre[rows, L] = nn(R.wuT[rows, :], n2)
            yield
            for r in range(rows.start, rows.stop, 32):
                for b in range(L.start, L.stop, 128):
                    at = (slice(r, r + 32), slice(b, b + 128))
                    v = R.pre[at] + R.ubv[r:r + 32, :]
                    v2 = v * v
                    t = jnp.tanh(v * (C0 + C1 * v2))
                    h1 = 0.5 + 0.5 * t
                    hid = v * h1
                    R.gp[it, r:r + 32, b:b + 128] = h1 + (hid - hid * h1) * (2.0 * C0 + 6.0 * C1 * v2)
                    R.hT[it, r:r + 32, b:b + 128] = hid.astype(BF)
            yield
        y = nn(R.wdT[...], R.hT[it, 0:FF, L])
        for b in range(L.start, L.stop, 128):
            out = R.mid[:, b:b + 128] + R.vecs[7] + y[:, b - L.start:b - L.start + 128]
            R.finish_forward(it, b, out.astype(BF))
        if it == 1:
            R.send(c, 0)
        yield
    for it in (1, 0):
        for half in range(2):
            rows = slice(512 * half, 512 * half + 512)
            R.pre[rows, L] = nn(R.wd_ref[rows, :], R.lowT[it, :, L])
            yield
            for r in range(rows.start, rows.stop, 32):
                for b in range(L.start, L.stop, 128):
                    at = (slice(r, r + 32), slice(b, b + 128))
                    R.dpre[it, r:r + 32, b:b + 128] = (R.pre[at] * R.gp[it, r:r + 32, b:b + 128]).astype(BF)
            yield
        R.dn[:, L] = nn(R.wu_ref[...], R.dpre[it, :, L])
        yield
        ln_backward(R.dn, R.gT, R.unit2.at[it], R.inv2.at[it], R.vecs.at[5], R.aln.at[2], R.aln.at[3], R.gT, R.alow.at[it], L)
        yield
        R.dmixT[:, L] = nn(R.wo_ref[...], R.alow[it, :, L]).astype(BF)
        yield
        for p in prompts:
            tok = slice(p * 128, p * 128 + 128)
            for h in range(HEADS):
                R.bdo[p, h // 2, 32 * (h % 4):32 * (h % 4) + 32, 128 * (h % 2):128 * (h % 2) + 128] = R.dmixT[32 * h:32 * h + 32, tok]
            for h2 in range(HEADS // 2):
                R.sc[p, :, 256 * h2:256 * h2 + 256] = nn(R.vN[it, p, 0:KEYS, 128 * (h2 // 2):128 * (h2 // 2) + 128], R.bdo[p, h2])
            yield
        for p in prompts:
            tok = slice(p * 128, p * 128 + 128)
            for h in range(HEADS):
                ln = slice(128 * h, 128 * h + 128)
                pT = R.p32[it, p, :, ln]
                t = pT * R.sc[p, :, ln]
                dsum = jnp.sum(t, axis=0, keepdims=True)
                R.ds16[p, 0:KEYS, ln] = (t - pT * dsum).astype(BF)
                R.dsN[p, :, ln] = R.ds16[p, :, ln].T
            yield
            for h2 in range(HEADS // 2):
                r = 64 * h2
                ln = slice(256 * h2, 256 * h2 + 256)
                for base, left, right, scaled in (
                    (512, R.dmixT[r:r + 64, tok], R.pN[it, p, :, ln], None),
                    (0, R.qkvT[it, 256 + r:320 + r, tok], R.ds16[p, :, ln], SCALE),
                    (256, R.qkvT[it, r:r + 64, tok], R.dsN[p, :, ln], SCALE)):
                    d = nn(left, right)
                    top, low = d[0:32, 0:128], d[32:64, 128:256]
                    if scaled is not None:
                        top, low = top * scaled, low * scaled
                    R.dqkvT[it, base + r:base + r + 32, tok] = top.astype(BF)
                    R.dqkvT[it, base + r + 32:base + r + 64, tok] = low.astype(BF)
            yield
        R.dn[:, L] = nn(R.wqkv[...], R.dqkvT[it, :, L])
        yield
        ln_backward(R.dn, R.gT, R.unit1.at[it], R.inv1.at[it], R.vecs.at[0], R.aln.at[0], R.aln.at[1], R.gT, R.gl16, L)
        for b in range(L.start, L.stop, 128):
            R.finish_backward(it, b, R.gl16[:, b:b + 128])
        yield


def weight_terms(R, it):
    for i in range(0, FF, 256):
        stop = i + 256 if i + 256 < FF else FF + 16
        R.add_wd(i, nt(R.hT[it, i:stop, :], R.lowT[it]))
        yield
    for j in range(FF // D):
        R.add_wu(j, nt(R.n2T[it], R.dpre[it, j * D:j * D + D, :]))
        yield
    R.add_wo(nt(R.mixT[it], R.alow[it]))
    yield
    for j in range(3):
        R.add_wqkv(j, nt(R.n1T[it], R.dqkvT[it, j * D:j * D + D, :]))
        yield


def run_group(R, masks, lag):
    chains = [chain(R, c, masks) for c in range(GROUP // CH)]
    counts = [0] * len(chains)
    done = [False] * len(chains)
    terms = []
    started = set()
    while not all(done) or terms:
        for i, ch in enumerate(chains):
            if done[i] or (i > 0 and counts[i] + lag > counts[i - 1] and not done[i - 1]):
                continue
            try:
                next(ch)
                counts[i] += 1
            except StopIteration:
                done[i] = True
        if min(counts) >= R.bwd1_done and 1 not in started:
            started.add(1)
            terms.append(weight_terms(R, 1))
        if all(done) and 0 not in started:
            started.add(0)
            terms.append(weight_terms(R, 0))
        for t in list(terms):
            try:
                next(t)
            except StopIteration:
                terms.remove(t)


SCRATCH = dict(
    wqkvT=((768, 256), BF), woT=((256, 256), BF), wuT=((1024, 256), BF), wdT=((256, 1024), BF), wqkv=((256, 768), BF),
    vecs=((8, 256, 128), F32), ubv=((1024, 128), F32),
    n1T=((2, 272, GROUP), BF), qkvT=((2, 768, GROUP), BF), kN=((PG, 128, 256), BF), vN=((2, PG, 128, 256), BF),
    bdq=((PG, 4, 128, 256), BF), bdo=((PG, 4, 128, 256), BF),
    sc=((PG, KEYS, 1024), F32), p32=((2, PG, KEYS, 1024), F32), p16=((2, PG, 128, 1024), BF), pN=((2, PG, 128, 1024), BF),
    ds16=((PG, 128, 1024), BF), dsN=((PG, 128, 1024), BF),
    mixT=((2, 272, GROUP), BF), uT=((256, GROUP), F32), eT=((256, GROUP), BF), mid=((256, GROUP), F32), gT=((256, GROUP), F32), dn=((256, GROUP), F32),
    gl16=((256, GROUP), BF),
    unit1=((2, 256, GROUP), F32), inv1=((2, 1, GROUP), F32), unit2=((2, 256, GROUP), F32), inv2=((2, 1, GROUP), F32),
    n2T=((2, 272, GROUP), BF), pre=((1024, GROUP), F32), gp=((2, 1024, GROUP), F32), hT=((2, 1040, GROUP), BF),
    lowT=((2, 256, GROUP), BF), dpre=((2, 1024, GROUP), BF), alow=((2, 256, GROUP), BF), dmixT=((256, GROUP), BF),
    dqkvT=((2, 768, GROUP), BF), aln=((4, 256, 128), F32))


def prologue(R, n1g, n1b, wq, qb, wk, wv, vb, wo, ob, n2g, n2b, wu, ub, wd, db):
    R.wqkvT[0:256, :] = wq[...].T
    R.wqkvT[256:512, :] = wk[...].T
    R.wqkvT[512:768, :] = wv[...].T
    R.woT[...] = wo[...].T
    R.wuT[...] = wu[...].T
    R.wdT[...] = wd[...].T
    R.wqkv[:, 0:256] = wq[...]
    R.wqkv[:, 256:512] = wk[...]
    R.wqkv[:, 512:768] = wv[...]
    for i, r in enumerate((n1g, n1b, qb, vb, ob, n2g, n2b, db)):
        R.vecs[i] = jnp.broadcast_to(r[...].astype(F32).reshape(1, D), (128, D)).T
    R.ubv[...] = jnp.broadcast_to(ub[...].astype(F32).reshape(1, FF), (128, FF)).T
    for r in (R.aln, R.bdq, R.bdo, R.ds16, R.p16):
        r[...] = jnp.zeros_like(r)
    for it in range(2):
        for r in (R.n1T, R.mixT, R.n2T):
            r[it, D:, :] = jnp.ones((16, GROUP), BF)
        R.hT[it, FF:, :] = jnp.ones((16, GROUP), BF)


LAG = 3
LAST_GRADIENTS = 2
MESH = pl.DeviceIdType.MESH
CUBE = (("dp", 2), ("section", 1), ("dp", 4))
PEERS = 7


class Place:
    def __init__(self, dp_bits):
        self.section = lax.axis_index("section")
        self.dp = lax.axis_index("dp")
        self.core = lax.rem(self.dp, 2)
        self.rest = [1 << b for b in range(3, dp_bits)]
        self.bits = [self.bit(axis, weight) for axis, weight in CUBE]
        self.cube = self.bits[0] + 2 * self.bits[1] + 4 * self.bits[2]

    def bit(self, axis, weight):
        return self.section if axis == "section" else lax.rem(lax.div(self.dp, weight), 2)

    def across(self, axis, weight):
        if axis == "section":
            return (1 - self.section, self.dp)
        return (self.section, self.dp + (1 - 2 * self.bit(axis, weight)) * weight)

    def peer(self, mask):
        section, dp, number = self.section, self.dp, 0
        for i, (axis, weight) in enumerate(CUBE):
            v = self.bits[i]
            if mask >> i & 1:
                if axis == "section":
                    section = 1 - section
                else:
                    dp = dp + (1 - 2 * v) * weight
                v = 1 - v
            number = number + v * (1 << i)
        return (section, dp), number

    def everyone(self):
        found = [self.across("dp", 1)] + [self.peer(m)[0] for m in range(1, PEERS + 1)]
        return found + [self.across("dp", w) for w in self.rest]


class Sums:
    def __init__(self, R, place, e, base, rows):
        self.R, self.place, self.e, self.base = R, place, e, base
        self.half, self.n = rows // 2, rows // 16
        self.sent = []
        self.buf = base // 2
        self.cbuf = base // 16
        self.keep = pl.multiple_of(base + place.core * self.half, 16)
        self.own = pl.multiple_of(self.keep + place.cube * self.n, 16)

    def copy(self, src, dst, slot, device):
        R = self.R
        c = pltpu.make_async_remote_copy(src_ref=src, dst_ref=dst, send_sem=R.sum_send.at[self.e, slot],
                                         recv_sem=R.sum_recv.at[self.e, slot], device_id=device, device_id_type=MESH)
        c.start()
        self.sent.append(c)
        return c

    def steps(self):
        R, place, half, n = self.R, self.place, self.half, self.n
        region = pl.ds(self.buf, half)
        away = pl.multiple_of(self.base + (1 - place.core) * half, 16)
        R.core_send[region, :] = R.acc[pl.ds(away, half), :].astype(BF)
        c = self.copy(R.core_send.at[region, :], R.core_recv.at[region, :], 0, place.across("dp", 1))
        yield
        c.wait_recv()
        small = pl.ds(self.cbuf, n)
        waits = []
        for m in range(1, PEERS + 1):
            device, number = place.peer(m)
            at = pl.multiple_of(number * n, 16)
            R.cube_send[m - 1, small, :] = (R.acc[pl.ds(pl.multiple_of(self.keep + at, 16), n), :]
                                            + R.core_recv[pl.ds(pl.multiple_of(self.buf + at, 16), n), :].astype(F32)).astype(BF)
            waits.append(self.copy(R.cube_send.at[m - 1, small, :], R.cube_recv.at[m - 1, small, :], m, device))
        total = R.acc[pl.ds(self.own, n), :] + R.core_recv[pl.ds(pl.multiple_of(self.buf + place.cube * n, 16), n), :].astype(F32)
        R.acc[pl.ds(self.own, n), :] = total
        yield
        for c in waits:
            c.wait_recv()
        total = R.acc[pl.ds(self.own, n), :]
        for m in range(PEERS):
            total = total + R.cube_recv[m, small, :].astype(F32)
        for i, weight in enumerate(place.rest):
            R.rest_send[i, small, :] = total.astype(BF)
            c = self.copy(R.rest_send.at[i, small, :], R.rest_recv.at[i, small, :], 2 * PEERS + 2 + i, place.across("dp", weight))
            yield
            c.wait_recv()
            total = R.rest_send[i, small, :].astype(F32) + R.rest_recv[i, small, :].astype(F32)
        own = pl.ds(self.own, n)
        R.sums[own, :] = total.astype(BF)
        waits = []
        for m in range(1, PEERS + 1):
            waits.append(self.copy(R.sums.at[own, :], R.sums.at[own, :], PEERS + m, place.peer(m)[0]))
        yield
        for c in waits:
            c.wait_recv()
        keep = pl.ds(self.keep, half)
        c = self.copy(R.sums.at[keep, :], R.sums.at[keep, :], 2 * PEERS + 1, place.across("dp", 1))
        yield
        c.wait_recv()

    def finish(self):
        for c in self.sent:
            c.wait_send()


class VectorSums(Sums):
    def __init__(self, R, place, e):
        self.R, self.place, self.e = R, place, e
        self.sent = []

    def steps(self):
        R, place = self.R, self.place
        R.vec_send[0] = R.vec[...]
        c = self.copy(R.vec_send.at[0], R.vec_recv.at[0], 0, place.across("dp", 1))
        yield
        c.wait_recv()
        R.vec_cube[place.cube] = R.vec_send[0] + R.vec_recv[0]
        waits = []
        for m in range(1, PEERS + 1):
            waits.append(self.copy(R.vec_cube.at[place.cube], R.vec_cube.at[place.cube], m, place.peer(m)[0]))
        yield
        for c in waits:
            c.wait_recv()
        total = R.vec_cube[0]
        for i in range(1, PEERS + 1):
            total = total + R.vec_cube[i]
        for i, weight in enumerate(place.rest):
            R.vec_send[1 + i] = total
            c = self.copy(R.vec_send.at[1 + i], R.vec_recv.at[1 + i], 2 * PEERS + 2 + i, place.across("dp", weight))
            yield
            c.wait_recv()
            total = R.vec_send[1 + i] + R.vec_recv[1 + i]
        R.vec[...] = total


FF_ROWS = 2 * FF + D
QKV_ROWS = 3 * D


def comm_scratch(rows, rest):
    blocks = rows // CH
    dma = pltpu.SemaphoreType.DMA
    total = FF_ROWS + QKV_ROWS
    slots = 2 * PEERS + 2 + rest
    return dict(
        xv=pltpu.VMEM((rows, 256), BF), ev=pltpu.VMEM((rows, 256), BF), gv=pltpu.VMEM((rows, 256), BF),
        stS=pltpu.VMEM((2, rows, 256), BF), grS=pltpu.VMEM((2, rows, 256), BF),
        used_v=pltpu.VMEM((rows // SLOTS, 128), jnp.int32),
        acc=pltpu.VMEM((total, 256), F32), ones_acc=pltpu.VMEM((9, 16, 256), F32),
        core_send=pltpu.VMEM((total // 2, 256), BF), core_recv=pltpu.VMEM((total // 2, 256), BF),
        cube_send=pltpu.VMEM((PEERS, total // 16, 256), BF), cube_recv=pltpu.VMEM((PEERS, total // 16, 256), BF),
        rest_send=pltpu.VMEM((rest, total // 16, 256), BF), rest_recv=pltpu.VMEM((rest, total // 16, 256), BF),
        vec_send=pltpu.VMEM((1 + rest, 16, 256), F32), vec_recv=pltpu.VMEM((1 + rest, 16, 256), F32),
        vec_cube=pltpu.VMEM((PEERS + 1, 16, 256), F32),
        in_sem=dma((blocks, 3)), local_sem=dma((blocks, 2)), ex_send=dma((blocks, 2)), ex_recv=dma((blocks, 2)),
        sum_send=dma((4, slots)), sum_recv=dma((4, slots)))


def kernel(dp_bits, x_hbm, e_hbm, g_hbm, counts_ref, lengths_ref, *refs):
    ws = refs[:15]
    st_hbm, gr_hbm, sums_ref, vec_ref = refs[15:19]
    R = Refs()
    for name, r in zip(list(SCRATCH) + list(comm_scratch(CH, 1)), refs[19:]):
        setattr(R, name, r)
    R.wo_ref, R.wu_ref, R.wd_ref = ws[7], ws[11], ws[13]
    R.sums, R.vec = sums_ref, vec_ref
    R.bwd1_done = 44
    aln, acc, ones_acc = R.aln, R.acc, R.ones_acc
    rows = R.xv.shape[0]
    blocks = rows // CH
    place = Place(dp_bits)
    section, dp = place.section, place.dp

    barrier = pltpu.get_barrier_semaphore()
    everyone = place.everyone()
    for device in everyone:
        pl.semaphore_signal(barrier, inc=1, device_id=device, device_id_type=MESH)

    def fetch(b, k):
        src = (x_hbm, e_hbm, g_hbm)[k]
        dst = (R.xv, R.ev, R.gv)[k]
        start = pl.multiple_of(b * CH, CH)
        return pltpu.make_async_copy(
            src.at[pl.ds(pl.multiple_of(section * rows, CH) + start, CH), :],
            dst.at[pl.ds(start, CH), :], R.in_sem.at[b, k])

    def start_fetches(b, c):
        for k in range(3):
            fetch(b, k).start()
        return c
    lax.fori_loop(0, blocks, start_fetches, 0)

    prologue(R, *ws)
    acc[...] = jnp.zeros_like(acc)
    ones_acc[...] = jnp.zeros_like(ones_acc)
    prompts = rows // SLOTS
    at_most = lengths_ref.shape[1]
    j_iota = lax.broadcasted_iota(jnp.int32, (1, at_most), 1)
    for p in range(prompts):
        count = counts_ref[section * prompts + p]
        kept = jnp.where(j_iota < count, lengths_ref[pl.ds(section * prompts + p, 1), :], 0)
        total = jnp.sum(kept.astype(F32), axis=1, keepdims=True).astype(jnp.int32)
        R.used_v[p:p + 1, :] = jnp.broadcast_to(total, (1, 128))

    k_iota = lax.broadcasted_iota(jnp.int32, (KEYS, SLOTS), 0)
    q_iota = lax.broadcasted_iota(jnp.int32, (KEYS, SLOTS), 1)

    def out_copies(b, k):
        stage, out = ((R.stS, st_hbm), (R.grS, gr_hbm))[k]
        here = pl.ds(pl.multiple_of(b * CH, CH), CH)
        there = pl.ds(pl.multiple_of(section * rows, CH) + pl.multiple_of(b * CH, CH), CH)
        own = pltpu.make_async_copy(stage.at[section, here, :], out.at[there, :], R.local_sem.at[b, k])
        sent = pltpu.make_async_remote_copy(
            src_ref=stage.at[1 - section, here, :], dst_ref=out.at[there, :],
            send_sem=R.ex_send.at[b, k], recv_sem=R.ex_recv.at[b, k],
            device_id=(1 - section, dp), device_id_type=MESH)
        return own, sent

    def add_wd(i, t):
        n = min(256, FF - i)
        acc[i:i + n, :] += t[0:n]
        if t.shape[0] > n:
            ones_acc[0] += t[n:]

    def add_wu(j, t):
        acc[FF + j * D:FF + j * D + D, :] += t[0:D]
        ones_acc[1 + j] += t[D:]

    def add_wqkv(j, t):
        acc[FF_ROWS + j * D:FF_ROWS + j * D + D, :] += t[0:D]
        ones_acc[5 + j] += t[D:]

    def add_wo(t):
        acc[2 * FF:2 * FF + D, :] += t[0:D]
        ones_acc[8] += t[D:]
    R.add_wd, R.add_wu, R.add_wqkv, R.add_wo = add_wd, add_wu, add_wqkv, add_wo

    pl.semaphore_wait(barrier, len(everyone))

    def group(g, carry):
        def at(b):
            return pl.ds(pl.multiple_of(g * GROUP + b, 128), 128)

        def load(c):
            b = g * (GROUP // CH) + c
            for k in range(3):
                fetch(b, k).wait()
            tok = slice(c * CH, c * CH + CH)
            src = pl.ds(pl.multiple_of(b * CH, CH), CH)
            e = R.ev[src, :].T
            R.eT[:, tok] = e
            R.uT[:, tok] = R.xv[src, :].T.astype(F32) + e.astype(F32)
            grad = R.gv[src, :].T
            R.gT[:, tok] = grad.astype(F32)
            R.lowT[1, :, tok] = grad
        R.load = load

        def finish_forward(it, b, out):
            R.stS[it, at(b), :] = out.T
            if it == 0:
                R.uT[:, b:b + 128] = out.astype(F32) + R.eT[:, b:b + 128].astype(F32)
        R.finish_forward = finish_forward

        def finish_backward(it, b, low):
            R.grS[it, at(b), :] = low.T
            if it == 1:
                R.gT[:, b:b + 128] = low.astype(F32)
                R.lowT[0, :, b:b + 128] = low
        R.finish_backward = finish_backward

        def send(c, k):
            for copy in out_copies(g * (GROUP // CH) + c, k):
                copy.start()
        R.send = send

        masks = []
        for p in range(PG):
            used = R.used_v[pl.ds(g * PG + p, 1), :]
            masks.append(jnp.where((k_iota <= q_iota) & (k_iota < used), 0.0, -1e30).astype(F32))
        run_group(R, masks, LAG)

        @pl.when(g < rows // GROUP - 1)
        def _():
            for c in range(GROUP // CH):
                send(c, 1)
        return carry

    lax.fori_loop(0, rows // GROUP, group, 0)

    for i, j in enumerate((0, 1, 5, 6)):
        vec_ref[j:j + 1, :] = jnp.sum(aln[i].T, axis=0, keepdims=True)
    for i, j in ((0, 7), (1, 8), (2, 9), (3, 10), (4, 11), (5, 2), (7, 3), (8, 4)):
        vec_ref[j:j + 1, :] = ones_acc[i, 0:1, :]
    vec_ref[12:16, :] = jnp.zeros((4, D), F32)

    sums = [Sums(R, place, 0, 0, FF), Sums(R, place, 1, FF, FF_ROWS - FF), Sums(R, place, 2, FF_ROWS, QKV_ROWS), VectorSums(R, place, 3)]
    running = [x.steps() for x in sums]
    turn = 0
    while running:
        for x in list(running):
            try:
                next(x)
            except StopIteration:
                running.remove(x)
        turn += 1
        if turn == LAST_GRADIENTS:
            for c in range(GROUP // CH):
                for copy in out_copies(blocks - GROUP // CH + c, 1):
                    copy.start()
    for x in sums:
        x.finish()

    def finish_out(b, c):
        for k in range(2):
            own, sent = out_copies(b, k)
            own.wait()
            sent.wait()
        return c
    lax.fori_loop(0, blocks, finish_out, 0)


def compute(x, e, g, counts, lengths, params, dp_size):
    local = x.shape[0]
    rows = local // 2
    dp_bits = dp_size.bit_length() - 1
    rest = dp_bits - 3
    hbm = pl.BlockSpec(memory_space=pl.ANY)
    smem = pl.BlockSpec(memory_space=pltpu.SMEM)
    vmem = pl.BlockSpec(memory_space=pltpu.VMEM)
    outs = [
        jax.ShapeDtypeStruct((local, 256), BF),
        jax.ShapeDtypeStruct((local, 256), BF),
        jax.ShapeDtypeStruct((3072, 256), BF),
        jax.ShapeDtypeStruct((16, 256), F32),
    ]
    return pl.pallas_call(
        functools.partial(kernel, dp_bits),
        out_shape=outs,
        in_specs=[hbm, hbm, hbm, smem, vmem] + [vmem] * 15,
        out_specs=[hbm, hbm, vmem, vmem],
        scratch_shapes=[pltpu.VMEM(s, t) for s, t in SCRATCH.values()] + list(comm_scratch(rows, rest).values()),
        compiler_params=pltpu.CompilerParams(
            vmem_limit_bytes=62 * 1024 * 1024, collective_id=0, has_side_effects=True),
    )(x, e, g, counts, lengths, *params)


CHUNKS = 8


def widen_kernel(st_ref, gr_ref, sums_ref, vec_ref, st_out, gr_out, n1g, n1b, wq, qb, wk, wv, vb, wo, ob, n2g, n2b, wu, ub, wd, db,
                 st_v, gr_v, gr_w, sums_v, wd_v, wu_v, wa_v, st_in, gr_in, sum_in, st_sem, gr_sem, w_sem):
    block = st_v.shape[0] // CHUNKS
    sums_in = [pltpu.make_async_copy(sums_ref.at[rows, :], sums_v.at[rows, :], sum_in.at[i])
               for i, rows in enumerate((pl.ds(0, FF), pl.ds(FF, FF + D + QKV_ROWS)))]
    parts = [pl.ds(i * block, block) for i in range(CHUNKS)]
    gr_ins = [pltpu.make_async_copy(gr_ref.at[r, :], gr_v.at[r, :], gr_in.at[i]) for i, r in enumerate(parts)]
    st_ins = [pltpu.make_async_copy(st_ref.at[r, :], st_v.at[r, :], st_in.at[i]) for i, r in enumerate(parts)]
    outs = []

    def out(src, dst, sem):
        c = pltpu.make_async_copy(src, dst, sem)
        c.start()
        outs.append(c)

    for c in gr_ins[:2] + sums_in + gr_ins[2:] + st_ins:
        c.start()

    def gradients(i):
        gr_ins[i].wait()
        gr_w[parts[i], :] = gr_v[parts[i], :].astype(F32)
        out(gr_w.at[parts[i], :], gr_out.at[0, parts[i], :], gr_sem.at[i])

    gradients(0)
    gradients(1)
    sums_in[0].wait()
    wd_v[...] = sums_v[0:FF, :].astype(F32)
    out(wd_v, wd, w_sem.at[0])
    sums_in[1].wait()
    for j in range(FF // D):
        wu_v[:, D * j:D * j + D] = sums_v[FF + D * j:FF + D * j + D, :].astype(F32)
    out(wu_v, wu, w_sem.at[1])
    wa_v[...] = sums_v[2 * FF:2 * FF + 4 * D, :].astype(F32)
    for j, r in enumerate((wo, wq, wk, wv)):
        out(wa_v.at[D * j:D * j + D, :], r, w_sem.at[2 + j])
    for i in range(2, CHUNKS):
        gradients(i)
    for j in range(FF // D):
        ub[D * j:D * j + D] = vec_ref[8 + j]
    for j, r in enumerate((n1g, n1b, qb, vb, ob, n2g, n2b, db)):
        r[...] = vec_ref[j]
    for i in range(CHUNKS):
        st_ins[i].wait()
        out(st_v.at[parts[i], :], st_out.at[0, parts[i], :], st_sem.at[i])
    for c in outs:
        c.wait()


def widen(st, gr, sums, vec, params):
    local = st.shape[0]
    outs = [jax.ShapeDtypeStruct((1, local, 256), BF), jax.ShapeDtypeStruct((1, local, 256), F32)]
    outs += [jax.ShapeDtypeStruct(p.shape, F32) for p in params]
    hbm = pl.BlockSpec(memory_space=pl.ANY)
    vmem = pl.BlockSpec(memory_space=pltpu.VMEM)
    dma = pltpu.SemaphoreType.DMA
    return pl.pallas_call(
        widen_kernel,
        out_shape=outs,
        in_specs=[hbm, hbm, hbm, vmem],
        out_specs=[hbm, hbm] + [hbm if len(p.shape) == 2 else vmem for p in params],
        scratch_shapes=[
            pltpu.VMEM((local, 256), BF), pltpu.VMEM((local, 256), BF), pltpu.VMEM((local, 256), F32),
            pltpu.VMEM(sums.shape, BF), pltpu.VMEM((FF, D), F32), pltpu.VMEM((D, FF), F32), pltpu.VMEM((4 * D, D), F32),
            dma((CHUNKS,)), dma((CHUNKS,)), dma((2,)), dma((CHUNKS,)), dma((CHUNKS,)), dma((6,))],
        compiler_params=pltpu.CompilerParams(vmem_limit_bytes=60 * 1024 * 1024),
    )(st, gr, sums, vec)


def solution(mesh):
    dp_size = mesh.shape["dp"]

    def body(x, e, g, counts, lengths, *params):
        st, gr, sums, vec = compute(x, e, g, counts, lengths, params, dp_size)
        return tuple(widen(st, gr, sums, vec, params))

    placed = (P("dp", None),) * 3 + (P("dp"), P("dp", None)) + (P(),) * 15
    return jax.shard_map(
        body,
        mesh=mesh,
        in_specs=placed,
        out_specs=(P("section", "dp", None),) * 2 + (P(),) * 15,
        check_vma=False,
    )
```

```python
import functools
import math

import jax
import jax.numpy as jnp
from jax import lax
from jax.experimental import pallas as pl
from jax.experimental.pallas import tpu as pltpu
from jax.sharding import PartitionSpec as P

BF = jnp.bfloat16
F32 = jnp.float32
SLOTS = 128
HEADS = 8
KEYS = 112
USED = 104
GROUP = 512
CH = 256
PG = GROUP // SLOTS
EPS = 1e-5


def nn(a, b):
    return lax.dot_general(a, b, (((1,), (0,)), ((), ())), preferred_element_type=F32)


def nt(a, b):
    return lax.dot_general(a, b, (((1,), (1,)), ((), ())), preferred_element_type=F32)


C0 = math.sqrt(2.0 / math.pi)
C1 = C0 * 0.044715
SCALE = 32 ** -0.5
D = 256
FF = 1024


def ln_forward(u_ref, gain, bias, unit_ref, inv_ref, n_ref, lanes):
    for b in range(lanes.start, lanes.stop, 128):
        ln = slice(b, b + 128)
        u = u_ref[:, ln]
        mean = jnp.sum(u, axis=0, keepdims=True) * (1.0 / D)
        c = u - mean
        var = jnp.sum(c * c, axis=0, keepdims=True) * (1.0 / D)
        inv = lax.rsqrt(var + EPS)
        unit = c * inv
        unit_ref[:, ln] = unit
        inv_ref[:, ln] = inv
        n_ref[0:D, ln] = (unit * gain[...] + bias[...]).astype(BF)


def ln_backward(gn_ref, res_ref, unit_ref, inv_ref, gain, gain_acc, bias_acc, out_ref, low_ref, lanes):
    for b in range(lanes.start, lanes.stop, 128):
        ln = slice(b, b + 128)
        gn = gn_ref[:, ln]
        unit = unit_ref[:, ln]
        t = gn * unit
        gain_acc[...] += t
        bias_acc[...] += gn
        s = gn * gain[...]
        m1 = jnp.sum(s, axis=0, keepdims=True) * (1.0 / D)
        m2 = jnp.sum(t * gain[...], axis=0, keepdims=True) * (1.0 / D)
        out = res_ref[:, ln] + inv_ref[:, ln] * (s - m1 - unit * m2)
        out_ref[:, ln] = out
        low_ref[:, ln] = out.astype(BF)


class Refs:
    pass


def chain(R, c, masks):
    L = slice(c * CH, c * CH + CH)
    prompts = range(c * CH // SLOTS, (c + 1) * CH // SLOTS)
    rest = jnp.zeros((KEYS - USED, SLOTS), F32)
    R.load(c)
    yield
    for it in range(2):
        ln_forward(R.uT, R.vecs.at[0], R.vecs.at[1], R.unit1.at[it], R.inv1.at[it], R.n1T.at[it], L)
        yield
        n1 = R.n1T[it, 0:D, L]
        for j, vec in ((0, 2), (1, None), (2, 3)):
            rows = slice(256 * j, 256 * j + 256)
            y = nn(R.wqkvT[rows, :], n1)
            if vec is not None:
                v = R.vecs[vec]
                y = y + jnp.concatenate([v] * (CH // 128), axis=1)
            R.qkvT[it, rows, L] = y.astype(BF)
        yield
        for p in prompts:
            tok = slice(p * 128, p * 128 + 128)
            for h in range(HEADS):
                R.bdq[p, h // 2, 32 * (h % 4):32 * (h % 4) + 32, 128 * (h % 2):128 * (h % 2) + 128] = R.qkvT[it, 32 * h:32 * h + 32, tok]
            R.kN[p] = R.qkvT[it, 256:512, tok].T
            for h2 in range(HEADS // 2):
                R.sc[p, :, 256 * h2:256 * h2 + 256] = nn(R.kN[p, 0:KEYS, 128 * (h2 // 2):128 * (h2 // 2) + 128], R.bdq[p, h2])
            R.vN[it, p] = R.qkvT[it, 512:768, tok].T
            yield
        for p in prompts:
            tok = slice(p * 128, p * 128 + 128)
            for h in range(HEADS):
                ln = slice(128 * h, 128 * h + 128)
                s = R.sc[p, 0:USED, ln] + masks[p]
                m = jnp.max(s, axis=0, keepdims=True)
                pe = jnp.exp2((s - m) * (SCALE * math.log2(math.e)))
                l = jnp.sum(pe, axis=0, keepdims=True)
                pT = pe * (1.0 / l)
                R.p32[it, p, 0:USED, ln] = pT
                R.p16[it, p, 0:KEYS, ln] = jnp.concatenate([pT, rest], axis=0).astype(BF)
            yield
            for h2 in range(HEADS // 2):
                ln = slice(256 * h2, 256 * h2 + 256)
                o = nn(R.qkvT[it, 512 + 64 * h2:576 + 64 * h2, tok], R.p16[it, p, :, ln])
                R.mixT[it, 64 * h2:64 * h2 + 32, tok] = o[0:32, 0:128].astype(BF)
                R.mixT[it, 64 * h2 + 32:64 * h2 + 64, tok] = o[32:64, 128:256].astype(BF)
            yield
        y = nn(R.woT[...], R.mixT[it, 0:D, L])
        for b in range(L.start, L.stop, 128):
            R.mid[:, b:b + 128] = R.uT[:, b:b + 128] + R.vecs[4] + y[:, b - L.start:b - L.start + 128]
        yield
        for p in prompts:
            for h in range(HEADS):
                ln = slice(128 * h, 128 * h + 128)
                R.pN[it, p, :, ln] = R.p16[it, p, :, ln].T
        ln_forward(R.mid, R.vecs.at[5], R.vecs.at[6], R.unit2.at[it], R.inv2.at[it], R.n2T.at[it], L)
        yield
        n2 = R.n2T[it, 0:D, L]
        for half in range(2):
            rows = slice(512 * half, 512 * half + 512)
            R.pre[rows, L] = nn(R.wuT[rows, :], n2)
            yield
            for r in range(rows.start, rows.stop, 32):
                for b in range(L.start, L.stop, 128):
                    at = (slice(r, r + 32), slice(b, b + 128))
                    v = R.pre[at] + R.ubv[r:r + 32, :]
                    v2 = v * v
                    t = jnp.tanh(v * (C0 + C1 * v2))
                    h1 = 0.5 + 0.5 * t
                    hid = v * h1
                    R.gp[it, r:r + 32, b:b + 128] = h1 + (hid - hid * h1) * (2.0 * C0 + 6.0 * C1 * v2)
                    R.hT[it, r:r + 32, b:b + 128] = hid.astype(BF)
            yield
        y = nn(R.wdT[...], R.hT[it, 0:FF, L])
        for b in range(L.start, L.stop, 128):
            out = R.mid[:, b:b + 128] + R.vecs[7] + y[:, b - L.start:b - L.start + 128]
            R.finish_forward(it, b, out.astype(BF))
        if it == 1:
            R.send(c, 0)
        yield
    for it in (1, 0):
        for half in range(2):
            rows = slice(512 * half, 512 * half + 512)
            R.pre[rows, L] = nn(R.wd_ref[rows, :], R.lowT[it, :, L])
            yield
            for r in range(rows.start, rows.stop, 32):
                for b in range(L.start, L.stop, 128):
                    at = (slice(r, r + 32), slice(b, b + 128))
                    R.dpre[it, r:r + 32, b:b + 128] = (R.pre[at] * R.gp[it, r:r + 32, b:b + 128]).astype(BF)
            yield
        R.dn[:, L] = nn(R.wu_ref[...], R.dpre[it, :, L])
        yield
        ln_backward(R.dn, R.gT, R.unit2.at[it], R.inv2.at[it], R.vecs.at[5], R.aln.at[2], R.aln.at[3], R.gT, R.alow.at[it], L)
        yield
        R.dmixT[:, L] = nn(R.wo_ref[...], R.alow[it, :, L]).astype(BF)
        yield
        for p in prompts:
            tok = slice(p * 128, p * 128 + 128)
            for h in range(HEADS):
                R.bdo[p, h // 2, 32 * (h % 4):32 * (h % 4) + 32, 128 * (h % 2):128 * (h % 2) + 128] = R.dmixT[32 * h:32 * h + 32, tok]
            for h2 in range(HEADS // 2):
                R.sc[p, :, 256 * h2:256 * h2 + 256] = nn(R.vN[it, p, 0:KEYS, 128 * (h2 // 2):128 * (h2 // 2) + 128], R.bdo[p, h2])
            yield
        for p in prompts:
            tok = slice(p * 128, p * 128 + 128)
            for h in range(HEADS):
                ln = slice(128 * h, 128 * h + 128)
                pT = R.p32[it, p, 0:USED, ln]
                t = pT * R.sc[p, 0:USED, ln]
                dsum = jnp.sum(t, axis=0, keepdims=True)
                R.ds16[p, 0:KEYS, ln] = jnp.concatenate([t - pT * dsum, rest], axis=0).astype(BF)
                R.dsN[p, :, ln] = R.ds16[p, :, ln].T
            yield
            for h2 in range(HEADS // 2):
                r = 64 * h2
                ln = slice(256 * h2, 256 * h2 + 256)
                for base, left, right, scaled in (
                    (512, R.dmixT[r:r + 64, tok], R.pN[it, p, :, ln], None),
                    (0, R.qkvT[it, 256 + r:320 + r, tok], R.ds16[p, :, ln], SCALE),
                    (256, R.qkvT[it, r:r + 64, tok], R.dsN[p, :, ln], SCALE)):
                    d = nn(left, right)
                    top, low = d[0:32, 0:128], d[32:64, 128:256]
                    if scaled is not None:
                        top, low = top * scaled, low * scaled
                    R.dqkvT[it, base + r:base + r + 32, tok] = top.astype(BF)
                    R.dqkvT[it, base + r + 32:base + r + 64, tok] = low.astype(BF)
            yield
        R.dn[:, L] = nn(R.wqkv[...], R.dqkvT[it, :, L])
        yield
        ln_backward(R.dn, R.gT, R.unit1.at[it], R.inv1.at[it], R.vecs.at[0], R.aln.at[0], R.aln.at[1], R.gT, R.gl16, L)
        for b in range(L.start, L.stop, 128):
            R.finish_backward(it, b, R.gl16[:, b:b + 128])
        yield


def weight_terms(R, it):
    for i in range(0, FF, 256):
        stop = i + 256 if i + 256 < FF else FF + 16
        R.add_wd(i, nt(R.hT[it, i:stop, :], R.lowT[it]))
        yield
    for j in range(FF // D):
        R.add_wu(j, nt(R.n2T[it], R.dpre[it, j * D:j * D + D, :]))
        yield
    R.add_wo(nt(R.mixT[it], R.alow[it]))
    yield
    for j in range(3):
        R.add_wqkv(j, nt(R.n1T[it], R.dqkvT[it, j * D:j * D + D, :]))
        yield


def run_group(R, masks, lag):
    chains = [chain(R, c, masks) for c in range(GROUP // CH)]
    counts = [0] * len(chains)
    done = [False] * len(chains)
    terms = []
    started = set()
    while not all(done) or terms:
        for i, ch in enumerate(chains):
            if done[i] or (i > 0 and counts[i] + lag > counts[i - 1] and not done[i - 1]):
                continue
            try:
                next(ch)
                counts[i] += 1
            except StopIteration:
                done[i] = True
        if min(counts) >= R.bwd1_done and 1 not in started:
            started.add(1)
            terms.append(weight_terms(R, 1))
        if all(done) and 0 not in started:
            started.add(0)
            terms.append(weight_terms(R, 0))
        for t in list(terms):
            try:
                next(t)
            except StopIteration:
                terms.remove(t)


SCRATCH = dict(
    wqkvT=((768, 256), BF), woT=((256, 256), BF), wuT=((1024, 256), BF), wdT=((256, 1024), BF), wqkv=((256, 768), BF),
    vecs=((8, 256, 128), F32), ubv=((1024, 128), F32),
    n1T=((2, 272, GROUP), BF), qkvT=((2, 768, GROUP), BF), kN=((PG, 128, 256), BF), vN=((2, PG, 128, 256), BF),
    bdq=((PG, 4, 128, 256), BF), bdo=((PG, 4, 128, 256), BF),
    sc=((PG, KEYS, 1024), F32), p32=((2, PG, KEYS, 1024), F32), p16=((2, PG, 128, 1024), BF), pN=((2, PG, 128, 1024), BF),
    ds16=((PG, 128, 1024), BF), dsN=((PG, 128, 1024), BF),
    mixT=((2, 272, GROUP), BF), uT=((256, GROUP), F32), eT=((256, GROUP), BF), mid=((256, GROUP), F32), gT=((256, GROUP), F32), dn=((256, GROUP), F32),
    gl16=((256, GROUP), BF),
    unit1=((2, 256, GROUP), F32), inv1=((2, 1, GROUP), F32), unit2=((2, 256, GROUP), F32), inv2=((2, 1, GROUP), F32),
    n2T=((2, 272, GROUP), BF), pre=((1024, GROUP), F32), gp=((2, 1024, GROUP), F32), hT=((2, 1040, GROUP), BF),
    lowT=((2, 256, GROUP), BF), dpre=((2, 1024, GROUP), BF), alow=((2, 256, GROUP), BF), dmixT=((256, GROUP), BF),
    dqkvT=((2, 768, GROUP), BF), aln=((4, 256, 128), F32))


def prologue(R, n1g, n1b, wq, qb, wk, wv, vb, wo, ob, n2g, n2b, wu, ub, wd, db):
    R.wqkvT[0:256, :] = wq[...].T
    R.wqkvT[256:512, :] = wk[...].T
    R.wqkvT[512:768, :] = wv[...].T
    R.woT[...] = wo[...].T
    R.wuT[...] = wu[...].T
    R.wdT[...] = wd[...].T
    R.wqkv[:, 0:256] = wq[...]
    R.wqkv[:, 256:512] = wk[...]
    R.wqkv[:, 512:768] = wv[...]
    for i, r in enumerate((n1g, n1b, qb, vb, ob, n2g, n2b, db)):
        R.vecs[i] = jnp.broadcast_to(r[...].astype(F32).reshape(1, D), (128, D)).T
    R.ubv[...] = jnp.broadcast_to(ub[...].astype(F32).reshape(1, FF), (128, FF)).T
    for r in (R.aln, R.bdq, R.bdo, R.ds16, R.p16):
        r[...] = jnp.zeros_like(r)
    for it in range(2):
        for r in (R.n1T, R.mixT, R.n2T):
            r[it, D:, :] = jnp.ones((16, GROUP), BF)
        R.hT[it, FF:, :] = jnp.ones((16, GROUP), BF)


LAG = 3
LAST_GRADIENTS = 2
MESH = pl.DeviceIdType.MESH
CUBE = (("dp", 2), ("section", 1), ("dp", 4))
PEERS = 7


class Place:
    def __init__(self, dp_bits):
        self.section = lax.axis_index("section")
        self.dp = lax.axis_index("dp")
        self.core = lax.rem(self.dp, 2)
        self.rest = [1 << b for b in range(3, dp_bits)]
        self.bits = [self.bit(axis, weight) for axis, weight in CUBE]
        self.cube = self.bits[0] + 2 * self.bits[1] + 4 * self.bits[2]

    def bit(self, axis, weight):
        return self.section if axis == "section" else lax.rem(lax.div(self.dp, weight), 2)

    def across(self, axis, weight):
        if axis == "section":
            return (1 - self.section, self.dp)
        return (self.section, self.dp + (1 - 2 * self.bit(axis, weight)) * weight)

    def peer(self, mask):
        section, dp, number = self.section, self.dp, 0
        for i, (axis, weight) in enumerate(CUBE):
            v = self.bits[i]
            if mask >> i & 1:
                if axis == "section":
                    section = 1 - section
                else:
                    dp = dp + (1 - 2 * v) * weight
                v = 1 - v
            number = number + v * (1 << i)
        return (section, dp), number

    def everyone(self):
        found = [self.across("dp", 1)] + [self.peer(m)[0] for m in range(1, PEERS + 1)]
        return found + [self.across("dp", w) for w in self.rest]


class Sums:
    def __init__(self, R, place, e, base, rows):
        self.R, self.place, self.e, self.base = R, place, e, base
        self.half, self.n = rows // 2, rows // 16
        self.sent = []
        self.buf = base // 2
        self.cbuf = base // 16
        self.keep = pl.multiple_of(base + place.core * self.half, 16)
        self.own = pl.multiple_of(self.keep + place.cube * self.n, 16)

    def copy(self, src, dst, slot, device):
        R = self.R
        c = pltpu.make_async_remote_copy(src_ref=src, dst_ref=dst, send_sem=R.sum_send.at[self.e, slot],
                                         recv_sem=R.sum_recv.at[self.e, slot], device_id=device, device_id_type=MESH)
        c.start()
        self.sent.append(c)
        return c

    def steps(self):
        R, place, half, n = self.R, self.place, self.half, self.n
        region = pl.ds(self.buf, half)
        away = pl.multiple_of(self.base + (1 - place.core) * half, 16)
        R.core_send[region, :] = R.acc[pl.ds(away, half), :].astype(BF)
        c = self.copy(R.core_send.at[region, :], R.core_recv.at[region, :], 0, place.across("dp", 1))
        yield
        c.wait_recv()
        small = pl.ds(self.cbuf, n)
        waits = []
        for m in range(1, PEERS + 1):
            device, number = place.peer(m)
            at = pl.multiple_of(number * n, 16)
            R.cube_send[m - 1, small, :] = (R.acc[pl.ds(pl.multiple_of(self.keep + at, 16), n), :]
                                            + R.core_recv[pl.ds(pl.multiple_of(self.buf + at, 16), n), :].astype(F32)).astype(BF)
            waits.append(self.copy(R.cube_send.at[m - 1, small, :], R.cube_recv.at[m - 1, small, :], m, device))
        total = R.acc[pl.ds(self.own, n), :] + R.core_recv[pl.ds(pl.multiple_of(self.buf + place.cube * n, 16), n), :].astype(F32)
        R.acc[pl.ds(self.own, n), :] = total
        yield
        for c in waits:
            c.wait_recv()
        total = R.acc[pl.ds(self.own, n), :]
        for m in range(PEERS):
            total = total + R.cube_recv[m, small, :].astype(F32)
        for i, weight in enumerate(place.rest):
            R.rest_send[i, small, :] = total.astype(BF)
            c = self.copy(R.rest_send.at[i, small, :], R.rest_recv.at[i, small, :], 2 * PEERS + 2 + i, place.across("dp", weight))
            yield
            c.wait_recv()
            total = R.rest_send[i, small, :].astype(F32) + R.rest_recv[i, small, :].astype(F32)
        own = pl.ds(self.own, n)
        R.sums[own, :] = total.astype(BF)
        waits = []
        for m in range(1, PEERS + 1):
            waits.append(self.copy(R.sums.at[own, :], R.sums.at[own, :], PEERS + m, place.peer(m)[0]))
        yield
        for c in waits:
            c.wait_recv()
        keep = pl.ds(self.keep, half)
        c = self.copy(R.sums.at[keep, :], R.sums.at[keep, :], 2 * PEERS + 1, place.across("dp", 1))
        yield
        c.wait_recv()

    def finish(self):
        for c in self.sent:
            c.wait_send()


class VectorSums(Sums):
    def __init__(self, R, place, e):
        self.R, self.place, self.e = R, place, e
        self.sent = []

    def steps(self):
        R, place = self.R, self.place
        R.vec_send[0] = R.vec[...]
        c = self.copy(R.vec_send.at[0], R.vec_recv.at[0], 0, place.across("dp", 1))
        yield
        c.wait_recv()
        R.vec_cube[place.cube] = R.vec_send[0] + R.vec_recv[0]
        waits = []
        for m in range(1, PEERS + 1):
            waits.append(self.copy(R.vec_cube.at[place.cube], R.vec_cube.at[place.cube], m, place.peer(m)[0]))
        yield
        for c in waits:
            c.wait_recv()
        total = R.vec_cube[0]
        for i in range(1, PEERS + 1):
            total = total + R.vec_cube[i]
        for i, weight in enumerate(place.rest):
            R.vec_send[1 + i] = total
            c = self.copy(R.vec_send.at[1 + i], R.vec_recv.at[1 + i], 2 * PEERS + 2 + i, place.across("dp", weight))
            yield
            c.wait_recv()
            total = R.vec_send[1 + i] + R.vec_recv[1 + i]
        R.vec[...] = total


FF_ROWS = 2 * FF + D
QKV_ROWS = 3 * D


def comm_scratch(rows, rest):
    blocks = rows // CH
    dma = pltpu.SemaphoreType.DMA
    total = FF_ROWS + QKV_ROWS
    slots = 2 * PEERS + 2 + rest
    return dict(
        stS=pltpu.VMEM((2, rows, 256), BF), grS=pltpu.VMEM((2, rows, 256), BF),
        used_v=pltpu.VMEM((rows // SLOTS, 128), jnp.int32),
        acc=pltpu.VMEM((total, 256), F32), ones_acc=pltpu.VMEM((9, 16, 256), F32),
        core_send=pltpu.VMEM((total // 2, 256), BF), core_recv=pltpu.VMEM((total // 2, 256), BF),
        cube_send=pltpu.VMEM((PEERS, total // 16, 256), BF), cube_recv=pltpu.VMEM((PEERS, total // 16, 256), BF),
        rest_send=pltpu.VMEM((rest, total // 16, 256), BF), rest_recv=pltpu.VMEM((rest, total // 16, 256), BF),
        vec_send=pltpu.VMEM((1 + rest, 16, 256), F32), vec_recv=pltpu.VMEM((1 + rest, 16, 256), F32),
        vec_cube=pltpu.VMEM((PEERS + 1, 16, 256), F32),
        in_sem=dma((blocks, 3)), local_sem=dma((blocks, 2)), ex_send=dma((blocks, 2)), ex_recv=dma((blocks, 2)),
        sum_send=dma((4, slots)), sum_recv=dma((4, slots)))


def kernel(dp_bits, x_hbm, e_hbm, g_hbm, counts_ref, lengths_ref, *refs):
    ws = refs[:15]
    st_hbm, gr_hbm, sums_ref, vec_ref = refs[15:19]
    R = Refs()
    for name, r in zip(list(SCRATCH) + list(comm_scratch(CH, 1)), refs[19:]):
        setattr(R, name, r)
    R.wo_ref, R.wu_ref, R.wd_ref = ws[7], ws[11], ws[13]
    R.sums, R.vec = sums_ref, vec_ref
    R.bwd1_done = 44
    aln, acc, ones_acc = R.aln, R.acc, R.ones_acc
    rows = R.stS.shape[1]
    blocks = rows // CH
    place = Place(dp_bits)
    section, dp = place.section, place.dp

    barrier = pltpu.get_barrier_semaphore()
    everyone = place.everyone()
    for device in everyone:
        pl.semaphore_signal(barrier, inc=1, device_id=device, device_id_type=MESH)

    def fetch(b, k):
        src = (x_hbm, e_hbm, g_hbm)[k]
        dst = (R.grS.at[0], R.stS.at[0], R.grS.at[1])[k]
        start = pl.multiple_of(b * CH, CH)
        return pltpu.make_async_copy(
            src.at[pl.ds(pl.multiple_of(section * rows, CH) + start, CH), :],
            dst.at[pl.ds(start, CH), :], R.in_sem.at[b, k])

    def start_fetches(b, c):
        for k in range(3):
            fetch(b, k).start()
        return c
    lax.fori_loop(0, blocks, start_fetches, 0)

    prologue(R, *ws)
    acc[...] = jnp.zeros_like(acc)
    ones_acc[...] = jnp.zeros_like(ones_acc)
    prompts = rows // SLOTS
    at_most = lengths_ref.shape[1]
    j_iota = lax.broadcasted_iota(jnp.int32, (1, at_most), 1)
    for p in range(prompts):
        count = counts_ref[section * prompts + p]
        kept = jnp.where(j_iota < count, lengths_ref[pl.ds(section * prompts + p, 1), :], 0)
        total = jnp.sum(kept.astype(F32), axis=1, keepdims=True).astype(jnp.int32)
        R.used_v[p:p + 1, :] = jnp.broadcast_to(total, (1, 128))

    k_iota = lax.broadcasted_iota(jnp.int32, (USED, SLOTS), 0)
    q_iota = lax.broadcasted_iota(jnp.int32, (USED, SLOTS), 1)

    def out_copies(b, k):
        stage, out = ((R.stS, st_hbm), (R.grS, gr_hbm))[k]
        here = pl.ds(pl.multiple_of(b * CH, CH), CH)
        there = pl.ds(pl.multiple_of(section * rows, CH) + pl.multiple_of(b * CH, CH), CH)
        own = pltpu.make_async_copy(stage.at[section, here, :], out.at[there, :], R.local_sem.at[b, k])
        sent = pltpu.make_async_remote_copy(
            src_ref=stage.at[1 - section, here, :], dst_ref=out.at[there, :],
            send_sem=R.ex_send.at[b, k], recv_sem=R.ex_recv.at[b, k],
            device_id=(1 - section, dp), device_id_type=MESH)
        return own, sent

    def add_wd(i, t):
        n = min(256, FF - i)
        acc[i:i + n, :] += t[0:n]
        if t.shape[0] > n:
            ones_acc[0] += t[n:]

    def add_wu(j, t):
        acc[FF + j * D:FF + j * D + D, :] += t[0:D]
        ones_acc[1 + j] += t[D:]

    def add_wqkv(j, t):
        acc[FF_ROWS + j * D:FF_ROWS + j * D + D, :] += t[0:D]
        ones_acc[5 + j] += t[D:]

    def add_wo(t):
        acc[2 * FF:2 * FF + D, :] += t[0:D]
        ones_acc[8] += t[D:]
    R.add_wd, R.add_wu, R.add_wqkv, R.add_wo = add_wd, add_wu, add_wqkv, add_wo

    pl.semaphore_wait(barrier, len(everyone))

    def group(g, carry):
        def at(b):
            return pl.ds(pl.multiple_of(g * GROUP + b, 128), 128)

        def load(c):
            b = g * (GROUP // CH) + c
            for k in range(3):
                fetch(b, k).wait()
            tok = slice(c * CH, c * CH + CH)
            src = pl.ds(pl.multiple_of(b * CH, CH), CH)
            e = R.stS[0, src, :].T
            R.eT[:, tok] = e
            R.uT[:, tok] = R.grS[0, src, :].T.astype(F32) + e.astype(F32)
            grad = R.grS[1, src, :].T
            R.gT[:, tok] = grad.astype(F32)
            R.lowT[1, :, tok] = grad
        R.load = load

        def finish_forward(it, b, out):
            R.stS[it, at(b), :] = out.T
            if it == 0:
                R.uT[:, b:b + 128] = out.astype(F32) + R.eT[:, b:b + 128].astype(F32)
        R.finish_forward = finish_forward

        def finish_backward(it, b, low):
            R.grS[it, at(b), :] = low.T
            if it == 1:
                R.gT[:, b:b + 128] = low.astype(F32)
                R.lowT[0, :, b:b + 128] = low
        R.finish_backward = finish_backward

        def send(c, k):
            for copy in out_copies(g * (GROUP // CH) + c, k):
                copy.start()
        R.send = send

        masks = []
        for p in range(PG):
            used = R.used_v[pl.ds(g * PG + p, 1), :]
            masks.append(jnp.where((k_iota <= q_iota) & (k_iota < used), 0.0, -1e30).astype(F32))
        run_group(R, masks, LAG)

        @pl.when(g < rows // GROUP - 1)
        def _():
            for c in range(GROUP // CH):
                send(c, 1)
        return carry

    lax.fori_loop(0, rows // GROUP, group, 0)

    for i, j in enumerate((0, 1, 5, 6)):
        vec_ref[j:j + 1, :] = jnp.sum(aln[i].T, axis=0, keepdims=True)
    for i, j in ((0, 7), (1, 8), (2, 9), (3, 10), (4, 11), (5, 2), (7, 3), (8, 4)):
        vec_ref[j:j + 1, :] = ones_acc[i, 0:1, :]
    vec_ref[12:16, :] = jnp.zeros((4, D), F32)

    sums = [Sums(R, place, 0, 0, FF), Sums(R, place, 1, FF, FF_ROWS - FF), Sums(R, place, 2, FF_ROWS, QKV_ROWS), VectorSums(R, place, 3)]
    running = [x.steps() for x in sums]
    turn = 0
    while running:
        for x in list(running):
            try:
                next(x)
            except StopIteration:
                running.remove(x)
        turn += 1
        if turn == LAST_GRADIENTS:
            for c in range(GROUP // CH):
                for copy in out_copies(blocks - GROUP // CH + c, 1):
                    copy.start()
    for x in sums:
        x.finish()

    def finish_out(b, c):
        for k in range(2):
            own, sent = out_copies(b, k)
            own.wait()
            sent.wait()
        return c
    lax.fori_loop(0, blocks, finish_out, 0)


def compute(x, e, g, counts, lengths, params, dp_size):
    local = x.shape[0]
    rows = local // 2
    dp_bits = dp_size.bit_length() - 1
    rest = dp_bits - 3
    hbm = pl.BlockSpec(memory_space=pl.ANY)
    smem = pl.BlockSpec(memory_space=pltpu.SMEM)
    vmem = pl.BlockSpec(memory_space=pltpu.VMEM)
    outs = [
        jax.ShapeDtypeStruct((local, 256), BF),
        jax.ShapeDtypeStruct((local, 256), BF),
        jax.ShapeDtypeStruct((3072, 256), BF),
        jax.ShapeDtypeStruct((16, 256), F32),
    ]
    return pl.pallas_call(
        functools.partial(kernel, dp_bits),
        out_shape=outs,
        in_specs=[hbm, hbm, hbm, smem, vmem] + [vmem] * 15,
        out_specs=[hbm, hbm, vmem, vmem],
        scratch_shapes=[pltpu.VMEM(s, t) for s, t in SCRATCH.values()] + list(comm_scratch(rows, rest).values()),
        compiler_params=pltpu.CompilerParams(
            vmem_limit_bytes=57 * 1024 * 1024, collective_id=0, has_side_effects=True),
    )(x, e, g, counts, lengths, *params)


CHUNKS = 2


def widen_kernel(st_ref, gr_ref, sums_ref, vec_ref, st_out, gr_out, n1g, n1b, wq, qb, wk, wv, vb, wo, ob, n2g, n2b, wu, ub, wd, db,
                 st_v, gr_v, gr_w, sums_v, wd_v, wu_v, wa_v, st_in, gr_in, sum_in, st_sem, gr_sem, w_sem, v_sem, ub_v, *vec_v):
    block = st_v.shape[0] // CHUNKS
    sums_in = [pltpu.make_async_copy(sums_ref.at[rows, :], sums_v.at[rows, :], sum_in.at[i])
               for i, rows in enumerate((pl.ds(0, FF), pl.ds(FF, FF + D + QKV_ROWS)))]
    parts = [pl.ds(i * block, block) for i in range(CHUNKS)]
    gr_ins = [pltpu.make_async_copy(gr_ref.at[r, :], gr_v.at[r, :], gr_in.at[i]) for i, r in enumerate(parts)]
    st_ins = [pltpu.make_async_copy(st_ref.at[r, :], st_v.at[r, :], st_in.at[i]) for i, r in enumerate(parts)]
    outs = []

    def out(src, dst, sem):
        c = pltpu.make_async_copy(src, dst, sem)
        c.start()
        outs.append(c)

    for c in gr_ins[:2] + sums_in + gr_ins[2:] + st_ins:
        c.start()

    def gradients(i):
        gr_ins[i].wait()
        gr_w[parts[i], :] = gr_v[parts[i], :].astype(F32)
        out(gr_w.at[parts[i], :], gr_out.at[0, parts[i], :], gr_sem.at[i])

    for j in range(FF // D):
        ub_v[D * j:D * j + D] = vec_ref[8 + j]
    out(ub_v, ub, v_sem.at[8])
    for j, (r, v) in enumerate(zip((n1g, n1b, qb, vb, ob, n2g, n2b, db), vec_v)):
        v[...] = vec_ref[j]
        out(v, r, v_sem.at[j])
    gradients(0)
    sums_in[0].wait()
    wd_v[...] = sums_v[0:FF, :].astype(F32)
    out(wd_v, wd, w_sem.at[0])
    sums_in[1].wait()
    for j in range(FF // D):
        wu_v[:, D * j:D * j + D] = sums_v[FF + D * j:FF + D * j + D, :].astype(F32)
    out(wu_v, wu, w_sem.at[1])
    wa_v[...] = sums_v[2 * FF:2 * FF + 4 * D, :].astype(F32)
    for j, r in enumerate((wo, wq, wk, wv)):
        out(wa_v.at[D * j:D * j + D, :], r, w_sem.at[2 + j])
    for i in range(1, CHUNKS):
        gradients(i)
    for i in range(CHUNKS):
        st_ins[i].wait()
        out(st_v.at[parts[i], :], st_out.at[0, parts[i], :], st_sem.at[i])
    for c in outs:
        c.wait()


def widen(st, gr, sums, vec, params):
    local = st.shape[0]
    outs = [jax.ShapeDtypeStruct((1, local, 256), BF), jax.ShapeDtypeStruct((1, local, 256), F32)]
    outs += [jax.ShapeDtypeStruct(p.shape, F32) for p in params]
    hbm = pl.BlockSpec(memory_space=pl.ANY)
    vmem = pl.BlockSpec(memory_space=pltpu.VMEM)
    dma = pltpu.SemaphoreType.DMA
    return pl.pallas_call(
        widen_kernel,
        out_shape=outs,
        in_specs=[hbm, hbm, hbm, vmem],
        out_specs=[hbm] * len(outs),
        scratch_shapes=[
            pltpu.VMEM((local, 256), BF), pltpu.VMEM((local, 256), BF), pltpu.VMEM((local, 256), F32),
            pltpu.VMEM(sums.shape, BF), pltpu.VMEM((FF, D), F32), pltpu.VMEM((D, FF), F32), pltpu.VMEM((4 * D, D), F32),
            dma((CHUNKS,)), dma((CHUNKS,)), dma((2,)), dma((CHUNKS,)), dma((CHUNKS,)), dma((6,)), dma((9,)), pltpu.VMEM((FF,), F32)] + [pltpu.VMEM((D,), F32)] * 8,
        compiler_params=pltpu.CompilerParams(vmem_limit_bytes=58 * 1024 * 1024),
    )(st, gr, sums, vec)


def solution(mesh):
    dp_size = mesh.shape["dp"]

    def body(x, e, g, counts, lengths, *params):
        st, gr, sums, vec = compute(x, e, g, counts, lengths, params, dp_size)
        return tuple(widen(st, gr, sums, vec, params))

    placed = (P("dp", None),) * 3 + (P("dp"), P("dp", None)) + (P(),) * 15
    return jax.shard_map(
        body,
        mesh=mesh,
        in_specs=placed,
        out_specs=(P("section", "dp", None),) * 2 + (P(),) * 15,
        check_vma=False,
    )
```

```python
import functools
import math

import jax
import jax.numpy as jnp
from jax import lax
from jax.experimental import pallas as pl
from jax.experimental.pallas import tpu as pltpu
from jax.sharding import PartitionSpec as P

BF = jnp.bfloat16
F32 = jnp.float32
SLOTS = 128
HEADS = 8
KEYS = 112
USED = 104
GROUP = 512
CH = 256
PG = GROUP // SLOTS
EPS = 1e-5


def nn(a, b):
    return lax.dot_general(a, b, (((1,), (0,)), ((), ())), preferred_element_type=F32)


def nt(a, b):
    return lax.dot_general(a, b, (((1,), (1,)), ((), ())), preferred_element_type=F32)


C0 = math.sqrt(2.0 / math.pi)
C1 = C0 * 0.044715
SCALE = 32 ** -0.5
D = 256
FF = 1024


def ln_forward(u_ref, gain, bias, unit_ref, inv_ref, n_ref, lanes):
    for b in range(lanes.start, lanes.stop, 128):
        ln = slice(b, b + 128)
        u = u_ref[:, ln]
        mean = jnp.sum(u, axis=0, keepdims=True) * (1.0 / D)
        c = u - mean
        var = jnp.sum(c * c, axis=0, keepdims=True) * (1.0 / D)
        inv = lax.rsqrt(var + EPS)
        unit = c * inv
        unit_ref[:, ln] = unit
        inv_ref[:, ln] = inv
        n_ref[0:D, ln] = (unit * gain[...] + bias[...]).astype(BF)


def ln_backward(gn_ref, res_ref, unit_ref, inv_ref, gain, gain_acc, bias_acc, out_ref, low_ref, lanes):
    for b in range(lanes.start, lanes.stop, 128):
        ln = slice(b, b + 128)
        gn = gn_ref[:, ln]
        unit = unit_ref[:, ln]
        t = gn * unit
        gain_acc[...] += t
        bias_acc[...] += gn
        s = gn * gain[...]
        m1 = jnp.sum(s, axis=0, keepdims=True) * (1.0 / D)
        m2 = jnp.sum(t * gain[...], axis=0, keepdims=True) * (1.0 / D)
        out = res_ref[:, ln] + inv_ref[:, ln] * (s - m1 - unit * m2)
        out_ref[:, ln] = out
        low_ref[:, ln] = out.astype(BF)


class Refs:
    pass


def chain(R, c, masks):
    L = slice(c * CH, c * CH + CH)
    prompts = range(c * CH // SLOTS, (c + 1) * CH // SLOTS)
    rest = jnp.zeros((KEYS - USED, SLOTS), F32)
    R.load(c)
    yield
    for it in range(2):
        ln_forward(R.uT, R.vecs.at[0], R.vecs.at[1], R.unit1.at[it], R.inv1.at[it], R.n1T.at[it], L)
        yield
        n1 = R.n1T[it, 0:D, L]
        for j, vec in ((0, 2), (1, None), (2, 3)):
            rows = slice(256 * j, 256 * j + 256)
            y = nn(R.wqkvT[rows, :], n1)
            if vec is not None:
                v = R.vecs[vec]
                y = y + jnp.concatenate([v] * (CH // 128), axis=1)
            R.qkvT[it, rows, L] = y.astype(BF)
        yield
        for p in prompts:
            tok = slice(p * 128, p * 128 + 128)
            for h in range(HEADS):
                R.bdq[p, h // 2, 32 * (h % 4):32 * (h % 4) + 32, 128 * (h % 2):128 * (h % 2) + 128] = R.qkvT[it, 32 * h:32 * h + 32, tok]
            R.kN[p] = R.qkvT[it, 256:512, tok].T
            for h2 in range(HEADS // 2):
                R.sc[p, :, 256 * h2:256 * h2 + 256] = nn(R.kN[p, 0:KEYS, 128 * (h2 // 2):128 * (h2 // 2) + 128], R.bdq[p, h2])
            R.vN[it, p] = R.qkvT[it, 512:768, tok].T
            yield
        for p in prompts:
            tok = slice(p * 128, p * 128 + 128)
            for h in range(HEADS):
                ln = slice(128 * h, 128 * h + 128)
                s = R.sc[p, 0:USED, ln] + masks[p]
                m = jnp.max(s, axis=0, keepdims=True)
                pe = jnp.exp2((s - m) * (SCALE * math.log2(math.e)))
                l = jnp.sum(pe, axis=0, keepdims=True)
                pT = pe * (1.0 / l)
                R.p32[it, p, 0:USED, ln] = pT
                R.p16[it, p, 0:KEYS, ln] = jnp.concatenate([pT, rest], axis=0).astype(BF)
            yield
            for h2 in range(HEADS // 2):
                ln = slice(256 * h2, 256 * h2 + 256)
                o = nn(R.qkvT[it, 512 + 64 * h2:576 + 64 * h2, tok], R.p16[it, p, :, ln])
                R.mixT[it, 64 * h2:64 * h2 + 32, tok] = o[0:32, 0:128].astype(BF)
                R.mixT[it, 64 * h2 + 32:64 * h2 + 64, tok] = o[32:64, 128:256].astype(BF)
            yield
        y = nn(R.woT[...], R.mixT[it, 0:D, L])
        for b in range(L.start, L.stop, 128):
            R.mid[:, b:b + 128] = R.uT[:, b:b + 128] + R.vecs[4] + y[:, b - L.start:b - L.start + 128]
        yield
        for p in prompts:
            for h in range(HEADS):
                ln = slice(128 * h, 128 * h + 128)
                R.pN[it, p, :, ln] = R.p16[it, p, :, ln].T
        ln_forward(R.mid, R.vecs.at[5], R.vecs.at[6], R.unit2.at[it], R.inv2.at[it], R.n2T.at[it], L)
        yield
        n2 = R.n2T[it, 0:D, L]
        for half in range(2):
            rows = slice(512 * half, 512 * half + 512)
            R.pre[rows, L] = nn(R.wuT[rows, :], n2)
            yield
            for r in range(rows.start, rows.stop, 32):
                for b in range(L.start, L.stop, 128):
                    at = (slice(r, r + 32), slice(b, b + 128))
                    v = R.pre[at] + R.ubv[r:r + 32, :]
                    v2 = v * v
                    t = jnp.tanh(v * (C0 + C1 * v2))
                    h1 = 0.5 + 0.5 * t
                    hid = v * h1
                    R.gp[it, r:r + 32, b:b + 128] = h1 + (hid - hid * h1) * (2.0 * C0 + 6.0 * C1 * v2)
                    R.hT[it, r:r + 32, b:b + 128] = hid.astype(BF)
            yield
        y = nn(R.wdT[...], R.hT[it, 0:FF, L])
        for b in range(L.start, L.stop, 128):
            out = R.mid[:, b:b + 128] + R.vecs[7] + y[:, b - L.start:b - L.start + 128]
            R.finish_forward(it, b, out.astype(BF))
        if it == 1:
            R.send(c, 0)
        yield
    for it in (1, 0):
        for half in range(2):
            rows = slice(512 * half, 512 * half + 512)
            R.pre[rows, L] = nn(R.wd_ref[rows, :], R.lowT[it, :, L])
            yield
            for r in range(rows.start, rows.stop, 32):
                for b in range(L.start, L.stop, 128):
                    at = (slice(r, r + 32), slice(b, b + 128))
                    R.dpre[it, r:r + 32, b:b + 128] = (R.pre[at] * R.gp[it, r:r + 32, b:b + 128]).astype(BF)
            yield
        R.dn[:, L] = nn(R.wu_ref[...], R.dpre[it, :, L])
        yield
        ln_backward(R.dn, R.gT, R.unit2.at[it], R.inv2.at[it], R.vecs.at[5], R.aln.at[2], R.aln.at[3], R.gT, R.alow.at[it], L)
        yield
        R.dmixT[:, L] = nn(R.wo_ref[...], R.alow[it, :, L]).astype(BF)
        yield
        for p in prompts:
            tok = slice(p * 128, p * 128 + 128)
            for h in range(HEADS):
                R.bdo[p, h // 2, 32 * (h % 4):32 * (h % 4) + 32, 128 * (h % 2):128 * (h % 2) + 128] = R.dmixT[32 * h:32 * h + 32, tok]
            for h2 in range(HEADS // 2):
                R.sc[p, :, 256 * h2:256 * h2 + 256] = nn(R.vN[it, p, 0:KEYS, 128 * (h2 // 2):128 * (h2 // 2) + 128], R.bdo[p, h2])
            yield
        for p in prompts:
            tok = slice(p * 128, p * 128 + 128)
            for h in range(HEADS):
                ln = slice(128 * h, 128 * h + 128)
                pT = R.p32[it, p, 0:USED, ln]
                t = pT * R.sc[p, 0:USED, ln]
                dsum = jnp.sum(t, axis=0, keepdims=True)
                R.ds16[p, 0:KEYS, ln] = jnp.concatenate([t - pT * dsum, rest], axis=0).astype(BF)
                R.dsN[p, :, ln] = R.ds16[p, :, ln].T
            yield
            for h2 in range(HEADS // 2):
                r = 64 * h2
                ln = slice(256 * h2, 256 * h2 + 256)
                for base, left, right, scaled in (
                    (512, R.dmixT[r:r + 64, tok], R.pN[it, p, :, ln], None),
                    (0, R.qkvT[it, 256 + r:320 + r, tok], R.ds16[p, :, ln], SCALE),
                    (256, R.qkvT[it, r:r + 64, tok], R.dsN[p, :, ln], SCALE)):
                    d = nn(left, right)
                    top, low = d[0:32, 0:128], d[32:64, 128:256]
                    if scaled is not None:
                        top, low = top * scaled, low * scaled
                    R.dqkvT[it, base + r:base + r + 32, tok] = top.astype(BF)
                    R.dqkvT[it, base + r + 32:base + r + 64, tok] = low.astype(BF)
            yield
        R.dn[:, L] = nn(R.wqkv[...], R.dqkvT[it, :, L])
        yield
        ln_backward(R.dn, R.gT, R.unit1.at[it], R.inv1.at[it], R.vecs.at[0], R.aln.at[0], R.aln.at[1], R.gT, R.gl16, L)
        for b in range(L.start, L.stop, 128):
            R.finish_backward(it, b, R.gl16[:, b:b + 128])
        yield


def weight_terms(R, it):
    for i in range(0, FF, 256):
        stop = i + 256 if i + 256 < FF else FF + 16
        R.add_wd(i, nt(R.hT[it, i:stop, :], R.lowT[it]))
        yield
    for j in range(FF // D):
        R.add_wu(j, nt(R.n2T[it], R.dpre[it, j * D:j * D + D, :]))
        yield
    R.add_wo(nt(R.mixT[it], R.alow[it]))
    yield
    for j in range(3):
        R.add_wqkv(j, nt(R.n1T[it], R.dqkvT[it, j * D:j * D + D, :]))
        yield


def run_group(R, masks, lag):
    chains = [chain(R, c, masks) for c in range(GROUP // CH)]
    counts = [0] * len(chains)
    done = [False] * len(chains)
    terms = []
    started = set()
    while not all(done) or terms:
        for i, ch in enumerate(chains):
            if done[i] or (i > 0 and counts[i] + lag > counts[i - 1] and not done[i - 1]):
                continue
            try:
                next(ch)
                counts[i] += 1
            except StopIteration:
                done[i] = True
        if min(counts) >= R.bwd1_done and 1 not in started:
            started.add(1)
            terms.append(weight_terms(R, 1))
        if all(done) and 0 not in started:
            started.add(0)
            terms.append(weight_terms(R, 0))
        for t in list(terms):
            try:
                next(t)
            except StopIteration:
                terms.remove(t)


SCRATCH = dict(
    wqkvT=((768, 256), BF), woT=((256, 256), BF), wuT=((1024, 256), BF), wdT=((256, 1024), BF), wqkv=((256, 768), BF),
    vecs=((8, 256, 128), F32), ubv=((1024, 128), F32),
    n1T=((2, 272, GROUP), BF), qkvT=((2, 768, GROUP), BF), kN=((PG, 128, 256), BF), vN=((2, PG, 128, 256), BF),
    bdq=((PG, 4, 128, 256), BF), bdo=((PG, 4, 128, 256), BF),
    sc=((PG, KEYS, 1024), F32), p32=((2, PG, KEYS, 1024), F32), p16=((2, PG, 128, 1024), BF), pN=((2, PG, 128, 1024), BF),
    ds16=((PG, 128, 1024), BF), dsN=((PG, 128, 1024), BF),
    mixT=((2, 272, GROUP), BF), uT=((256, GROUP), F32), eT=((256, GROUP), BF), mid=((256, GROUP), F32), gT=((256, GROUP), F32), dn=((256, GROUP), F32),
    gl16=((256, GROUP), BF),
    unit1=((2, 256, GROUP), F32), inv1=((2, 1, GROUP), F32), unit2=((2, 256, GROUP), F32), inv2=((2, 1, GROUP), F32),
    n2T=((2, 272, GROUP), BF), pre=((1024, GROUP), F32), gp=((2, 1024, GROUP), F32), hT=((2, 1040, GROUP), BF),
    lowT=((2, 256, GROUP), BF), dpre=((2, 1024, GROUP), BF), alow=((2, 256, GROUP), BF), dmixT=((256, GROUP), BF),
    dqkvT=((2, 768, GROUP), BF), aln=((4, 256, 128), F32))


def prologue(R, n1g, n1b, wq, qb, wk, wv, vb, wo, ob, n2g, n2b, wu, ub, wd, db):
    R.wqkvT[0:256, :] = wq[...].T
    R.wqkvT[256:512, :] = wk[...].T
    R.wqkvT[512:768, :] = wv[...].T
    R.woT[...] = wo[...].T
    R.wuT[...] = wu[...].T
    R.wdT[...] = wd[...].T
    R.wqkv[:, 0:256] = wq[...]
    R.wqkv[:, 256:512] = wk[...]
    R.wqkv[:, 512:768] = wv[...]
    for i, r in enumerate((n1g, n1b, qb, vb, ob, n2g, n2b, db)):
        R.vecs[i] = jnp.broadcast_to(r[...].astype(F32).reshape(1, D), (128, D)).T
    R.ubv[...] = jnp.broadcast_to(ub[...].astype(F32).reshape(1, FF), (128, FF)).T
    for r in (R.aln, R.bdq, R.bdo, R.ds16, R.p16):
        r[...] = jnp.zeros_like(r)
    for it in range(2):
        for r in (R.n1T, R.mixT, R.n2T):
            r[it, D:, :] = jnp.ones((16, GROUP), BF)
        R.hT[it, FF:, :] = jnp.ones((16, GROUP), BF)


LAG = 3
LAST_GRADIENTS = 2
MESH = pl.DeviceIdType.MESH
CUBE = (("dp", 2), ("section", 1), ("dp", 4))
PEERS = 7
FARTHEST_FIRST = (7, 6, 5, 3, 4, 2, 1)


class Place:
    def __init__(self, dp_bits):
        self.section = lax.axis_index("section")
        self.dp = lax.axis_index("dp")
        self.core = lax.rem(self.dp, 2)
        self.rest = [1 << b for b in range(3, dp_bits)]
        self.bits = [self.bit(axis, weight) for axis, weight in CUBE]
        self.cube = self.bits[0] + 2 * self.bits[1] + 4 * self.bits[2]

    def bit(self, axis, weight):
        return self.section if axis == "section" else lax.rem(lax.div(self.dp, weight), 2)

    def across(self, axis, weight):
        if axis == "section":
            return (1 - self.section, self.dp)
        return (self.section, self.dp + (1 - 2 * self.bit(axis, weight)) * weight)

    def peer(self, mask):
        section, dp, number = self.section, self.dp, 0
        for i, (axis, weight) in enumerate(CUBE):
            v = self.bits[i]
            if mask >> i & 1:
                if axis == "section":
                    section = 1 - section
                else:
                    dp = dp + (1 - 2 * v) * weight
                v = 1 - v
            number = number + v * (1 << i)
        return (section, dp), number

    def everyone(self):
        found = [self.across("dp", 1)] + [self.peer(m)[0] for m in range(1, PEERS + 1)]
        return found + [self.across("dp", w) for w in self.rest]


class Sums:
    def __init__(self, R, place, e, base, rows):
        self.R, self.place, self.e, self.base = R, place, e, base
        self.half, self.n = rows // 2, rows // 16
        self.sent = []
        self.buf = base // 2
        self.cbuf = base // 16
        self.keep = pl.multiple_of(base + place.core * self.half, 16)
        self.own = pl.multiple_of(self.keep + place.cube * self.n, 16)

    def copy(self, src, dst, slot, device):
        R = self.R
        c = pltpu.make_async_remote_copy(src_ref=src, dst_ref=dst, send_sem=R.sum_send.at[self.e, slot],
                                         recv_sem=R.sum_recv.at[self.e, slot], device_id=device, device_id_type=MESH)
        c.start()
        self.sent.append(c)
        return c

    def steps(self):
        R, place, half, n = self.R, self.place, self.half, self.n
        region = pl.ds(self.buf, half)
        away = pl.multiple_of(self.base + (1 - place.core) * half, 16)
        R.core_send[region, :] = R.acc[pl.ds(away, half), :].astype(BF)
        c = self.copy(R.core_send.at[region, :], R.core_recv.at[region, :], 0, place.across("dp", 1))
        yield
        c.wait_recv()
        small = pl.ds(self.cbuf, n)
        waits = []
        for m in FARTHEST_FIRST:
            device, number = place.peer(m)
            at = pl.multiple_of(number * n, 16)
            R.cube_send[m - 1, small, :] = (R.acc[pl.ds(pl.multiple_of(self.keep + at, 16), n), :]
                                            + R.core_recv[pl.ds(pl.multiple_of(self.buf + at, 16), n), :].astype(F32)).astype(BF)
            waits.append(self.copy(R.cube_send.at[m - 1, small, :], R.cube_recv.at[m - 1, small, :], m, device))
        total = R.acc[pl.ds(self.own, n), :] + R.core_recv[pl.ds(pl.multiple_of(self.buf + place.cube * n, 16), n), :].astype(F32)
        R.acc[pl.ds(self.own, n), :] = total
        yield
        for c in waits:
            c.wait_recv()
        total = R.acc[pl.ds(self.own, n), :]
        for m in range(PEERS):
            total = total + R.cube_recv[m, small, :].astype(F32)
        for i, weight in enumerate(place.rest):
            R.rest_send[i, small, :] = total.astype(BF)
            c = self.copy(R.rest_send.at[i, small, :], R.rest_recv.at[i, small, :], 2 * PEERS + 2 + i, place.across("dp", weight))
            yield
            c.wait_recv()
            total = R.rest_send[i, small, :].astype(F32) + R.rest_recv[i, small, :].astype(F32)
        own = pl.ds(self.own, n)
        R.sums[own, :] = total.astype(BF)
        waits = []
        for m in FARTHEST_FIRST:
            waits.append(self.copy(R.sums.at[own, :], R.sums.at[own, :], PEERS + m, place.peer(m)[0]))
        yield
        for c in waits:
            c.wait_recv()
        keep = pl.ds(self.keep, half)
        c = self.copy(R.sums.at[keep, :], R.sums.at[keep, :], 2 * PEERS + 1, place.across("dp", 1))
        yield
        c.wait_recv()

    def finish(self):
        for c in self.sent:
            c.wait_send()


class VectorSums(Sums):
    def __init__(self, R, place, e):
        self.R, self.place, self.e = R, place, e
        self.sent = []

    def steps(self):
        R, place = self.R, self.place
        R.vec_send[0] = R.vec[...]
        c = self.copy(R.vec_send.at[0], R.vec_recv.at[0], 0, place.across("dp", 1))
        yield
        c.wait_recv()
        R.vec_cube[place.cube] = R.vec_send[0] + R.vec_recv[0]
        waits = []
        for m in FARTHEST_FIRST:
            waits.append(self.copy(R.vec_cube.at[place.cube], R.vec_cube.at[place.cube], m, place.peer(m)[0]))
        yield
        for c in waits:
            c.wait_recv()
        total = R.vec_cube[0]
        for i in range(1, PEERS + 1):
            total = total + R.vec_cube[i]
        for i, weight in enumerate(place.rest):
            R.vec_send[1 + i] = total
            c = self.copy(R.vec_send.at[1 + i], R.vec_recv.at[1 + i], 2 * PEERS + 2 + i, place.across("dp", weight))
            yield
            c.wait_recv()
            total = R.vec_send[1 + i] + R.vec_recv[1 + i]
        R.vec[...] = total


FF_ROWS = 2 * FF + D
QKV_ROWS = 3 * D


def comm_scratch(rows, rest):
    blocks = rows // CH
    dma = pltpu.SemaphoreType.DMA
    total = FF_ROWS + QKV_ROWS
    slots = 2 * PEERS + 2 + rest
    return dict(
        stS=pltpu.VMEM((2, rows, 256), BF), grS=pltpu.VMEM((2, rows, 256), BF),
        used_v=pltpu.VMEM((rows // SLOTS, 128), jnp.int32),
        acc=pltpu.VMEM((total, 256), F32), ones_acc=pltpu.VMEM((9, 16, 256), F32),
        core_send=pltpu.VMEM((total // 2, 256), BF), core_recv=pltpu.VMEM((total // 2, 256), BF),
        cube_send=pltpu.VMEM((PEERS, total // 16, 256), BF), cube_recv=pltpu.VMEM((PEERS, total // 16, 256), BF),
        rest_send=pltpu.VMEM((rest, total // 16, 256), BF), rest_recv=pltpu.VMEM((rest, total // 16, 256), BF),
        vec_send=pltpu.VMEM((1 + rest, 16, 256), F32), vec_recv=pltpu.VMEM((1 + rest, 16, 256), F32),
        vec_cube=pltpu.VMEM((PEERS + 1, 16, 256), F32),
        in_sem=dma((blocks, 3)), local_sem=dma((blocks, 2)), ex_send=dma((blocks, 2)), ex_recv=dma((blocks, 2)),
        sum_send=dma((4, slots)), sum_recv=dma((4, slots)))


def kernel(dp_bits, x_hbm, e_hbm, g_hbm, counts_ref, lengths_ref, *refs):
    ws = refs[:15]
    st_hbm, gr_hbm, sums_ref, vec_ref = refs[15:19]
    R = Refs()
    for name, r in zip(list(SCRATCH) + list(comm_scratch(CH, 1)), refs[19:]):
        setattr(R, name, r)
    R.wo_ref, R.wu_ref, R.wd_ref = ws[7], ws[11], ws[13]
    R.sums, R.vec = sums_ref, vec_ref
    R.bwd1_done = 44
    aln, acc, ones_acc = R.aln, R.acc, R.ones_acc
    rows = R.stS.shape[1]
    blocks = rows // CH
    place = Place(dp_bits)
    section, dp = place.section, place.dp

    barrier = pltpu.get_barrier_semaphore()
    everyone = place.everyone()
    for device in everyone:
        pl.semaphore_signal(barrier, inc=1, device_id=device, device_id_type=MESH)

    def fetch(b, k):
        src = (x_hbm, e_hbm, g_hbm)[k]
        dst = (R.grS.at[0], R.stS.at[0], R.grS.at[1])[k]
        start = pl.multiple_of(b * CH, CH)
        return pltpu.make_async_copy(
            src.at[pl.ds(pl.multiple_of(section * rows, CH) + start, CH), :],
            dst.at[pl.ds(start, CH), :], R.in_sem.at[b, k])

    def start_fetches(b, c):
        for k in range(3):
            fetch(b, k).start()
        return c
    lax.fori_loop(0, blocks, start_fetches, 0)

    prologue(R, *ws)
    acc[...] = jnp.zeros_like(acc)
    ones_acc[...] = jnp.zeros_like(ones_acc)
    prompts = rows // SLOTS
    at_most = lengths_ref.shape[1]
    j_iota = lax.broadcasted_iota(jnp.int32, (1, at_most), 1)
    for p in range(prompts):
        count = counts_ref[section * prompts + p]
        kept = jnp.where(j_iota < count, lengths_ref[pl.ds(section * prompts + p, 1), :], 0)
        total = jnp.sum(kept.astype(F32), axis=1, keepdims=True).astype(jnp.int32)
        R.used_v[p:p + 1, :] = jnp.broadcast_to(total, (1, 128))

    k_iota = lax.broadcasted_iota(jnp.int32, (USED, SLOTS), 0)
    q_iota = lax.broadcasted_iota(jnp.int32, (USED, SLOTS), 1)

    def out_copies(b, k):
        stage, out = ((R.stS, st_hbm), (R.grS, gr_hbm))[k]
        here = pl.ds(pl.multiple_of(b * CH, CH), CH)
        there = pl.ds(pl.multiple_of(section * rows, CH) + pl.multiple_of(b * CH, CH), CH)
        own = pltpu.make_async_copy(stage.at[section, here, :], out.at[there, :], R.local_sem.at[b, k])
        sent = pltpu.make_async_remote_copy(
            src_ref=stage.at[1 - section, here, :], dst_ref=out.at[there, :],
            send_sem=R.ex_send.at[b, k], recv_sem=R.ex_recv.at[b, k],
            device_id=(1 - section, dp), device_id_type=MESH)
        return own, sent

    def add_wd(i, t):
        n = min(256, FF - i)
        acc[i:i + n, :] += t[0:n]
        if t.shape[0] > n:
            ones_acc[0] += t[n:]

    def add_wu(j, t):
        acc[FF + j * D:FF + j * D + D, :] += t[0:D]
        ones_acc[1 + j] += t[D:]

    def add_wqkv(j, t):
        acc[FF_ROWS + j * D:FF_ROWS + j * D + D, :] += t[0:D]
        ones_acc[5 + j] += t[D:]

    def add_wo(t):
        acc[2 * FF:2 * FF + D, :] += t[0:D]
        ones_acc[8] += t[D:]
    R.add_wd, R.add_wu, R.add_wqkv, R.add_wo = add_wd, add_wu, add_wqkv, add_wo

    pl.semaphore_wait(barrier, len(everyone))

    def group(g, carry):
        def at(b):
            return pl.ds(pl.multiple_of(g * GROUP + b, 128), 128)

        def load(c):
            b = g * (GROUP // CH) + c
            for k in range(3):
                fetch(b, k).wait()
            tok = slice(c * CH, c * CH + CH)
            src = pl.ds(pl.multiple_of(b * CH, CH), CH)
            e = R.stS[0, src, :].T
            R.eT[:, tok] = e
            R.uT[:, tok] = R.grS[0, src, :].T.astype(F32) + e.astype(F32)
            grad = R.grS[1, src, :].T
            R.gT[:, tok] = grad.astype(F32)
            R.lowT[1, :, tok] = grad
        R.load = load

        def finish_forward(it, b, out):
            R.stS[it, at(b), :] = out.T
            if it == 0:
                R.uT[:, b:b + 128] = out.astype(F32) + R.eT[:, b:b + 128].astype(F32)
        R.finish_forward = finish_forward

        def finish_backward(it, b, low):
            R.grS[it, at(b), :] = low.T
            if it == 1:
                R.gT[:, b:b + 128] = low.astype(F32)
                R.lowT[0, :, b:b + 128] = low
        R.finish_backward = finish_backward

        def send(c, k):
            for copy in out_copies(g * (GROUP // CH) + c, k):
                copy.start()
        R.send = send

        masks = []
        for p in range(PG):
            used = R.used_v[pl.ds(g * PG + p, 1), :]
            masks.append(jnp.where((k_iota <= q_iota) & (k_iota < used), 0.0, -1e30).astype(F32))
        run_group(R, masks, LAG)

        @pl.when(g < rows // GROUP - 1)
        def _():
            for c in range(GROUP // CH):
                send(c, 1)
        return carry

    lax.fori_loop(0, rows // GROUP, group, 0)

    for i, j in enumerate((0, 1, 5, 6)):
        vec_ref[j:j + 1, :] = jnp.sum(aln[i].T, axis=0, keepdims=True)
    for i, j in ((0, 7), (1, 8), (2, 9), (3, 10), (4, 11), (5, 2), (7, 3), (8, 4)):
        vec_ref[j:j + 1, :] = ones_acc[i, 0:1, :]
    vec_ref[12:16, :] = jnp.zeros((4, D), F32)

    sums = [Sums(R, place, 0, 0, FF), Sums(R, place, 1, FF, FF_ROWS - FF), Sums(R, place, 2, FF_ROWS, QKV_ROWS), VectorSums(R, place, 3)]
    running = [x.steps() for x in sums]
    turn = 0
    while running:
        for x in list(running):
            try:
                next(x)
            except StopIteration:
                running.remove(x)
        turn += 1
        if turn == LAST_GRADIENTS:
            for c in range(GROUP // CH):
                for copy in out_copies(blocks - GROUP // CH + c, 1):
                    copy.start()
    for x in sums:
        x.finish()

    def finish_out(b, c):
        for k in range(2):
            own, sent = out_copies(b, k)
            own.wait()
            sent.wait()
        return c
    lax.fori_loop(0, blocks, finish_out, 0)


def compute(x, e, g, counts, lengths, params, dp_size):
    local = x.shape[0]
    rows = local // 2
    dp_bits = dp_size.bit_length() - 1
    rest = dp_bits - 3
    hbm = pl.BlockSpec(memory_space=pl.ANY)
    smem = pl.BlockSpec(memory_space=pltpu.SMEM)
    vmem = pl.BlockSpec(memory_space=pltpu.VMEM)
    outs = [
        jax.ShapeDtypeStruct((local, 256), BF),
        jax.ShapeDtypeStruct((local, 256), BF),
        jax.ShapeDtypeStruct((3072, 256), BF),
        jax.ShapeDtypeStruct((16, 256), F32),
    ]
    return pl.pallas_call(
        functools.partial(kernel, dp_bits),
        out_shape=outs,
        in_specs=[hbm, hbm, hbm, smem, vmem] + [vmem] * 15,
        out_specs=[hbm, hbm, vmem, vmem],
        scratch_shapes=[pltpu.VMEM(s, t) for s, t in SCRATCH.values()] + list(comm_scratch(rows, rest).values()),
        compiler_params=pltpu.CompilerParams(
            vmem_limit_bytes=57 * 1024 * 1024, collective_id=0, has_side_effects=True),
    )(x, e, g, counts, lengths, *params)


CHUNKS = 2


def widen_kernel(st_ref, gr_ref, sums_ref, vec_ref, st_out, gr_out, n1g, n1b, wq, qb, wk, wv, vb, wo, ob, n2g, n2b, wu, ub, wd, db,
                 st_v, gr_v, gr_w, sums_v, wd_v, wu_v, wa_v, st_in, gr_in, sum_in, st_sem, gr_sem, w_sem, v_sem, ub_v, *vec_v):
    block = st_v.shape[0] // CHUNKS
    sums_in = [pltpu.make_async_copy(sums_ref.at[rows, :], sums_v.at[rows, :], sum_in.at[i])
               for i, rows in enumerate((pl.ds(0, FF), pl.ds(FF, FF + D + QKV_ROWS)))]
    parts = [pl.ds(i * block, block) for i in range(CHUNKS)]
    gr_ins = [pltpu.make_async_copy(gr_ref.at[r, :], gr_v.at[r, :], gr_in.at[i]) for i, r in enumerate(parts)]
    st_ins = [pltpu.make_async_copy(st_ref.at[r, :], st_v.at[r, :], st_in.at[i]) for i, r in enumerate(parts)]
    outs = []

    def out(src, dst, sem):
        c = pltpu.make_async_copy(src, dst, sem)
        c.start()
        outs.append(c)

    for c in gr_ins[:2] + sums_in + gr_ins[2:] + st_ins:
        c.start()

    def gradients(i):
        gr_ins[i].wait()
        gr_w[parts[i], :] = gr_v[parts[i], :].astype(F32)
        out(gr_w.at[parts[i], :], gr_out.at[0, parts[i], :], gr_sem.at[i])

    for j in range(FF // D):
        ub_v[D * j:D * j + D] = vec_ref[8 + j]
    out(ub_v, ub, v_sem.at[8])
    for j, (r, v) in enumerate(zip((n1g, n1b, qb, vb, ob, n2g, n2b, db), vec_v)):
        v[...] = vec_ref[j]
        out(v, r, v_sem.at[j])
    gradients(0)
    sums_in[0].wait()
    wd_v[...] = sums_v[0:FF, :].astype(F32)
    out(wd_v, wd, w_sem.at[0])
    sums_in[1].wait()
    for j in range(FF // D):
        wu_v[:, D * j:D * j + D] = sums_v[FF + D * j:FF + D * j + D, :].astype(F32)
    out(wu_v, wu, w_sem.at[1])
    wa_v[...] = sums_v[2 * FF:2 * FF + 4 * D, :].astype(F32)
    for j, r in enumerate((wo, wq, wk, wv)):
        out(wa_v.at[D * j:D * j + D, :], r, w_sem.at[2 + j])
    for i in range(1, CHUNKS):
        gradients(i)
    for i in range(CHUNKS):
        st_ins[i].wait()
        out(st_v.at[parts[i], :], st_out.at[0, parts[i], :], st_sem.at[i])
    for c in outs:
        c.wait()


def widen(st, gr, sums, vec, params):
    local = st.shape[0]
    outs = [jax.ShapeDtypeStruct((1, local, 256), BF), jax.ShapeDtypeStruct((1, local, 256), F32)]
    outs += [jax.ShapeDtypeStruct(p.shape, F32) for p in params]
    hbm = pl.BlockSpec(memory_space=pl.ANY)
    vmem = pl.BlockSpec(memory_space=pltpu.VMEM)
    dma = pltpu.SemaphoreType.DMA
    return pl.pallas_call(
        widen_kernel,
        out_shape=outs,
        in_specs=[hbm, hbm, hbm, vmem],
        out_specs=[hbm] * len(outs),
        scratch_shapes=[
            pltpu.VMEM((local, 256), BF), pltpu.VMEM((local, 256), BF), pltpu.VMEM((local, 256), F32),
            pltpu.VMEM(sums.shape, BF), pltpu.VMEM((FF, D), F32), pltpu.VMEM((D, FF), F32), pltpu.VMEM((4 * D, D), F32),
            dma((CHUNKS,)), dma((CHUNKS,)), dma((2,)), dma((CHUNKS,)), dma((CHUNKS,)), dma((6,)), dma((9,)), pltpu.VMEM((FF,), F32)] + [pltpu.VMEM((D,), F32)] * 8,
        compiler_params=pltpu.CompilerParams(vmem_limit_bytes=58 * 1024 * 1024),
    )(st, gr, sums, vec)


def solution(mesh):
    dp_size = mesh.shape["dp"]

    def body(x, e, g, counts, lengths, *params):
        st, gr, sums, vec = compute(x, e, g, counts, lengths, params, dp_size)
        return tuple(widen(st, gr, sums, vec, params))

    placed = (P("dp", None),) * 3 + (P("dp"), P("dp", None)) + (P(),) * 15
    return jax.shard_map(
        body,
        mesh=mesh,
        in_specs=placed,
        out_specs=(P("section", "dp", None),) * 2 + (P(),) * 15,
        check_vma=False,
    )
```
